32 devices in a mesh: shard: 4 (over z), rep: 8 (over y, x, core).
Axes of the slice: x: 2, y: 2, z: 4, core: 2. Of those that a mesh axis runs over, the one named last changes fastest.
Arguments:
- images: bfloat16 [160, 14, 14, 512], P(('shard', 'rep')), may hold values from -6 to 6
- region_ids: int32 [160, 14, 14], P(('shard', 'rep')), may hold values from 0 to 8, as said below
- image_counts: int32 [32], P(('shard', 'rep')), may hold values from 1 to 5, as said below
- rel_index: int32 [49, 49], replicated, may hold values from 0 to 168, as said below
- cotangent: bfloat16 [160, 14, 14, 512], P(('shard', 'rep')), may hold values from -6 to 6
- attention_weight: float32 [2, 512, 2048], P(None, None, 'shard')
- feedforward_weight: float32 [2, 512, 4096], P(None, None, 'shard')
- vector_params: float32 [2, 8848], P(None, 'shard')
- attention_first: float32 [2, 512, 2048], P(None, None, 'shard')
- feedforward_first: float32 [2, 512, 4096], P(None, None, 'shard')
- vector_first: float32 [2, 8848], P(None, 'shard')
- attention_second: float32 [2, 512, 2048], P(None, None, 'shard')
- feedforward_second: float32 [2, 512, 4096], P(None, None, 'shard')
- vector_second: float32 [2, 8848], P(None, 'shard')
Outputs:
- block_out: bfloat16 [160, 14, 14, 512], P(('shard', 'rep'))
- input_grad: bfloat16 [160, 14, 14, 512], P(('shard', 'rep'))
- attention_grad: float32 [2, 512, 2048], P(None, None, 'shard')
- feedforward_grad: float32 [2, 512, 4096], P(None, None, 'shard')
- vector_grad: float32 [2, 8848], P(None, 'shard')
- attention_new: float32 [2, 512, 2048], P(None, None, 'shard')
- feedforward_new: float32 [2, 512, 4096], P(None, None, 'shard')
- vector_new: float32 [2, 8848], P(None, 'shard')
- first_attention: float32 [2, 512, 2048], P(None, None, 'shard')
- first_feedforward: float32 [2, 512, 4096], P(None, None, 'shard')
- first_vector: float32 [2, 8848], P(None, 'shard')
- second_attention: float32 [2, 512, 2048], P(None, None, 'shard')
- second_feedforward: float32 [2, 512, 4096], P(None, None, 'shard')
- second_vector: float32 [2, 8848], P(None, 'shard')
The draws below stay inside these ranges and needn't reach their ends.
Inputs may be any that keep to these rules, and one draw needn't show every extreme that they name: `region_ids`: each image's ids form three bands of rows times three bands of columns, id = 3 * row band + column band; the first cut lies at 7, the second at a drawn place after it. `image_counts`: each group's images fill its first slots; some group is full and some holds one image. `rel_index`: pairs with equal relative offset share an entry, and each entry belongs to one offset.
All inputs are finite; a program needn't handle non-finite values.
Results may differ from the reference program's by a relative error of at most 0.025.
Values may be sent and summed in bfloat16 or wider, within the bound.
No kernel may reach another device: no remote copies, remote signals or barrier semaphores. Data moves between devices by JAX's collectives and lax.ppermute only.
A program may use at most 256 MiB of HBM per device.

```python
import math
import jax
import jax.numpy as jnp
from jax import lax

WIDTH = 512
HEADS = 16
INNER = 2048
WINDOW = 7
SIDE = 14
SHIFT = 3
TABLE = 169
LAYERS = 2
STEP = 10
IMG_DEV = 5
GROUPS = 32
IMAGES = 160
SMALL = 8848


def grad_base():
    return (98.0 * IMAGES * (IMG_DEV + 1) / IMG_DEV) ** 0.5


def attention_grad_scale():
    columns = jnp.arange(4 * WIDTH)
    return jnp.where(columns < 2 * WIDTH, 0.1, jnp.where(columns < 3 * WIDTH, 1.0, 0.5)).astype(jnp.float32)


def forward_grad_scale():
    columns = jnp.arange(2 * INNER)
    return jnp.where(columns < INNER, 0.5, 0.7).astype(jnp.float32)


def vector_grad_scale():
    spots = jnp.arange(SMALL)
    return jnp.where(spots < 8 * WIDTH + INNER, 0.5, 0.03).astype(jnp.float32)


def log_factor(key, shape):
    return jnp.exp(jax.random.uniform(key, shape, jnp.float32, math.log(0.5), math.log(8.0)))


def draw_region_ids(key, part):
    key = jax.random.fold_in(key, 3)
    row_key, col_key = jax.random.split(key)
    row_cut = jax.random.randint(row_key, (IMAGES, 1, 1), SIDE - WINDOW + 1, SIDE)
    col_cut = jax.random.randint(col_key, (IMAGES, 1, 1), SIDE - WINDOW + 1, SIDE)
    row_pos = jnp.arange(SIDE).reshape(1, SIDE, 1)
    col_pos = jnp.arange(SIDE).reshape(1, 1, SIDE)
    row_band = (row_pos >= SIDE - WINDOW).astype(jnp.int32) + (row_pos >= row_cut).astype(jnp.int32)
    col_band = (col_pos >= SIDE - WINDOW).astype(jnp.int32) + (col_pos >= col_cut).astype(jnp.int32)
    return (row_band * 3 + col_band).astype(jnp.int32)


def draw_image_counts(key, part):
    key = jax.random.fold_in(key, 5)
    count_key, full_key, single_key = jax.random.split(key, 3)
    counts = 1 + jax.random.randint(count_key, (GROUPS,), 0, IMG_DEV)
    full_at = jax.random.randint(full_key, (), 0, GROUPS)
    single_at = (full_at + 1 + jax.random.randint(single_key, (), 0, GROUPS - 1)) % GROUPS
    spots = jnp.arange(GROUPS)
    counts = jnp.where(spots == full_at, IMG_DEV, counts)
    counts = jnp.where(spots == single_at, 1, counts)
    return counts.astype(jnp.int32)


def draw_rel_index(key, part):
    key = jax.random.fold_in(key, 7)
    spots = jnp.arange(WINDOW * WINDOW)
    row_pos = spots // WINDOW
    col_pos = spots % WINDOW
    offsets = (row_pos[:, None] - row_pos[None, :] + WINDOW - 1) * (2 * WINDOW - 1) + (col_pos[:, None] - col_pos[None, :] + WINDOW - 1)
    relabel = jax.random.permutation(key, TABLE)
    return relabel[offsets].astype(jnp.int32)


def draw_attention_weight(key, part):
    key = jax.random.fold_in(key, 11)
    shape = (LAYERS, WIDTH, 4 * WIDTH)
    base = jnp.clip(jax.random.normal(key, shape, jnp.float32), -4.0, 4.0)
    columns = jnp.arange(4 * WIDTH)
    scale = jnp.where(columns < 3 * WIDTH, WIDTH ** (-0.5), (7.0 / WIDTH) ** 0.5).astype(jnp.float32)
    return base * scale


def draw_feedforward_weight(key, part):
    key = jax.random.fold_in(key, 13)
    shape = (LAYERS, WIDTH, 2 * INNER)
    base = jnp.clip(jax.random.normal(key, shape, jnp.float32), -4.0, 4.0)
    columns = jnp.arange(2 * INNER)
    scale = jnp.where(columns < INNER, WIDTH ** (-0.5), 1.5 * INNER ** (-0.5)).astype(jnp.float32)
    return base * scale


def draw_vector_params(key, part):
    key = jax.random.fold_in(key, 17)
    shape = (LAYERS, SMALL)
    base = jnp.clip(jax.random.normal(key, shape, jnp.float32), -4.0, 4.0)
    spots = jnp.arange(SMALL)
    gains = (spots < WIDTH) | (spots >= 2 * WIDTH) & (spots < 3 * WIDTH)
    table_part = spots >= 8 * WIDTH + INNER
    return jnp.where(gains, 1.0 + 0.2 * base, jnp.where(table_part, base, 0.3 * base)).astype(jnp.float32)


def draw_attention_first(key, part):
    key = jax.random.fold_in(key, 19)
    shape = (LAYERS, WIDTH, 4 * WIDTH)
    base = jnp.clip(jax.random.normal(key, shape, jnp.float32), -4.0, 4.0)
    return 0.1111 * grad_base() * attention_grad_scale() * base


def draw_feedforward_first(key, part):
    key = jax.random.fold_in(key, 23)
    shape = (LAYERS, WIDTH, 2 * INNER)
    base = jnp.clip(jax.random.normal(key, shape, jnp.float32), -4.0, 4.0)
    return 0.1111 * grad_base() * forward_grad_scale() * base


def draw_vector_first(key, part):
    key = jax.random.fold_in(key, 29)
    shape = (LAYERS, SMALL)
    base = jnp.clip(jax.random.normal(key, shape, jnp.float32), -4.0, 4.0)
    return 0.1111 * grad_base() * vector_grad_scale() * base


def draw_attention_second(key, part):
    key = jax.random.fold_in(key, 31)
    scale = grad_base() * attention_grad_scale()
    return 0.001 * scale * scale * log_factor(key, (LAYERS, WIDTH, 4 * WIDTH))


def draw_feedforward_second(key, part):
    key = jax.random.fold_in(key, 37)
    scale = grad_base() * forward_grad_scale()
    return 0.001 * scale * scale * log_factor(key, (LAYERS, WIDTH, 2 * INNER))


def draw_vector_second(key, part):
    key = jax.random.fold_in(key, 41)
    scale = grad_base() * vector_grad_scale()
    return 0.001 * scale * scale * log_factor(key, (LAYERS, SMALL))


def shard_levels(own_key, dims, cuts, smallest, top_value):
    level, own = 1.0, jax.random.fold_in(own_key, 6)
    for position, blocks in cuts:
        steps = jnp.exp(jax.random.uniform(jax.random.fold_in(own, position), (blocks,), jnp.float32, smallest / len(cuts), top_value / len(cuts)))
        level = level * jnp.repeat(steps, dims[position] // blocks).reshape([-1 if axis == position else 1 for axis in range(len(dims))])
    return level


def gaussian(own_key, extent, width, most, cuts=(), dtype=jnp.bfloat16):
    factor_of = shard_levels(own_key, extent, cuts, -0.22, 0.18) if cuts else 1.0
    array = jax.random.normal(own_key, extent, jnp.float32) * width * factor_of
    return jnp.minimum(jnp.maximum(array, -most), most).astype(dtype)


def setup_inputs(seed: int = 0) -> dict:
    streams_of = jax.random.split(jax.random.key(seed), 15)
    images = gaussian(streams_of[0], (IMAGES, SIDE, SIDE, WIDTH), 1.0, 6.0, ((0, 32),))
    region_ids = draw_region_ids(jax.random.fold_in(streams_of[14], 71), 0)
    image_counts = draw_image_counts(jax.random.fold_in(streams_of[14], 71), 0)
    rel_index = draw_rel_index(jax.random.fold_in(streams_of[14], 71), 0)
    cotangent = gaussian(streams_of[4], (IMAGES, SIDE, SIDE, WIDTH), 1.0, 6.0, ((0, 32),))
    attention_weight = draw_attention_weight(jax.random.fold_in(streams_of[14], 71), 0)
    feedforward_weight = draw_feedforward_weight(jax.random.fold_in(streams_of[14], 71), 0)
    vector_params = draw_vector_params(jax.random.fold_in(streams_of[14], 71), 0)
    attention_first = draw_attention_first(jax.random.fold_in(streams_of[14], 71), 0)
    feedforward_first = draw_feedforward_first(jax.random.fold_in(streams_of[14], 71), 0)
    vector_first = draw_vector_first(jax.random.fold_in(streams_of[14], 71), 0)
    attention_second = draw_attention_second(jax.random.fold_in(streams_of[14], 71), 0)
    feedforward_second = draw_feedforward_second(jax.random.fold_in(streams_of[14], 71), 0)
    vector_second = draw_vector_second(jax.random.fold_in(streams_of[14], 71), 0)
    return {"images": images, "region_ids": region_ids, "image_counts": image_counts, "rel_index": rel_index, "cotangent": cotangent, "attention_weight": attention_weight, "feedforward_weight": feedforward_weight, "vector_params": vector_params, "attention_first": attention_first, "feedforward_first": feedforward_first, "vector_first": vector_first, "attention_second": attention_second, "feedforward_second": feedforward_second, "vector_second": vector_second}


@jax.custom_vjp
def low(v):
    return lax.optimization_barrier(v.astype(jnp.bfloat16)).astype(jnp.float32)

@jax.custom_vjp
def low_back(v):
    return v

def low_keep(v):
    return (low(v), None)

def low_pass(kept, grad):
    return (grad,)

def back_keep(v):
    return (v, None)

def back_low(kept, grad):
    return (low(grad),)
low.defvjp(low_keep, low_pass)
low_back.defvjp(back_keep, back_low)
EPS_NORM = 1e-05
EPS_ADAM = 1e-08
BETA_ONE = 0.9
BETA_TWO = 0.999
RATE_MATRIX = 0.1
RATE_VECTOR = 1.0
DECAY_MATRIX = 0.05
MASK_FILL = -100.0
HIGH = lax.Precision.HIGHEST

def unpack(vector):
    pieces = [vector[number * WIDTH:(number + 1) * WIDTH] for number in range(8)]
    pieces.append(vector[8 * WIDTH:8 * WIDTH + INNER])
    pieces.append(vector[8 * WIDTH + INNER:])
    return pieces

def normalize(values, gain, offset):
    centered = values - lax.optimization_barrier(jnp.mean(values, axis=-1, keepdims=True))
    variance = lax.optimization_barrier(jnp.mean(centered * centered, axis=-1, keepdims=True))
    return centered * lax.rsqrt(variance + EPS_NORM) * gain + offset

def to_windows(grid_field):
    image_count = grid_field.shape[0]
    channels = grid_field.shape[-1]
    across = SIDE // WINDOW
    grid_field = grid_field.reshape(image_count, across, WINDOW, across, WINDOW, channels)
    grid_field = grid_field.transpose(0, 1, 3, 2, 4, 5)
    return grid_field.reshape(image_count * across * across, WINDOW * WINDOW, channels)

def from_windows(window_field, image_count):
    channels = window_field.shape[-1]
    across = SIDE // WINDOW
    window_field = window_field.reshape(image_count, across, across, WINDOW, WINDOW, channels)
    window_field = window_field.transpose(0, 1, 3, 2, 4, 5)
    return window_field.reshape(image_count, SIDE, SIDE, channels)

def region_mask(regions):
    region_win = to_windows(regions[..., None]).reshape(-1, WINDOW * WINDOW)
    same = region_win[:, :, None] == region_win[:, None, :]
    return jnp.where(same, jnp.float32(0.0), jnp.float32(MASK_FILL))

def block(residual, attention_w, forward_w, vector_w, mask, rel_index, shifted):
    gain_one, offset_one, gain_two, offset_two, bias_query, bias_value, bias_proj, bias_out, bias_inner, bias_table = unpack(vector_w)
    image_count = residual.shape[0]
    head_size = WIDTH // HEADS
    normed = low(normalize(residual, gain_one, offset_one))
    if shifted:
        normed = jnp.roll(normed, (-SHIFT, -SHIFT), (1, 2))
    flat_in = to_windows(normed).reshape(-1, WIDTH)
    projected = jnp.dot(flat_in, attention_w[:, :3 * WIDTH], precision=HIGH)
    query_states = low(low_back(projected[:, :WIDTH] + bias_query))
    key_states = low(low_back(projected[:, WIDTH:2 * WIDTH]))
    value_states = low(low_back(projected[:, 2 * WIDTH:] + bias_value))
    window_count = flat_in.shape[0] // (WINDOW * WINDOW)
    head_shape = (window_count, WINDOW * WINDOW, HEADS, head_size)
    raw_scores = low_back(jnp.einsum('wihd,wjhd->whij', query_states.reshape(head_shape), key_states.reshape(head_shape), precision=HIGH))
    bias_grid = bias_table.reshape(HEADS, TABLE)[:, rel_index]
    scores = raw_scores * head_size ** (-0.5) + bias_grid[None]
    if shifted:
        scores = scores + mask[:, None]
    soft_weights = low(jax.nn.softmax(scores, axis=-1))
    attended = low(low_back(jnp.einsum('whij,wjhd->wihd', soft_weights, value_states.reshape(head_shape), precision=HIGH)))
    attended = attended.reshape(-1, WIDTH)
    branch = jnp.dot(attended, attention_w[:, 3 * WIDTH:], precision=HIGH) + bias_proj
    branch = from_windows(branch.reshape(window_count, WINDOW * WINDOW, WIDTH), image_count)
    if shifted:
        branch = jnp.roll(branch, (SHIFT, SHIFT), (1, 2))
    middle = residual + low_back(branch)
    second = low(normalize(middle, gain_two, offset_two)).reshape(-1, WIDTH)
    pre_act = low_back(jnp.dot(second, forward_w[:, :INNER], precision=HIGH) + bias_inner)
    activated = low(jax.nn.gelu(pre_act, approximate=False))
    result = low_back(jnp.dot(activated, forward_w[:, INNER:].T, precision=HIGH) + bias_out)
    return middle + result.reshape(residual.shape)

def forward_pass(residual, attention_all, forward_all, vector_all, mask, rel_index):
    attention_all = low(attention_all)
    forward_all = low(forward_all)
    vector_all = low(vector_all)
    for layer_id in range(LAYERS):
        residual = block(residual, attention_all[layer_id], forward_all[layer_id], vector_all[layer_id], mask, rel_index, layer_id % 2 == 1)
    return residual

def adam_update(weight, grad, first, second, rate, decay):
    first_new = BETA_ONE * first + (1.0 - BETA_ONE) * grad
    second_new = BETA_TWO * second + (1.0 - BETA_TWO) * grad * grad
    first_hat = first_new / (1.0 - BETA_ONE ** STEP)
    second_hat = second_new / (1.0 - BETA_TWO ** STEP)
    weight_new = weight - rate * (first_hat / (jnp.sqrt(second_hat) + EPS_ADAM) + decay * weight)
    return (weight_new, first_new, second_new)

def reference(images, region_ids, image_counts, rel_index, cotangent, attention_weight, feedforward_weight, vector_params, attention_first, feedforward_first, vector_first, attention_second, feedforward_second, vector_second):
    group_count = image_counts.shape[0]
    grid_shape = (group_count, IMG_DEV, SIDE, SIDE, WIDTH)
    inputs_all = images.astype(jnp.float32).reshape(grid_shape)
    cotangent_all = cotangent.astype(jnp.float32).reshape(grid_shape)
    regions_all = region_ids.reshape(group_count, IMG_DEV, SIDE, SIDE)

    def one_group(totals, group):
        inputs, grad_out, regions, count = group
        live_mask = (jnp.arange(IMG_DEV) < count).astype(jnp.float32)
        mask = region_mask(regions)

        def run(inputs_in, attention_in, forward_in, vector_in):
            return forward_pass(inputs_in, attention_in, forward_in, vector_in, mask, rel_index)
        outputs, pull = jax.vjp(run, inputs, attention_weight, feedforward_weight, vector_params)
        grad_in, grad_attention, grad_forward, grad_vector = pull(grad_out * live_mask[:, None, None, None])
        totals = (totals[0] + grad_attention, totals[1] + grad_forward, totals[2] + grad_vector)
        return (totals, (outputs.astype(jnp.bfloat16), grad_in.astype(jnp.bfloat16)))
    zeros = (jnp.zeros(attention_weight.shape, jnp.float32), jnp.zeros(feedforward_weight.shape, jnp.float32), jnp.zeros(vector_params.shape, jnp.float32))
    totals, outs_all = lax.scan(one_group, zeros, (inputs_all, cotangent_all, regions_all, image_counts))
    block_out = outs_all[0].reshape(images.shape)
    input_grad = outs_all[1].reshape(images.shape)
    attention_grad, feedforward_grad, vector_grad = totals
    attention_new, first_attention, second_attention = adam_update(attention_weight, attention_grad, attention_first, attention_second, RATE_MATRIX, DECAY_MATRIX)
    feedforward_new, first_feedforward, second_feedforward = adam_update(feedforward_weight, feedforward_grad, feedforward_first, feedforward_second, RATE_MATRIX, DECAY_MATRIX)
    vector_new, first_vector, second_vector = adam_update(vector_params, vector_grad, vector_first, vector_second, RATE_VECTOR, 0.0)
    return (block_out, input_grad, attention_grad, feedforward_grad, vector_grad, attention_new, feedforward_new, vector_new, first_attention, first_feedforward, first_vector, second_attention, second_feedforward, second_vector)
```

```python
import functools

import jax
import jax.numpy as jnp
from jax import lax
from jax.experimental import pallas as pl
from jax.experimental.pallas import tpu as pltpu
from jax.sharding import PartitionSpec as P

HEADS = 16
WINDOW = 7
SIDE = 14
SHIFT = 3
TABLE = 169
LAYERS = 2
STEP = 10

EPS_NORM = 1e-05
EPS_ADAM = 1e-08
BETA_ONE = 0.9
BETA_TWO = 0.999
RATE_MATRIX = 0.1
RATE_VECTOR = 1.0
DECAY_MATRIX = 0.05
MASK_FILL = -100.0
PAD_FILL = -1e30
HIGH = lax.Precision.HIGHEST

ACROSS = SIDE // WINDOW
WINDOWS = ACROSS * ACROSS
TOKENS = WINDOW * WINDOW
IMAGE = SIDE * SIDE
IMAGE_ROWS = 208
WINDOW_ROWS = 56
SLOT = 64
ROWS = WINDOWS * WINDOW_ROWS
SPARE = ROWS + 8
GROUP = 4
VMEM_BYTES = 56 * 1024 * 1024
SMALL_VMEM = 14 * 1024 * 1024


def params(bytes_limit=VMEM_BYTES):
    return pltpu.CompilerParams(vmem_limit_bytes=bytes_limit)


def cost(flops, moved, exps=0):
    return pl.CostEstimate(flops=int(flops), bytes_accessed=int(moved), transcendentals=int(exps))


def ordered_call(body, args, after, in_specs, prefetch=0, grid=None, **rest):
    count, extra = len(args), len(after)
    shapes = rest.pop("out_shape")
    shapes = list(shapes) if isinstance(shapes, (list, tuple)) else [shapes]
    results = len(shapes)

    def run(*refs):
        ins, refs = refs[:count], refs[count + extra :]
        outs, token, scratch = refs[:results], refs[results], refs[results + 1 :]
        token[...] = jnp.zeros(token.shape, token.dtype)
        return body(*ins, *outs, *scratch)

    in_specs = list(in_specs) + [pl.BlockSpec(memory_space=pl.ANY)] * extra
    out_specs = rest.pop("out_specs", [pl.BlockSpec(memory_space=pltpu.VMEM)] * results)
    out_specs = list(out_specs) if isinstance(out_specs, (list, tuple)) else [out_specs]
    if grid is None:
        out_specs.append(pl.BlockSpec(memory_space=pltpu.VMEM))
    else:
        out_specs.append(pl.BlockSpec((8, 128), lambda *_: (0, 0)))
    shapes.append(jax.ShapeDtypeStruct((8, 128), jnp.float32))
    if prefetch:
        rest["grid_spec"] = pltpu.PrefetchScalarGridSpec(
            num_scalar_prefetch=prefetch,
            grid=grid,
            in_specs=in_specs,
            out_specs=out_specs,
            scratch_shapes=rest.pop("scratch_shapes", ()),
        )
    else:
        rest.update(in_specs=in_specs, out_specs=out_specs)
        if grid is not None:
            rest["grid"] = grid
    return pl.pallas_call(run, out_shape=shapes, **rest)(*args, *after)


def far(value):
    return pltpu.with_memory_space_constraint(value, pltpu.HBM)


def dot(left, right):
    return jnp.dot(left, right, preferred_element_type=jnp.float32)


def dot_cols(left, right):
    return lax.dot_general(
        left, right, (((1,), (1,)), ((), ())), preferred_element_type=jnp.float32
    )


def dot_rows(left, right):
    return lax.dot_general(
        left, right, (((0,), (0,)), ((), ())), preferred_element_type=jnp.float32
    )


def segments(shifted):
    move = SHIFT if shifted else 0
    found = []
    for down in range(ACROSS):
        for right in range(ACROSS):
            base = (down * ACROSS + right) * WINDOW_ROWS
            for line in range(WINDOW):
                row = (down * WINDOW + line + move) % SIDE
                col = (right * WINDOW + move) % SIDE
                first = min(WINDOW, SIDE - col)
                spot = base + line * WINDOW
                found.append((spot, row * SIDE + col, first))
                if first < WINDOW:
                    found.append((spot + first, row * SIDE, WINDOW - first))
    return found


def into_windows(window_ref, image_ref, shifted):
    for window in range(WINDOWS):
        start = window * WINDOW_ROWS + TOKENS
        stop = (window + 1) * WINDOW_ROWS
        window_ref[start:stop, :] = jnp.zeros((stop - start, window_ref.shape[1]), jnp.float32)
    for spot, source, count in segments(shifted):
        window_ref[spot : spot + count, :] = image_ref[source : source + count, :]


def from_windows(image_ref, window_ref, shifted):
    image_ref[IMAGE:IMAGE_ROWS, :] = jnp.zeros(
        (IMAGE_ROWS - IMAGE, image_ref.shape[1]), jnp.float32
    )
    for spot, source, count in segments(shifted):
        image_ref[source : source + count, :] = window_ref[spot : spot + count, :]


def rows_to_field(field_ref, image, rows_ref, start):
    for line in range(SIDE):
        here = slice(start + line * SIDE, start + (line + 1) * SIDE)
        field_ref[image, line] = rows_ref[here, :].astype(jnp.bfloat16)


def field_to_rows(rows_ref, start, field_ref, image, factor):
    for line in range(SIDE):
        here = slice(start + line * SIDE, start + (line + 1) * SIDE)
        rows_ref[here, :] = field_ref[image, line].astype(jnp.float32) * factor
    rows_ref[start + IMAGE : start + IMAGE_ROWS, :] = jnp.zeros(
        (IMAGE_ROWS - IMAGE, rows_ref.shape[1]), jnp.float32
    )


def unit_norm(values):
    width = values.shape[-1]
    centered = values - jnp.sum(values, axis=-1, keepdims=True) * (1.0 / width)
    variance = jnp.sum(centered * centered, axis=-1, keepdims=True) * (1.0 / width)
    inverse = lax.rsqrt(variance + EPS_NORM)
    return centered * inverse, inverse


def normal_parts(points):
    below = 0.5 + 0.5 * lax.erf(points * (0.5**0.5))
    return below, jnp.exp(points * points * -0.5) * 0.3989422804014327


def norm_pull(grad, unit, inverse, gain):
    width = grad.shape[-1]
    scaled = grad * gain
    mean_one = jnp.sum(scaled, axis=-1, keepdims=True) * (1.0 / width)
    mean_two = jnp.sum(scaled * unit, axis=-1, keepdims=True) * (1.0 / width)
    return inverse * (scaled - mean_one - unit * mean_two)


def block_mask(token_limit):
    rows = lax.broadcasted_iota(jnp.int32, (GROUP * SLOT, GROUP * 32), 0)
    cols = lax.broadcasted_iota(jnp.int32, (GROUP * SLOT, GROUP * 32), 1)
    keep = ((rows // SLOT) == (cols // 32)) & ((rows % SLOT) < token_limit)
    return jnp.where(keep, 1.0, 0.0).astype(jnp.bfloat16)


def fold_heads(crossed):
    lanes = lax.broadcasted_iota(jnp.int32, (SLOT, GROUP * 32), 1) // 32
    total = jnp.where(lanes == 0, crossed[:SLOT], 0.0)
    for head in range(1, GROUP):
        part = crossed[head * SLOT : (head + 1) * SLOT]
        total = jnp.where(lanes == head, part, total)
    return total


def pad_slot(values):
    spare = jnp.zeros((SLOT - WINDOW_ROWS, values.shape[1]), jnp.float32)
    return jnp.concatenate([values, spare], axis=0).astype(jnp.bfloat16)


def fill_weights(ids_ref, own_ref, held, weight_ref):
    units, _, rep_count, part_rows, piece = weight_ref.shape
    for unit in range(units):
        for rep in range(rep_count):
            rows = own_ref[
                0, rep * part_rows : (rep + 1) * part_rows, unit * piece : (unit + 1) * piece
            ]
            weight_ref[unit, ids_ref[0], rep] = rows.astype(jnp.bfloat16)
        for key, ref in enumerate(held):
            for line in range(ref.shape[1]):
                weight_ref[unit, ids_ref[0] ^ (line + 1), ids_ref[1] ^ key] = ref[unit, line]


def weight_of(weight_ref, unit, shard):
    pieces = weight_ref[unit, shard]
    return pieces.reshape(pieces.shape[0] * pieces.shape[1], pieces.shape[2])


def once(shape, index):
    return pl.BlockSpec(shape, lambda *_: index, pipeline_mode=pl.Buffered(1))


def weight_args(layer, own, held, first_unit, units):
    specs = [once((1,) + own.shape[1:], (layer, 0, 0))]
    specs += [once((units,) + held[0].shape[1:], (first_unit // units, 0, 0, 0))] * len(held)
    return (far(own), *held), specs


def attend_kernel(shifted, held_count, ids_ref, x_ref, vector_ref, bias_ref, mask_ref, *refs):
    own_ref, held, refs = refs[0], refs[1 : 1 + held_count], refs[1 + held_count :]
    middle_ref, project_ref, prob_ref, attended_ref, field, states, heads_out, weight_ref = refs
    shard_count = weight_ref.shape[1]
    piece = weight_ref.shape[4]
    width = x_ref.shape[1]

    @pl.when(pl.program_id(0) == 0)
    def _():
        fill_weights(ids_ref, own_ref, held, weight_ref)

    third = 3 * shard_count // 4
    head_scale = (width // HEADS) ** (-0.5)
    into_windows(field, x_ref, shifted)
    states[ROWS:SPARE, :] = jnp.zeros((SPARE - ROWS, states.shape[1]), jnp.float32)
    unit, _ = unit_norm(field[:ROWS, :])
    normed = (unit * vector_ref[0:1, :] + vector_ref[1:2, :]).astype(jnp.bfloat16)
    for shard in range(third):
        part = dot(normed, weight_of(weight_ref, 0, shard))
        kind, start = divmod(shard * piece, width)
        if kind == 0:
            part = part + vector_ref[4:5, start : start + piece]
        if kind == 2:
            part = part + vector_ref[5:6, start : start + piece]
        states[:ROWS, shard * piece : (shard + 1) * piece] = part
        project_ref[:, shard * piece : (shard + 1) * piece] = part.astype(jnp.bfloat16)
    select = block_mask(SLOT)
    for window in range(WINDOWS):
        rows = slice(window * WINDOW_ROWS, window * WINDOW_ROWS + SLOT)
        if shifted:
            mask = mask_ref[window]
            mask = jnp.concatenate([mask] * (GROUP * SLOT // mask.shape[1]), axis=1)
        for group in range(HEADS // GROUP):
            lanes = slice(group * 128, (group + 1) * 128)
            query = states[rows, group * 128 : group * 128 + 128].astype(jnp.bfloat16)
            key = states[rows, width + group * 128 : width + group * 128 + 128]
            value = states[rows, 2 * width + group * 128 : 2 * width + group * 128 + 128]
            spread = jnp.concatenate([query] * GROUP, axis=0) * select
            cols = slice(group * GROUP * SLOT, (group + 1) * GROUP * SLOT)
            raw = dot_cols(key.astype(jnp.bfloat16), spread)[:WINDOW_ROWS]
            scores = raw * head_scale + bias_ref[:, cols]
            if shifted:
                scores = scores + mask
            top = jnp.max(scores, axis=0, keepdims=True)
            powers = jnp.exp(scores - top)
            total = jnp.sum(powers, axis=0, keepdims=True)
            soft = pad_slot(powers * (1.0 / total))
            prob_ref[window, :, cols] = soft
            crossed = dot_rows(soft, value.astype(jnp.bfloat16))
            heads_out[window * WINDOW_ROWS : (window + 1) * WINDOW_ROWS, lanes] = fold_heads(
                crossed
            )[:WINDOW_ROWS]
    attended = heads_out[...].astype(jnp.bfloat16)
    attended_ref[...] = attended
    for shard in range(third, shard_count):
        start = (shard - third) * piece
        branch = dot(attended, weight_of(weight_ref, 0, shard))
        branch = branch + vector_ref[6:7, start : start + piece]
        field[:ROWS, start : start + piece] = field[:ROWS, start : start + piece] + branch
    from_windows(middle_ref, field, shifted)


def attend(shifted, ids, x_rows, weights, vectors, bias, mask, after=()):
    layer, own, held, first_unit = weights
    rep_count, shard_count = len(held), held[0].shape[1] + 1
    part_rows, piece = held[0].shape[2:]
    width = x_rows.shape[1]
    images = x_rows.shape[0] // IMAGE_ROWS
    mask_spec = (
        pl.BlockSpec((WINDOWS,) + mask.shape[1:], lambda image: (image, 0, 0))
        if shifted
        else pl.BlockSpec(mask.shape, lambda image: (0, 0, 0))
    )
    weight_values, weight_specs = weight_args(layer, own, held, first_unit, 1)
    return ordered_call(
        functools.partial(attend_kernel, shifted, rep_count),
        (ids, x_rows, vectors, bias, mask, *weight_values),
        after,
        grid=(images,),
        in_specs=[
            pl.BlockSpec(memory_space=pltpu.SMEM),
            pl.BlockSpec((IMAGE_ROWS, width), lambda image: (image, 0)),
            once(vectors.shape, (0, 0)),
            once(bias.shape, (0, 0)),
            mask_spec,
        ]
        + weight_specs,
        out_specs=[
            pl.BlockSpec((IMAGE_ROWS, width), lambda image: (image, 0)),
            pl.BlockSpec((ROWS, 3 * width), lambda image: (image, 0)),
            pl.BlockSpec((WINDOWS, SLOT, HEADS * SLOT), lambda image: (image, 0, 0)),
            pl.BlockSpec((ROWS, width), lambda image: (image, 0)),
        ],
        out_shape=[
            jax.ShapeDtypeStruct((images * IMAGE_ROWS, width), jnp.float32),
            pltpu.HBM((images * ROWS, 3 * width), jnp.bfloat16),
            pltpu.HBM((images * WINDOWS, SLOT, HEADS * SLOT), jnp.bfloat16),
            pltpu.HBM((images * ROWS, width), jnp.bfloat16),
        ],
        scratch_shapes=[
            pltpu.VMEM((SPARE, width), jnp.float32),
            pltpu.VMEM((SPARE, 3 * width), jnp.float32),
            pltpu.VMEM((ROWS, width), jnp.float32),
            pltpu.VMEM((1, shard_count, rep_count, part_rows, piece), jnp.bfloat16),
        ],
        compiler_params=params(18 * 1024 * 1024),
        cost_estimate=cost(images * ROWS * width * width * 16, 16e6, images * ROWS * HEADS * SLOT),
        name="attend_shifted" if shifted else "attend",
    )


def row_halves(rows):
    middle = -(-rows // 32) * 16
    return [slice(0, middle), slice(middle, rows)]


def feed_kernel(held_count, final, ids_ref, middle_ref, vector_ref, inner_ref, *refs):
    own_ref, held, refs = refs[0], refs[1 : 1 + held_count], refs[1 + held_count :]
    out_ref, act_ref, slope_ref, normed, work_one, work_two, weight_ref, turned = refs[:8]
    next_ref = refs[8] if final else out_ref
    chunk = pl.program_id(0)
    blocks = middle_ref.shape[0] // IMAGE_ROWS
    units, shard_count = weight_ref.shape[:2]

    @pl.when(chunk == 0)
    def _():
        fill_weights(ids_ref, own_ref, held, weight_ref)
        for block in range(blocks):
            rows = slice(block * IMAGE_ROWS, (block + 1) * IMAGE_ROWS)
            middle = middle_ref[rows, :]
            unit, _ = unit_norm(middle)
            normed[rows, :] = (unit * vector_ref[2:3, :] + vector_ref[3:4, :]).astype(
                jnp.bfloat16
            )
            next_ref[rows, :] = middle + vector_ref[7:8, :]

    up = weight_of(weight_ref, chunk % units, chunk // units)
    down = weight_of(weight_ref, chunk % units, shard_count // 2 + chunk // units)
    turned[...] = down.T
    offset = inner_ref[0]
    halves = row_halves(blocks * IMAGE_ROWS)
    for half, work in zip(halves, (work_one, work_two)):
        work[...] = dot(normed[half, :], up)
    step = 16
    for half, work in zip(halves, (work_one, work_two)):
        for start in range(half.start, half.stop, step):
            here = slice(start, start + step)
            points = work[start - half.start : start - half.start + step, :] + offset
            below, bell = normal_parts(points)
            act_ref[here, :] = (points * below).astype(jnp.bfloat16)
            slope_ref[here, :] = (below + points * bell).astype(jnp.bfloat16)
        next_ref[half, :] += dot(act_ref[half, :], turned[...])

    if final:

        @pl.when(chunk == pl.num_programs(0) - 1)
        def _():
            for image in range(blocks):
                rows_to_field(out_ref, image, next_ref, image * IMAGE_ROWS)


def feed(ids, middle, weights, vectors, inner, final_shape=None, after=()):
    layer, own, held, first_unit = weights
    rep_count, shard_count = len(held), held[0].shape[1] + 1
    part_rows, piece = held[0].shape[2:]
    tokens, width = middle.shape
    chunks = 4 * width // piece
    units = 2 * chunks // shard_count
    weight_values, weight_specs = weight_args(layer, own, held, first_unit, units)
    return ordered_call(
        functools.partial(feed_kernel, rep_count, final_shape is not None),
        (ids, middle, vectors, inner.reshape(chunks, 1, piece), *weight_values),
        after,
        grid=(chunks,),
        in_specs=[
            pl.BlockSpec(memory_space=pltpu.SMEM),
            once((tokens, width), (0, 0)),
            once(vectors.shape, (0, 0)),
            pl.BlockSpec((1, 1, piece), lambda chunk: (chunk, 0, 0)),
        ]
        + weight_specs,
        out_specs=[
            once(final_shape, (0, 0, 0, 0)) if final_shape else once((tokens, width), (0, 0)),
            pl.BlockSpec((tokens, piece), lambda chunk: (0, chunk)),
            pl.BlockSpec((tokens, piece), lambda chunk: (0, chunk)),
        ],
        out_shape=[
            jax.ShapeDtypeStruct(final_shape, jnp.bfloat16)
            if final_shape
            else jax.ShapeDtypeStruct((tokens, width), jnp.float32),
            pltpu.HBM((tokens, chunks * piece), jnp.bfloat16),
            pltpu.HBM((tokens, chunks * piece), jnp.bfloat16),
        ],
        scratch_shapes=[
            pltpu.VMEM((tokens, width), jnp.bfloat16),
        ]
        + [
            pltpu.VMEM((half.stop - half.start, piece), jnp.float32) for half in row_halves(tokens)
        ]
        + [
            pltpu.VMEM((units, shard_count, rep_count, part_rows, piece), jnp.bfloat16),
            pltpu.VMEM((piece, width), jnp.bfloat16),
        ]
        + ([pltpu.VMEM((tokens, width), jnp.float32)] if final_shape else []),
        compiler_params=params(30 * 1024 * 1024),
        cost_estimate=cost(tokens * width * width * 16, 16e6, tokens * 8 * width),
        name="feed",
    )


def split_halves(values, stage, core, keep_ref, send_ref, lead):
    stage[...] = values.reshape(stage.shape)
    for chip in range(stage.shape[0] // 2):
        keep_ref[lead + (chip,)] = stage[2 * chip + core].astype(jnp.bfloat16)
        send_ref[lead + (chip,)] = stage[2 * chip + 1 - core].astype(jnp.bfloat16)


def feed_back_kernel(
    held_count, raw, ids_ref, count_ref, grad_ref, middle_ref, vector_ref, act_ref, slope_ref, *refs
):
    own_ref, held, refs = refs[0], refs[1 : 1 + held_count], refs[1 + held_count :]
    out_ref, small_ref, inner_ref, keep_ref, send_ref = refs[:5]
    normed, low_grad, inner_grad, total, stage, weight_ref = refs[5:11]
    turned_normed, turned_grad, turned, work_one, work_two = refs[11:16]
    field_ref, grad_ref = grad_ref, refs[16] if raw else grad_ref
    chunk = pl.program_id(0)
    core = lax.rem(ids_ref[1], 2)
    blocks = middle_ref.shape[0] // IMAGE_ROWS
    units, shard_count = weight_ref.shape[:2]

    @pl.when(chunk == 0)
    def _():
        fill_weights(ids_ref, own_ref, held, weight_ref)
        if raw:
            for image in range(blocks):
                live = jnp.where(image < count_ref[0], 1.0, 0.0)
                field_to_rows(grad_ref, image * IMAGE_ROWS, field_ref, image, live)
        bias_sum = jnp.zeros((1, low_grad.shape[1]), jnp.float32)
        for block in range(blocks):
            rows = slice(block * IMAGE_ROWS, (block + 1) * IMAGE_ROWS)
            unit, _ = unit_norm(middle_ref[rows, :])
            normed[rows, :] = (unit * vector_ref[2:3, :] + vector_ref[3:4, :]).astype(
                jnp.bfloat16
            )
            rounded = grad_ref[rows, :].astype(jnp.bfloat16)
            low_grad[rows, :] = rounded
            bias_sum = bias_sum + jnp.sum(rounded.astype(jnp.float32), axis=0, keepdims=True)
            total[rows, :] = jnp.zeros((IMAGE_ROWS, total.shape[1]), jnp.float32)
        small_ref[2:3, :] = bias_sum
        turned_normed[...] = normed[...].T
        turned_grad[...] = low_grad[...].T

    up = weight_of(weight_ref, chunk % units, chunk // units)
    down = weight_of(weight_ref, chunk % units, shard_count // 2 + chunk // units)
    turned[...] = up.T
    bias_sum = jnp.zeros((1, up.shape[1]), jnp.float32)
    halves = row_halves(blocks * IMAGE_ROWS)
    for half, work in zip(halves, (work_one, work_two)):
        work[...] = dot(low_grad[half, :], down)
    step = 16
    for half, work in zip(halves, (work_one, work_two)):
        for start in range(half.start, half.stop, step):
            here = slice(start, start + step)
            slope = slope_ref[here, :].astype(jnp.float32)
            grad_act = work[start - half.start : start - half.start + step, :]
            grad_pre = (grad_act * slope).astype(jnp.bfloat16)
            inner_grad[here, :] = grad_pre
            bias_sum = bias_sum + jnp.sum(grad_pre.astype(jnp.float32), axis=0, keepdims=True)
        total[half, :] += dot(inner_grad[half, :], turned[...])
    inner_ref[0] = bias_sum
    grad_up = dot(turned_normed[...], inner_grad[...])
    split_halves(grad_up, stage, core, keep_ref, send_ref, (0, 0, 0))
    grad_down = dot(turned_grad[...], act_ref[...])
    split_halves(grad_down, stage, core, keep_ref, send_ref, (0, 1, 0))

    @pl.when(chunk == pl.num_programs(0) - 1)
    def _():
        gain_sum = jnp.zeros((1, total.shape[1]), jnp.float32)
        offset_sum = jnp.zeros((1, total.shape[1]), jnp.float32)
        for block in range(blocks):
            rows = slice(block * IMAGE_ROWS, (block + 1) * IMAGE_ROWS)
            unit, inverse = unit_norm(middle_ref[rows, :])
            pulled = total[rows, :]
            gain_sum = gain_sum + jnp.sum(pulled * unit, axis=0, keepdims=True)
            offset_sum = offset_sum + jnp.sum(pulled, axis=0, keepdims=True)
            out_ref[rows, :] = grad_ref[rows, :] + norm_pull(
                pulled, unit, inverse, vector_ref[2:3, :]
            )
        small_ref[0:1, :] = gain_sum
        small_ref[1:2, :] = offset_sum


def feed_back(ids, counts, grad, middle, weights, vectors, act, slope, after=()):
    layer, own, held, first_unit = weights
    rep_count, shard_count = len(held), held[0].shape[1] + 1
    part_rows, piece = held[0].shape[2:]
    tokens, width = middle.shape
    chunks = 4 * width // piece
    half = shard_count // 2
    units = chunks // half
    grad_shape = (units, 2, half, rep_count // 2, part_rows, piece)
    grad_spec = pl.BlockSpec(
        (1, 2, 1) + grad_shape[3:], lambda chunk: (chunk % units, 0, chunk // units, 0, 0, 0)
    )
    weight_values, weight_specs = weight_args(layer, own, held, first_unit, units)
    out = ordered_call(
        functools.partial(feed_back_kernel, rep_count, grad.ndim > 2),
        (ids, counts, grad, middle, vectors, act, slope, *weight_values),
        after,
        grid=(chunks,),
        in_specs=[
            pl.BlockSpec(memory_space=pltpu.SMEM),
            pl.BlockSpec(memory_space=pltpu.SMEM),
            once(grad.shape, (0,) * grad.ndim),
            once((tokens, width), (0, 0)),
            once(vectors.shape, (0, 0)),
            pl.BlockSpec((tokens, piece), lambda chunk: (0, chunk)),
            pl.BlockSpec((tokens, piece), lambda chunk: (0, chunk)),
        ]
        + weight_specs,
        out_specs=[
            pl.BlockSpec((tokens, width), lambda chunk: (0, 0)),
            pl.BlockSpec((8, width), lambda chunk: (0, 0)),
            pl.BlockSpec((1, 1, piece), lambda chunk: (chunk, 0, 0)),
            grad_spec,
            grad_spec,
        ],
        out_shape=[
            jax.ShapeDtypeStruct((tokens, width), jnp.float32),
            jax.ShapeDtypeStruct((8, width), jnp.float32),
            jax.ShapeDtypeStruct((chunks, 1, piece), jnp.float32),
            jax.ShapeDtypeStruct(grad_shape, jnp.bfloat16),
            jax.ShapeDtypeStruct(grad_shape, jnp.bfloat16),
        ],
        scratch_shapes=[
            pltpu.VMEM((tokens, width), jnp.bfloat16),
            pltpu.VMEM((tokens, width), jnp.bfloat16),
            pltpu.VMEM((tokens, piece), jnp.bfloat16),
            pltpu.VMEM((tokens, width), jnp.float32),
            pltpu.VMEM((rep_count, part_rows, piece), jnp.float32),
            pltpu.VMEM((units, shard_count, rep_count, part_rows, piece), jnp.bfloat16),
            pltpu.VMEM((width, tokens), jnp.bfloat16),
            pltpu.VMEM((width, tokens), jnp.bfloat16),
            pltpu.VMEM((piece, width), jnp.bfloat16),
        ]
        + [
            pltpu.VMEM((half.stop - half.start, piece), jnp.float32) for half in row_halves(tokens)
        ]
        + ([pltpu.VMEM((tokens, width), jnp.float32)] if grad.ndim > 2 else []),
        compiler_params=params(38 * 1024 * 1024),
        cost_estimate=cost(tokens * width * width * 32, 24e6),
        name="feed_back",
    )
    flat = (units, shard_count) + grad_shape[3:]
    return out[0], out[1], out[2], out[3].reshape(flat), out[4].reshape(flat), out[5]


def attend_back_kernel(
    shifted,
    held_count,
    final,
    ids_ref,
    grad_ref,
    x_ref,
    vector_ref,
    project_ref,
    prob_ref,
    attended_ref,
    *refs,
):
    own_ref, held, refs = refs[0], refs[1 : 1 + held_count], refs[1 + held_count :]
    out_ref, small_ref, score_ref = refs[:3]
    keep_refs, send_refs, refs = refs[3:5], refs[5:7], refs[7:]
    field, grad_field, states, grad_heads, grad_states = refs[:5]
    normed_all, project_all, attended_all, grad_all, stage, weight_ref, turned = refs[5:12]
    image = pl.program_id(0)
    core = lax.rem(ids_ref[1], 2)
    shard_count = weight_ref.shape[1]
    piece = weight_ref.shape[4]
    width = x_ref.shape[1]
    third = 3 * shard_count // 4
    head_scale = (width // HEADS) ** (-0.5)
    rows_all = pl.ds(pl.multiple_of(image * ROWS, ROWS), ROWS)

    @pl.when(image == 0)
    def _():
        fill_weights(ids_ref, own_ref, held, weight_ref)
        for shard in range(shard_count):
            turned[shard] = weight_of(weight_ref, 0, shard).T
        small_ref[...] = jnp.zeros(small_ref.shape, jnp.float32)
        score_ref[...] = jnp.zeros(score_ref.shape, jnp.float32)

    into_windows(field, x_ref, shifted)
    into_windows(grad_field, grad_ref, shifted)
    unit, inverse = unit_norm(field[:ROWS, :])
    normed_all[rows_all, :] = (unit * vector_ref[0:1, :] + vector_ref[1:2, :]).astype(
        jnp.bfloat16
    )
    field[:ROWS, :] = unit
    grad_branch = grad_field[:ROWS, :].astype(jnp.bfloat16)
    grad_all[rows_all, :] = grad_branch
    attended_all[rows_all, :] = attended_ref[...]
    small_ref[4:5, :] += jnp.sum(grad_branch.astype(jnp.float32), axis=0, keepdims=True)
    grad_heads[ROWS:SPARE, :] = jnp.zeros((SPARE - ROWS, width), jnp.float32)
    states[ROWS:SPARE, :] = jnp.zeros((SPARE - ROWS, states.shape[1]), jnp.float32)
    states[:ROWS, :] = project_ref[...].astype(jnp.float32)
    branch = jnp.zeros((ROWS, width), jnp.float32)
    for shard in range(third, shard_count):
        start = (shard - third) * piece
        branch = branch + dot(grad_branch[:, start : start + piece], turned[shard])
    grad_heads[:ROWS, :] = branch
    select = block_mask(TOKENS)
    for window in range(WINDOWS):
        rows = slice(window * WINDOW_ROWS, window * WINDOW_ROWS + SLOT)
        out_rows = slice(window * WINDOW_ROWS, (window + 1) * WINDOW_ROWS)
        for group in range(HEADS // GROUP):
            first = group * 128
            cols = slice(group * GROUP * SLOT, (group + 1) * GROUP * SLOT)
            query = states[rows, first : first + 128].astype(jnp.bfloat16)
            key = states[rows, width + first : width + first + 128].astype(jnp.bfloat16)
            value = states[rows, 2 * width + first : 2 * width + first + 128].astype(jnp.bfloat16)
            arrived = grad_heads[rows, first : first + 128].astype(jnp.bfloat16)
            spread_query = jnp.concatenate([query] * GROUP, axis=0) * select
            spread_grad = jnp.concatenate([arrived] * GROUP, axis=0) * select
            soft = prob_ref[window, :, cols]
            exact = soft.astype(jnp.float32)[:WINDOW_ROWS]
            grad_soft = dot_cols(value, spread_grad)[:WINDOW_ROWS]
            delta = jnp.sum(grad_soft * exact, axis=0, keepdims=True)
            grad_scores = exact * (grad_soft - delta)
            score_ref[:, cols] += grad_scores
            grad_raw = pad_slot(grad_scores * head_scale)
            grad_key = dot(grad_raw, spread_query)[:WINDOW_ROWS]
            grad_value = dot(soft, spread_grad)[:WINDOW_ROWS]
            grad_query = fold_heads(dot_rows(grad_raw, key))[:WINDOW_ROWS]
            grad_states[out_rows, first : first + 128] = grad_query
            grad_states[out_rows, width + first : width + first + 128] = grad_key
            grad_states[out_rows, 2 * width + first : 2 * width + first + 128] = grad_value
    grad_project = grad_states[...].astype(jnp.bfloat16)
    project_all[rows_all, :] = grad_project
    column = jnp.sum(grad_project.astype(jnp.float32), axis=0, keepdims=True)
    small_ref[2:3, :] += column[:, :width]
    small_ref[3:4, :] += column[:, 2 * width :]
    pulled = jnp.zeros((ROWS, width), jnp.float32)
    for shard in range(third):
        pulled = pulled + dot(
            grad_project[:, shard * piece : (shard + 1) * piece], turned[shard]
        )
    unit = field[:ROWS, :]
    small_ref[0:1, :] += jnp.sum(pulled * unit, axis=0, keepdims=True)
    small_ref[1:2, :] += jnp.sum(pulled, axis=0, keepdims=True)
    grad_field[:ROWS, :] = grad_field[:ROWS, :] + norm_pull(
        pulled, unit, inverse, vector_ref[0:1, :]
    )
    if final:
        from_windows(refs[12], grad_field, shifted)
        rows_to_field(out_ref, 0, refs[12], 0)
    else:
        from_windows(out_ref, grad_field, shifted)

    @pl.when(image == pl.num_programs(0) - 1)
    def _():
        turned_normed, turned_attended = normed_all[...].T, attended_all[...].T
        for shard in range(shard_count):
            if shard < third:
                grad = dot(turned_normed, project_all[:, shard * piece : (shard + 1) * piece])
            else:
                start = (shard - third) * piece
                grad = dot(turned_attended, grad_all[:, start : start + piece])
            half, index = divmod(shard, shard_count // 2)
            split_halves(grad, stage, core, keep_refs[half], send_refs[half], (0, index))


def attend_back(
    shifted, ids, grad, x_rows, weights, vectors, project, prob, attended, final_shape, after=()
):
    layer, own, held, first_unit = weights
    rep_count, shard_count = len(held), held[0].shape[1] + 1
    part_rows, piece = held[0].shape[2:]
    width = x_rows.shape[1]
    images = x_rows.shape[0] // IMAGE_ROWS
    grad_shape = (1, shard_count // 2, rep_count // 2, part_rows, piece)
    weight_values, weight_specs = weight_args(layer, own, held, first_unit, 1)
    return ordered_call(
        functools.partial(attend_back_kernel, shifted, rep_count, final_shape is not None),
        (ids, grad, x_rows, vectors, project, prob, attended, *weight_values),
        after,
        grid=(images,),
        in_specs=[
            pl.BlockSpec(memory_space=pltpu.SMEM),
            pl.BlockSpec((IMAGE_ROWS, width), lambda image: (image, 0)),
            pl.BlockSpec((IMAGE_ROWS, width), lambda image: (image, 0)),
            once(vectors.shape, (0, 0)),
            pl.BlockSpec((ROWS, 3 * width), lambda image: (image, 0)),
            pl.BlockSpec((WINDOWS, SLOT, HEADS * SLOT), lambda image: (image, 0, 0)),
            pl.BlockSpec((ROWS, width), lambda image: (image, 0)),
        ]
        + weight_specs,
        out_specs=[
            pl.BlockSpec((1,) + final_shape[1:], lambda image: (image, 0, 0, 0))
            if final_shape
            else pl.BlockSpec((IMAGE_ROWS, width), lambda image: (image, 0)),
            pl.BlockSpec((8, width), lambda image: (0, 0)),
            pl.BlockSpec((WINDOW_ROWS, HEADS * SLOT), lambda image: (0, 0)),
        ]
        + [pl.BlockSpec(grad_shape, lambda image: (0, 0, 0, 0, 0))] * 4,
        out_shape=[
            jax.ShapeDtypeStruct(final_shape, jnp.bfloat16)
            if final_shape
            else jax.ShapeDtypeStruct((images * IMAGE_ROWS, width), jnp.float32),
            jax.ShapeDtypeStruct((8, width), jnp.float32),
            jax.ShapeDtypeStruct((WINDOW_ROWS, HEADS * SLOT), jnp.float32),
        ]
        + [jax.ShapeDtypeStruct(grad_shape, jnp.bfloat16)] * 4,
        scratch_shapes=[
            pltpu.VMEM((SPARE, width), jnp.float32),
            pltpu.VMEM((SPARE, width), jnp.float32),
            pltpu.VMEM((SPARE, 3 * width), jnp.float32),
            pltpu.VMEM((SPARE, width), jnp.float32),
            pltpu.VMEM((ROWS, 3 * width), jnp.float32),
            pltpu.VMEM((images * ROWS, width), jnp.bfloat16),
            pltpu.VMEM((images * ROWS, 3 * width), jnp.bfloat16),
            pltpu.VMEM((images * ROWS, width), jnp.bfloat16),
            pltpu.VMEM((images * ROWS, width), jnp.bfloat16),
            pltpu.VMEM((rep_count, part_rows, piece), jnp.float32),
            pltpu.VMEM((1, shard_count, rep_count, part_rows, piece), jnp.bfloat16),
            pltpu.VMEM((shard_count, piece, width), jnp.bfloat16),
        ]
        + ([pltpu.VMEM((IMAGE_ROWS, width), jnp.float32)] if final_shape else []),
        compiler_params=params(34 * 1024 * 1024),
        cost_estimate=cost(images * ROWS * width * width * 32, 20e6),
        name="attend_back_shifted" if shifted else "attend_back",
    )


def relay_kernel(count, extra, ids_ref, *refs):
    arrived, outs = refs[:count], refs[count:]
    for key, ref in enumerate(arrived):
        spot = 0
        for line_ref in outs[:-1] if extra else outs:
            rows = line_ref.shape[2]
            for index in range(line_ref.shape[0]):
                if ref.shape[0] == 1:
                    line_ref[index, key] = ref[0, spot * rows : (spot + 1) * rows, :]
                else:
                    line_ref[index, key] = ref[spot]
                spot += 1
        if extra:
            outs[-1][ids_ref[0] ^ (key + 1)] = ref[0, ref.shape[1] - extra :, :]


def relay(ids, arrived, split, extra, after=(), memory=SMALL_VMEM):
    units, rows, piece = arrived[0].shape
    part_rows = (units * rows - extra) // sum(split)
    shapes = [(count, len(arrived), part_rows, piece) for count in split]
    if extra:
        shapes.append((len(arrived) + 1, extra, piece))
    return ordered_call(
        functools.partial(relay_kernel, len(arrived), extra),
        (ids, *arrived),
        after,
        [pl.BlockSpec(memory_space=pltpu.SMEM)]
        + [pl.BlockSpec(memory_space=pltpu.VMEM)] * len(arrived),
        out_shape=[jax.ShapeDtypeStruct(shape, jnp.bfloat16) for shape in shapes],
        compiler_params=params(memory),
        cost_estimate=cost(0, 1e6),
        name="relay",
    )


def parts_kernel(layers, ids_ref, *refs):
    vector_ref, weight_refs, outs = refs[0], refs[1 : 1 + 2 * layers], refs[1 + 2 * layers :]
    piece = outs[0].shape[2]
    rows = weight_refs[0].shape[1]

    def units_of(index):
        ref = weight_refs[index]
        return [
            ref[0, :, start : start + piece].astype(jnp.bfloat16)
            for start in range(0, ref.shape[2], piece)
        ]

    spot = 0
    for part in units_of(1) + units_of(0):
        outs[0][0, spot : spot + rows, :] = part
        spot += rows
    lines = []
    length = vector_ref.shape[1]
    for layer in range(layers):
        for start in range(0, length, piece):
            line = vector_ref[layer : layer + 1, start : min(start + piece, length)]
            if line.shape[1] < piece:
                spare = jnp.zeros((1, piece - line.shape[1]), jnp.float32)
                line = jnp.concatenate([line, spare], axis=1)
            lines.append(line)
    lines.append(jnp.zeros((outs[0].shape[1] - spot - len(lines), piece), jnp.float32))
    outs[0][0, spot:, :] = jnp.concatenate(lines, axis=0).astype(jnp.bfloat16)
    unit = 0
    for layer in range(1, layers):
        for part in units_of(2 * layer + 1) + units_of(2 * layer):
            outs[1][unit] = part
            unit += 1


def cut_parts(ids, attention, feedforward, vectors, extra):
    layers, rows, piece = attention.shape
    part_rows = rows // lax.axis_size("rep")
    units = 1 + feedforward.shape[2] // piece

    def spec(weight, layer):
        return pl.BlockSpec(
            (1, part_rows, weight.shape[2]), lambda step, ids: (layer, ids[1], 0)
        )

    shapes = [(1, units * part_rows + extra, piece), ((layers - 1) * units, part_rows, piece)]
    return ordered_call(
        functools.partial(parts_kernel, layers),
        (ids, vectors, *([attention, feedforward] * layers)),
        (),
        [pl.BlockSpec(vectors.shape, lambda step, ids: (0, 0))]
        + [spec(weight, layer) for layer in range(layers) for weight in (attention, feedforward)],
        prefetch=1,
        grid=(1,),
        out_specs=[pl.BlockSpec(shape, lambda step, ids: (0, 0, 0)) for shape in shapes],
        out_shape=[jax.ShapeDtypeStruct(shape, jnp.bfloat16) for shape in shapes],
        compiler_params=params(),
        cost_estimate=cost(0, 5e5),
        name="cut_parts",
    )


def xor_send(value, axis, key):
    size = lax.axis_size(axis)
    return lax.ppermute(value, axis, [(index, index ^ key) for index in range(size)])


def send_line(part, gate=None):
    held = {0: part}
    for bit in reversed(range(lax.axis_size("shard").bit_length() - 1)):
        for key in list(held):
            block = held[key]
            if gate is not None and len(held) > 1:
                block, _ = lax.optimization_barrier((block, gate))
            held[key ^ (1 << bit)] = xor_send(block, "shard", 1 << bit)
    return [held[key] for key in range(1, len(held))]


def hold(chips, after=()):
    token = ()
    if after:
        *chips, token = lax.optimization_barrier((*chips, *after))
        token = [token]
    own, _ = lax.optimization_barrier((chips[0], chips[1]))
    others = [xor_send(block, "rep", 1) for block in [own] + chips[1:]]
    return [block for pair in zip(chips, others) for block in pair], token


def core_sum_kernel(units, ids_ref, *refs):
    chip = ids_ref[1] // 2
    outs = refs[2 * len(units) :]
    first = 0
    for group, count in enumerate(units):
        keep_ref, arrived_ref = refs[2 * group : 2 * group + 2]

        @pl.when((pl.program_id(0) >= first) & (pl.program_id(0) < first + count))
        def _():
            for key, out in enumerate(outs):
                for shard in range(keep_ref.shape[1]):
                    total = keep_ref[0, shard, chip ^ key].astype(jnp.float32)
                    total = total + arrived_ref[0, shard, chip ^ key].astype(jnp.float32)
                    out[0, shard] = total.astype(jnp.bfloat16)

        first += count


def core_sum(ids, pairs, after=(), moved=1e5):
    half = lax.axis_size("shard") // 2
    pairs = [
        [value.reshape((-1, half) + value.shape[2:]) for value in pair] for pair in pairs
    ]
    _, _, chips, part_rows, piece = pairs[0][0].shape
    units = [keep.shape[0] for keep, _ in pairs]
    specs, first = [], 0
    for count in units:

        def index(unit, first=first, count=count):
            return (jnp.clip(unit - first, 0, count - 1), 0, 0, 0, 0)

        specs += [pl.BlockSpec((1, half, chips, part_rows, piece), index)] * 2
        first += count
    *sums, token = ordered_call(
        functools.partial(core_sum_kernel, units),
        (ids, *[value for pair in pairs for value in pair]),
        after,
        [pl.BlockSpec(memory_space=pltpu.SMEM)] + specs,
        grid=(sum(units),),
        out_specs=[pl.BlockSpec((1, half, part_rows, piece), lambda unit: (unit, 0, 0, 0))]
        * chips,
        out_shape=[jax.ShapeDtypeStruct((sum(units), half, part_rows, piece), jnp.bfloat16)]
        * chips,
        compiler_params=params(SMALL_VMEM),
        cost_estimate=cost(1e5, moved),
        name="core_sum",
    )
    return [part.reshape((-1, 2 * half, part_rows, piece)) for part in sums] + [token]


def plane_sum_kernel(count, rows, ids_ref, *refs):
    parts, vectors, outs = refs[:count], refs[count:-2], refs[-2:]
    for key in range(parts[0].shape[1]):
        shard = ids_ref[0] ^ key
        out = outs[key % 2]
        for unit in range(parts[0].shape[0]):
            total = parts[0][unit, shard].astype(jnp.float32)
            for part in parts[1:]:
                total = total + part[unit, shard].astype(jnp.float32)
            out[key // 2, unit, :rows, :] = total.astype(jnp.bfloat16)
        if vectors:
            total = vectors[0][shard].astype(jnp.float32) + vectors[1][shard].astype(jnp.float32)
            out[key // 2, 0, rows:, :] = total.astype(jnp.bfloat16)


def plane_sum(ids, parts, vectors=(), after=(), moved=4e6):
    units, shard_count, part_rows, piece = parts[0].shape
    extra = vectors[0].shape[1] if vectors else 0
    shape = (shard_count // 2, units, part_rows + extra, piece)
    return ordered_call(
        functools.partial(plane_sum_kernel, len(parts), part_rows),
        (ids, *parts, *vectors),
        after,
        [pl.BlockSpec(memory_space=pltpu.SMEM)]
        + [pl.BlockSpec(memory_space=pltpu.VMEM)] * (len(parts) + len(vectors)),
        out_shape=[jax.ShapeDtypeStruct(shape, jnp.bfloat16)] * 2,
        compiler_params=params(SMALL_VMEM),
        cost_estimate=cost(parts[0].size * 4, moved),
        name="plane_sum",
    )


def pair_sum_kernel(keep_ref, arrived_ref, *outs):
    for index in range(keep_ref.shape[0]):
        total = keep_ref[index].astype(jnp.float32) + arrived_ref[index].astype(jnp.float32)
        outs[index % 2][index // 2] = total.astype(jnp.bfloat16)


def pair_sum(keep, arrived, after=(), moved=4e6):
    count = keep.shape[0]
    shape = (max(count // 2, 1),) + keep.shape[1:]
    return ordered_call(
        pair_sum_kernel,
        (keep, arrived),
        after,
        [pl.BlockSpec(memory_space=pltpu.VMEM)] * 2,
        out_shape=[jax.ShapeDtypeStruct(shape, jnp.bfloat16)] * min(count, 2),
        compiler_params=params(SMALL_VMEM),
        cost_estimate=cost(keep.size, moved),
        name="pair_sum",
    )


def final_sum_kernel(*refs):
    out_ref = refs[-1]
    spot = 0
    for keep_ref, arrived_ref in (refs[0:2], refs[2:4]):
        rows = keep_ref.shape[2]
        for unit in range(keep_ref.shape[1]):
            total = keep_ref[0, unit].astype(jnp.float32) + arrived_ref[0, unit].astype(jnp.float32)
            out_ref[0, spot : spot + rows, :] = total.astype(jnp.bfloat16)
            spot += rows


def final_sum(first, second, after=()):
    rows = sum(pair[0].shape[1] * pair[0].shape[2] for pair in (first, second))
    args = (*first, *second)
    return ordered_call(
        final_sum_kernel,
        args,
        after,
        [pl.BlockSpec(memory_space=pltpu.VMEM)] * len(args),
        out_shape=jax.ShapeDtypeStruct((1, rows, args[0].shape[3]), jnp.bfloat16),
        compiler_params=params(SMALL_VMEM),
        cost_estimate=cost(1e6, 4e6),
        name="final_sum",
    )


def send_pair(value):
    return xor_send(value, "rep", 1)


def send_chips(parts):
    return [parts[0]] + [
        xor_send(parts[key], "rep", 2 * key) for key in range(1, lax.axis_size("rep") // 2)
    ]


def swap_line(away):
    stage = lax.axis_size("shard") // (2 * away.shape[0])
    return xor_send(away, "shard", stage)


def narrow_line(keep, arrived, after):
    token = after[0]
    while keep.shape[0] > 1:
        keep, away, token = pair_sum(keep, arrived, [token])
        arrived = swap_line(away)
    return keep, arrived, token


def finish_line(keep, arrived, after):
    while True:
        *sums, token = pair_sum(keep, arrived, after)
        if len(sums) == 1:
            return sums[0][0], token
        keep, away = sums
        arrived, after = swap_line(away), ()


def spread(total):
    chips = [total] + [
        xor_send(total, "rep", 2 * key) for key in range(1, lax.axis_size("rep") // 2)
    ]
    others = [send_pair(block) for block in chips]
    return [block for pair in zip(chips, others) for block in pair]


def adam_terms(weight, grad, first, second, rate, decay):
    first_new = BETA_ONE * first + (1.0 - BETA_ONE) * grad
    second_new = BETA_TWO * second + (1.0 - BETA_TWO) * grad * grad
    second_hat = second_new * (1.0 / (1.0 - BETA_TWO**STEP))
    below = second_hat * lax.rsqrt(jnp.maximum(second_hat, 1e-37)) + EPS_ADAM
    near = pl.reciprocal(below, approx=True)
    near = near * (2.0 - below * near)
    weight_new = weight * (1.0 - rate * decay) - first_new * (rate / (1.0 - BETA_ONE**STEP)) * near
    return (weight_new, first_new, second_new)


def adam_kernel(count, jobs, ids_ref, *refs):
    held, refs = refs[:count], refs[count:]
    kinds = 1 + max(kind for kind, _, _ in jobs)
    states, refs = [refs[3 * kind : 3 * kind + 3] for kind in range(kinds)], refs[3 * kinds :]
    sems, refs = refs[-3:], refs[:-3]
    loaded, made = refs[-2 * len(jobs) : -len(jobs)], refs[-len(jobs) :]
    stage, refs = refs[-2 * len(jobs) - 1], refs[: -2 * len(jobs) - 1]
    outs = refs[-4 * kinds :]
    outs = [outs[4 * kind : 4 * kind + 4] for kind in range(kinds)]
    steps, rows = loaded[0].shape[1:3]
    piece = stage.shape[2]
    part_rows = rows * steps // count
    held_copies = [
        pltpu.make_async_copy(held[key].at[0], stage.at[ids_ref[1] ^ key], sems[0].at[key])
        for key in range(count)
    ]
    loads, stores = {}, {}
    for job, (kind, layer, _) in enumerate(jobs):
        for step in range(steps):
            here = pl.ds(step * rows, rows)
            loads[job, step] = [
                pltpu.make_async_copy(
                    state.at[layer, here], loaded[job].at[index, step], sems[1].at[job, index, step]
                )
                for index, state in enumerate(states[kind])
            ]
            stores[job, step] = [
                pltpu.make_async_copy(
                    made[job].at[index, step], out.at[layer, here], sems[2].at[job, index, step]
                )
                for index, out in enumerate(outs[kind])
            ]
    for copy in held_copies + [copy for copies in loads.values() for copy in copies]:
        copy.start()
    for copy in held_copies:
        copy.wait()
    for job, (_, _, first) in enumerate(jobs):
        for step in range(steps):
            for copy in loads[job, step]:
                copy.wait()
            for part in range(rows // part_rows):
                lines = slice(part * part_rows, (part + 1) * part_rows)
                for unit in range(loaded[job].shape[3] // piece):
                    cols = slice(unit * piece, (unit + 1) * piece)
                    spot = first + unit * part_rows
                    grad = stage[step * (rows // part_rows) + part, spot : spot + part_rows, :]
                    grad = grad.astype(jnp.float32)
                    made[job][0, step, lines, cols] = grad
                    new = adam_terms(
                        loaded[job][0, step, lines, cols],
                        grad,
                        loaded[job][1, step, lines, cols],
                        loaded[job][2, step, lines, cols],
                        RATE_MATRIX,
                        DECAY_MATRIX,
                    )
                    for index, value in enumerate(new):
                        made[job][index + 1, step, lines, cols] = value
            for copy in stores[job, step]:
                copy.start()
    for copies in stores.values():
        for copy in copies:
            copy.wait()


def adam(ids, held, jobs, kinds, prior=(), after=()):
    held_rows, piece = held[0].shape[1:]
    steps = 4
    states = [state for kind in kinds for state in kind]
    shapes = [kind[0].shape for kind in kinds]
    blocks = [(steps, shapes[kind][1] // steps, shapes[kind][2]) for kind, _, _ in jobs]
    start = 1 + len(held) + len(states)
    first_out = 4 * (len(kinds) - 1)
    anywhere = pl.BlockSpec(memory_space=pl.ANY)
    *outs, token = ordered_call(
        functools.partial(adam_kernel, len(held), jobs),
        (ids, *held, *states, *prior),
        after,
        [pl.BlockSpec(memory_space=pltpu.SMEM)]
        + [anywhere] * (len(held) + len(states) + len(prior)),
        out_specs=[anywhere] * (4 * len(kinds)),
        out_shape=[
            jax.ShapeDtypeStruct(shape, jnp.float32) for shape in shapes for _ in range(4)
        ],
        input_output_aliases={start + index: first_out + index for index in range(len(prior))},
        scratch_shapes=[pltpu.VMEM((len(held), held_rows, piece), jnp.bfloat16)]
        + [pltpu.VMEM((3,) + block, jnp.float32) for block in blocks]
        + [pltpu.VMEM((4,) + block, jnp.float32) for block in blocks]
        + [
            pltpu.SemaphoreType.DMA((len(held),)),
            pltpu.SemaphoreType.DMA((len(jobs), 3, steps)),
            pltpu.SemaphoreType.DMA((len(jobs), 4, steps)),
        ],
        compiler_params=params(),
        cost_estimate=cost(1e6, 3e7),
        name="adam",
    )
    return [outs[4 * kind : 4 * kind + 4] for kind in range(len(kinds))], token


def vector_adam_kernel(count, rows, ids_ref, *refs):
    totals, states = refs[:count], refs[count : count + 3]
    outs, stage = refs[count + 3 : count + 7], refs[-1]
    for key, ref in enumerate(totals):
        stage[(ids_ref[1] // 2) ^ key] = ref[0, rows:, :].astype(jnp.float32)
    total = stage[0]
    for chip in range(1, count):
        total = total + stage[chip]
    layers, length = states[0].shape
    piece = total.shape[1]
    line = 0
    for layer in range(layers):
        for start in range(0, length, piece):
            here = slice(start, min(start + piece, length))
            this = slice(layer, layer + 1)
            grad = total[line : line + 1, : here.stop - here.start]
            outs[0][this, here] = grad
            new = adam_terms(*[ref[this, here] for ref in states[:1]], grad, *[
                ref[this, here] for ref in states[1:]
            ], RATE_VECTOR, 0.0)
            for out, value in zip(outs[1:], new):
                out[this, here] = value
            line += 1


def vector_adam(ids, totals, rows, weight, first, second, after=()):
    extra = totals[0].shape[1] - rows
    return ordered_call(
        functools.partial(vector_adam_kernel, len(totals), rows),
        (ids, *totals, weight, first, second),
        after,
        [pl.BlockSpec(memory_space=pltpu.SMEM)]
        + [pl.BlockSpec(memory_space=pltpu.VMEM)] * (len(totals) + 3),
        out_shape=[jax.ShapeDtypeStruct(weight.shape, jnp.float32)] * 4,
        scratch_shapes=[pltpu.VMEM((len(totals), extra, totals[0].shape[2]), jnp.float32)],
        compiler_params=params(SMALL_VMEM),
        cost_estimate=cost(weight.size * 10, weight.size * 16),
        name="vector_adam",
    )


def join_vectors(lines, layers, length):
    shard_count, _, piece = lines.shape
    used = -(-length // piece)
    lines = lines[:, : layers * used].reshape(shard_count, layers, used * piece)[:, :, :length]
    return lines.transpose(1, 0, 2).reshape(layers, shard_count * length)


def pack_kernel(length, has_prior, rel_ref, one_ref, two_ref, inner_ref, score_ref, *refs):
    prior_ref = refs[0] if has_prior else None
    out_ref, turned = refs[-2:]
    shard_count, _, piece = out_ref.shape
    spare = jnp.zeros((SLOT - WINDOW_ROWS, score_ref.shape[1]), jnp.float32)
    turned[...] = jnp.concatenate([score_ref[...], spare], axis=0).T
    entries = lax.broadcasted_iota(jnp.int32, (SLOT, 256), 1)
    table = jnp.zeros((2 * HEADS, 256), jnp.float32)
    for token in range(TOKENS):
        exact = turned[pl.ds(token, HEADS, stride=SLOT), :]
        high = exact.astype(jnp.bfloat16)
        low = (exact - high.astype(jnp.float32)).astype(jnp.bfloat16)
        same = jnp.where(rel_ref[:, token : token + 1] == entries, 1.0, 0.0).astype(jnp.bfloat16)
        table = table + dot(jnp.concatenate([high, low], axis=0), same)
    table = table[:HEADS] + table[HEADS:]
    if piece > 256:
        table = jnp.concatenate([table, jnp.zeros((HEADS, piece - 256), jnp.float32)], axis=1)
    rows = []
    for ref, row in (
        (one_ref, 0),
        (one_ref, 1),
        (two_ref, 0),
        (two_ref, 1),
        (one_ref, 2),
        (one_ref, 3),
        (one_ref, 4),
        (two_ref, 2),
    ):
        for start in range(0, one_ref.shape[1], piece):
            rows.append(ref[row : row + 1, start : start + piece])
    rows += [inner_ref[chunk] for chunk in range(inner_ref.shape[0])]
    lanes = lax.broadcasted_iota(jnp.int32, (1, piece), 1)
    entry_rows = [jnp.zeros((1, piece), jnp.float32)] * (-(-HEADS * TABLE // piece) + 1)
    for head in range(HEADS):
        row, lane = divmod(head * TABLE, piece)
        moved = table[head : head + 1]
        if lane:
            moved = pltpu.roll(moved, lane, 1)
        entry_rows[row] = entry_rows[row] + jnp.where(lanes >= lane, moved, 0.0)
        if lane + TABLE > piece:
            entry_rows[row + 1] = entry_rows[row + 1] + jnp.where(lanes < lane, moved, 0.0)
    used = -(-length // piece)
    rows += entry_rows
    rows += [jnp.zeros((1, piece), jnp.float32)] * (-len(rows) % 8 + 8)
    flat = jnp.concatenate(rows, axis=0)
    lanes = lax.broadcasted_iota(jnp.int32, (used, piece), 1)
    for shard in range(shard_count):
        row, lane = divmod(shard * length, piece)
        moved = pltpu.roll(flat, piece - lane, 1) if lane else flat
        lines = jnp.where(lanes < piece - lane, moved[row : row + used], moved[row + 1 : row + 1 + used])
        parts = [lines]
        if has_prior:
            parts.append(prior_ref[shard, :used, :])
        count = len(parts) * used
        parts.append(jnp.zeros((out_ref.shape[1] - count, piece), jnp.float32))
        out_ref[shard] = jnp.concatenate(parts, axis=0).astype(out_ref.dtype)


def pack(rel_slots, small_one, small_two, inner, scores, length, extra, prior=None, after=()):
    shard_count = lax.axis_size("shard")
    prior = () if prior is None else (prior,)
    args = (rel_slots, small_one, small_two, inner, scores) + prior
    return ordered_call(
        functools.partial(pack_kernel, length, len(prior)),
        args,
        after,
        [pl.BlockSpec(memory_space=pltpu.VMEM)] * len(args),
        out_shape=jax.ShapeDtypeStruct(
            (shard_count, extra if prior else 8, inner.shape[2]),
            jnp.bfloat16 if prior else jnp.float32,
        ),
        scratch_shapes=[pltpu.VMEM((HEADS * SLOT, SLOT), jnp.float32)],
        compiler_params=params(SMALL_VMEM),
        cost_estimate=cost(1e6, 1e6),
        name="pack",
    )


def image_rows(field):
    images, width = field.shape[0], field.shape[-1]
    flat = field.reshape(images, IMAGE, width)
    flat = jnp.pad(flat, ((0, 0), (0, IMAGE_ROWS - IMAGE), (0, 0)))
    return flat.reshape(images * IMAGE_ROWS, width)


def pair_mask(region_ids):
    images = region_ids.shape[0]
    cells = region_ids.reshape(images, ACROSS, WINDOW, ACROSS, WINDOW).transpose(0, 1, 3, 2, 4)
    cells = cells.reshape(images * WINDOWS, TOKENS)
    keys = jnp.pad(cells, ((0, 0), (0, WINDOW_ROWS - TOKENS)))
    queries = jnp.pad(cells, ((0, 0), (0, SLOT - TOKENS)))
    queries = jnp.concatenate([queries] * (128 // SLOT), axis=1)
    same = keys[:, :, None] == queries[:, None, :]
    return jnp.where(same, jnp.float32(0.0), jnp.float32(MASK_FILL))


def pair_slots(rel_index):
    spare = SLOT - TOKENS
    return jnp.pad(rel_index.T, ((0, spare), (0, spare)), constant_values=-1)


def pair_onehot(rel_slots):
    turned = rel_slots[:WINDOW_ROWS].reshape(1, -1)
    return (jnp.arange(TABLE)[:, None] == turned).astype(jnp.bfloat16)


def spread_table(table, onehot):
    bias = dot(table, onehot).reshape(HEADS, WINDOW_ROWS, SLOT).transpose(1, 0, 2)
    bias = bias.reshape(WINDOW_ROWS, HEADS * SLOT)
    real = jnp.arange(WINDOW_ROWS)[:, None] < TOKENS
    return jnp.where(real, bias, jnp.float32(PAD_FILL))


def shards(
    images,
    region_ids,
    image_counts,
    rel_index,
    cotangent,
    attention_weight,
    feedforward_weight,
    vector_params,
    attention_first,
    feedforward_first,
    vector_first,
    attention_second,
    feedforward_second,
    vector_second,
):
    shard_id, rep_id = lax.axis_index("shard"), lax.axis_index("rep")
    ids = jnp.stack([shard_id, rep_id]).astype(jnp.int32)
    width, piece = attention_weight.shape[1:]
    layers, length = vector_params.shape
    extra = -(-layers * -(-length // piece) // 16) * 16
    attention, feedforward = attention_weight, feedforward_weight

    rel_slots = pair_slots(rel_index)
    onehot = pair_onehot(rel_slots)
    mask = pair_mask(region_ids)
    no_mask = jnp.zeros((1, 8, 128), jnp.float32)
    residual = image_rows(images.astype(jnp.float32))

    feed_units = feedforward.shape[2] // piece
    part_zero, part_one, _ = cut_parts(ids, attention, feedforward, vector_params, extra)
    arrived_zero = send_line(part_zero)
    part_one, _ = lax.optimization_barrier((part_one, arrived_zero[1]))
    arrived_one = send_line(part_one, arrived_zero[-1])
    line_zero, lines, token = relay(ids, arrived_zero, [feed_units + 1], extra)
    lines = lax.dynamic_update_index_in_dim(lines, part_zero[0, -extra:], shard_id, 0)
    vectors_full = join_vectors(lines, layers, length)
    bulks = [flat[: 12 * width].astype(jnp.float32).reshape(12, width) for flat in vectors_full]
    inners = [bulk[8:].reshape(-1, 1, piece) for bulk in bulks]
    biases = [
        spread_table(flat[12 * width :].reshape(HEADS, -1), onehot) for flat in vectors_full
    ]
    chip_count = lax.axis_size("rep") // 2
    chips_zero = send_chips([line_zero] * chip_count)
    line_one, token = relay(ids, arrived_one, [feed_units + 1], 0)
    held_zero, token = hold(chips_zero, [token])
    chips_one = send_chips([line_one] * chip_count)
    attend_weights = [(0, attention, held_zero, feed_units)]
    feed_weights = [(0, feedforward, held_zero, 0)]
    first = attend(
        False,
        ids,
        residual,
        attend_weights[0],
        bulks[0],
        biases[0],
        no_mask,
        [*token, mask, biases[1], *bulks, *inners],
    )
    second = feed(ids, first[0], feed_weights[0], bulks[0], inners[0])
    held_one, token = hold(chips_one, [second[3]])
    attend_weights.append((1, attention, held_one, feed_units))
    feed_weights.append((1, feedforward, held_one, 0))
    stored = [(residual, bulks[0]) + tuple(first[:4]) + tuple(second[1:3])]
    residual = second[0]
    first = attend(
        True,
        ids,
        residual,
        attend_weights[1],
        bulks[1],
        biases[1],
        mask,
        token,
    )
    second = feed(ids, first[0], feed_weights[1], bulks[1], inners[1], images.shape)
    stored.append((residual, bulks[1]) + tuple(first[:4]) + tuple(second[1:3]))
    block_out = second[0]

    def back_feed(layer, grad, after):
        _, bulk, middle, _, _, _, act, slope = stored[layer]
        layer_id, own, held, first_unit = feed_weights[layer]
        weights = (layer_id, own, [far(block) for block in held], first_unit)
        if layer == LAYERS - 1:
            grad = far(grad)
        return feed_back(
            ids, image_counts, grad, far(middle), weights, bulk, far(act), far(slope), after
        )

    def back_attend(layer, grad, after):
        residual, bulk, _, project, prob, attended, _, _ = stored[layer]
        layer_id, own, held, first_unit = attend_weights[layer]
        weights = (layer_id, own, [far(block) for block in held], first_unit)
        return attend_back(
            layer % 2 == 1,
            ids,
            grad,
            far(residual),
            weights,
            bulk,
            far(project),
            far(prob),
            far(attended),
            images.shape if layer == 0 else None,
            after,
        )

    grad_state, small_f1, inner_f1, keep_f1, send_f1, _ = back_feed(1, cotangent, ())
    came_f1 = send_pair(send_f1)
    grad_state, small_a1, scores_a1, *halves, token = back_attend(1, grad_state, ())
    pairs_a1 = [(halves[index], send_pair(halves[2 + index])) for index in range(2)]
    *chips, token = core_sum(ids, [(keep_f1, came_f1)], [token])
    chips_f1 = send_chips(chips)
    grad_state, small_f0, inner_f0, keep_f0, send_f0, token = back_feed(0, grad_state, [token])
    keep_f1, away, token = plane_sum(ids, chips_f1, (), [token], 60e6)
    came_f0 = send_pair(lax.optimization_barrier((send_f0, token))[0])
    came_f1 = swap_line(away)
    vector_one, token = pack(
        rel_slots, small_a1, small_f1, inner_f1, scores_a1, length, extra, None, [token]
    )
    *chips, token = core_sum(ids, pairs_a1 + [(keep_f0, came_f0)], [token], 4e6)
    chips_af = send_chips(chips)
    keep_f1, away, token = pair_sum(keep_f1, came_f1, [token])
    came_f1 = swap_line(away)
    input_grad, small_a0, scores_a0, *halves, token = back_attend(0, grad_state, [token])
    total_f1, token = finish_line(keep_f1, came_f1, [token])
    *send_a0, _ = lax.optimization_barrier((*halves[2:], token))
    pairs_a0 = [(halves[index], send_pair(send_a0[index])) for index in range(2)]
    *chips, token = core_sum(ids, pairs_a0, [token])
    chips_a0 = send_chips(chips)
    vectors, token = pack(
        rel_slots, small_a0, small_f0, inner_f0, scores_a0, length, extra, vector_one, [token]
    )
    came_vectors = send_pair(vectors)
    keep_af, away, token = plane_sum(ids, chips_af, (), [token], 1e5)
    came_af = swap_line(away)
    total_f1, token = lax.optimization_barrier((total_f1, token))
    chips_f1 = send_chips([total_f1.reshape(1, -1, piece)] * (lax.axis_size("rep") // 2))
    keep_af, came_af, token = narrow_line(keep_af, came_af, [token])
    keep_a0, away, token = plane_sum(ids, chips_a0, (vectors, came_vectors), [token])
    came_a0 = swap_line(away)
    keep_a0, came_a0, token = narrow_line(keep_a0, came_a0, [token])
    held_f1, (token,) = hold(chips_f1, [token])
    total, token = final_sum((keep_af, came_af), (keep_a0, came_a0), [token])
    chips = send_chips([total] * (lax.axis_size("rep") // 2))
    attention_states = (attention, attention_first, attention_second)
    feedforward_states = (feedforward, feedforward_first, feedforward_second)
    part_rows = attention.shape[1] // lax.axis_size("rep")
    (feedforward_out,), token = adam(ids, held_f1, ((0, 1, 0),), (feedforward_states,), (), [token])
    held, (token,) = hold(chips, [token])
    *vector_out, token = vector_adam(
        ids,
        held[::2],
        total.shape[1] - extra,
        vector_params,
        vector_first,
        vector_second,
        [token],
    )
    (attention_out, feedforward_out), _ = adam(
        ids,
        held,
        ((0, 1, 0), (1, 0, part_rows), (0, 0, part_rows * (1 + feed_units))),
        (attention_states, feedforward_states),
        feedforward_out,
        [token],
    )
    vector_grad, vector_new, first_vector, second_vector = vector_out
    attention_grad, attention_new, first_attention, second_attention = attention_out
    feedforward_grad, feedforward_new, first_feedforward, second_feedforward = feedforward_out
    return (
        block_out,
        input_grad,
        attention_grad,
        feedforward_grad,
        vector_grad,
        attention_new,
        feedforward_new,
        vector_new,
        first_attention,
        first_feedforward,
        first_vector,
        second_attention,
        second_feedforward,
        second_vector,
    )


def solution(mesh):
    rows = P(("shard", "rep"), None, None, None)
    matrix = P(None, None, "shard")
    vector = P(None, "shard")
    states = (matrix, matrix, vector)
    return jax.shard_map(
        shards,
        mesh=mesh,
        in_specs=(rows, P(("shard", "rep"), None, None), P(("shard", "rep")), P(), rows)
        + states * 3,
        out_specs=(rows, rows) + states * 4,
        check_vma=False,
    )
```

```python
import functools

import jax
import jax.numpy as jnp
from jax import lax
from jax.experimental import pallas as pl
from jax.experimental.pallas import tpu as pltpu
from jax.sharding import PartitionSpec as P

HEADS = 16
WINDOW = 7
SIDE = 14
SHIFT = 3
TABLE = 169
LAYERS = 2
STEP = 10

EPS_NORM = 1e-05
EPS_ADAM = 1e-08
BETA_ONE = 0.9
BETA_TWO = 0.999
RATE_MATRIX = 0.1
RATE_VECTOR = 1.0
DECAY_MATRIX = 0.05
MASK_FILL = -100.0
PAD_FILL = -1e30
HIGH = lax.Precision.HIGHEST

ACROSS = SIDE // WINDOW
WINDOWS = ACROSS * ACROSS
TOKENS = WINDOW * WINDOW
IMAGE = SIDE * SIDE
IMAGE_ROWS = 208
WINDOW_ROWS = 56
SLOT = 64
ROWS = WINDOWS * WINDOW_ROWS
SPARE = ROWS + 8
GROUP = 4
VMEM_BYTES = 56 * 1024 * 1024
SMALL_VMEM = 14 * 1024 * 1024


def params(bytes_limit=VMEM_BYTES):
    return pltpu.CompilerParams(vmem_limit_bytes=bytes_limit)


def cost(flops, moved, exps=0):
    return pl.CostEstimate(flops=int(flops), bytes_accessed=int(moved), transcendentals=int(exps))


def ordered_call(body, args, after, in_specs, prefetch=0, grid=None, **rest):
    count, extra = len(args), len(after)
    shapes = rest.pop("out_shape")
    shapes = list(shapes) if isinstance(shapes, (list, tuple)) else [shapes]
    results = len(shapes)

    def run(*refs):
        ins, refs = refs[:count], refs[count + extra :]
        outs, token, scratch = refs[:results], refs[results], refs[results + 1 :]
        token[...] = jnp.zeros(token.shape, token.dtype)
        return body(*ins, *outs, *scratch)

    in_specs = list(in_specs) + [pl.BlockSpec(memory_space=pl.ANY)] * extra
    out_specs = rest.pop("out_specs", [pl.BlockSpec(memory_space=pltpu.VMEM)] * results)
    out_specs = list(out_specs) if isinstance(out_specs, (list, tuple)) else [out_specs]
    if grid is None:
        out_specs.append(pl.BlockSpec(memory_space=pltpu.VMEM))
    else:
        out_specs.append(pl.BlockSpec((8, 128), lambda *_: (0, 0)))
    shapes.append(jax.ShapeDtypeStruct((8, 128), jnp.float32))
    if prefetch:
        rest["grid_spec"] = pltpu.PrefetchScalarGridSpec(
            num_scalar_prefetch=prefetch,
            grid=grid,
            in_specs=in_specs,
            out_specs=out_specs,
            scratch_shapes=rest.pop("scratch_shapes", ()),
        )
    else:
        rest.update(in_specs=in_specs, out_specs=out_specs)
        if grid is not None:
            rest["grid"] = grid
    return pl.pallas_call(run, out_shape=shapes, **rest)(*args, *after)


def far(value):
    return pltpu.with_memory_space_constraint(value, pltpu.HBM)


def dot(left, right):
    return jnp.dot(left, right, preferred_element_type=jnp.float32)


def dot_cols(left, right):
    return lax.dot_general(
        left, right, (((1,), (1,)), ((), ())), preferred_element_type=jnp.float32
    )


def dot_rows(left, right):
    return lax.dot_general(
        left, right, (((0,), (0,)), ((), ())), preferred_element_type=jnp.float32
    )


def segments(shifted):
    move = SHIFT if shifted else 0
    found = []
    for down in range(ACROSS):
        for right in range(ACROSS):
            base = (down * ACROSS + right) * WINDOW_ROWS
            for line in range(WINDOW):
                row = (down * WINDOW + line + move) % SIDE
                col = (right * WINDOW + move) % SIDE
                first = min(WINDOW, SIDE - col)
                spot = base + line * WINDOW
                found.append((spot, row * SIDE + col, first))
                if first < WINDOW:
                    found.append((spot + first, row * SIDE, WINDOW - first))
    return found


def into_windows(window_ref, image_ref, shifted):
    for window in range(WINDOWS):
        start = window * WINDOW_ROWS + TOKENS
        stop = (window + 1) * WINDOW_ROWS
        window_ref[start:stop, :] = jnp.zeros((stop - start, window_ref.shape[1]), jnp.float32)
    for spot, source, count in segments(shifted):
        window_ref[spot : spot + count, :] = image_ref[source : source + count, :]


def from_windows(image_ref, window_ref, shifted):
    image_ref[IMAGE:IMAGE_ROWS, :] = jnp.zeros(
        (IMAGE_ROWS - IMAGE, image_ref.shape[1]), jnp.float32
    )
    for spot, source, count in segments(shifted):
        image_ref[source : source + count, :] = window_ref[spot : spot + count, :]


def rows_to_field(field_ref, image, rows_ref, start):
    for line in range(SIDE):
        here = slice(start + line * SIDE, start + (line + 1) * SIDE)
        field_ref[image, line] = rows_ref[here, :].astype(jnp.bfloat16)


def field_to_rows(rows_ref, start, field_ref, image, factor):
    for line in range(SIDE):
        here = slice(start + line * SIDE, start + (line + 1) * SIDE)
        rows_ref[here, :] = field_ref[image, line].astype(jnp.float32) * factor
    rows_ref[start + IMAGE : start + IMAGE_ROWS, :] = jnp.zeros(
        (IMAGE_ROWS - IMAGE, rows_ref.shape[1]), jnp.float32
    )


def unit_norm(values):
    width = values.shape[-1]
    centered = values - jnp.sum(values, axis=-1, keepdims=True) * (1.0 / width)
    variance = jnp.sum(centered * centered, axis=-1, keepdims=True) * (1.0 / width)
    inverse = lax.rsqrt(variance + EPS_NORM)
    return centered * inverse, inverse


def normal_parts(points):
    below = 0.5 + 0.5 * lax.erf(points * (0.5**0.5))
    return below, jnp.exp(points * points * -0.5) * 0.3989422804014327


def norm_pull(grad, unit, inverse, gain):
    width = grad.shape[-1]
    scaled = grad * gain
    mean_one = jnp.sum(scaled, axis=-1, keepdims=True) * (1.0 / width)
    mean_two = jnp.sum(scaled * unit, axis=-1, keepdims=True) * (1.0 / width)
    return inverse * (scaled - mean_one - unit * mean_two)


def block_mask(token_limit):
    rows = lax.broadcasted_iota(jnp.int32, (GROUP * SLOT, GROUP * 32), 0)
    cols = lax.broadcasted_iota(jnp.int32, (GROUP * SLOT, GROUP * 32), 1)
    keep = ((rows // SLOT) == (cols // 32)) & ((rows % SLOT) < token_limit)
    return jnp.where(keep, 1.0, 0.0).astype(jnp.bfloat16)


def fold_heads(crossed):
    lanes = lax.broadcasted_iota(jnp.int32, (SLOT, GROUP * 32), 1) // 32
    total = jnp.where(lanes == 0, crossed[:SLOT], 0.0)
    for head in range(1, GROUP):
        part = crossed[head * SLOT : (head + 1) * SLOT]
        total = jnp.where(lanes == head, part, total)
    return total


def pad_slot(values):
    spare = jnp.zeros((SLOT - WINDOW_ROWS, values.shape[1]), jnp.float32)
    return jnp.concatenate([values, spare], axis=0).astype(jnp.bfloat16)


def fill_weights(ids_ref, own_ref, held, weight_ref):
    units, _, rep_count, part_rows, piece = weight_ref.shape
    for unit in range(units):
        for rep in range(rep_count):
            rows = own_ref[
                0, rep * part_rows : (rep + 1) * part_rows, unit * piece : (unit + 1) * piece
            ]
            weight_ref[unit, ids_ref[0], rep] = rows.astype(jnp.bfloat16)
        for key, ref in enumerate(held):
            for line in range(ref.shape[1]):
                weight_ref[unit, ids_ref[0] ^ (line + 1), ids_ref[1] ^ key] = ref[unit, line]


def weight_of(weight_ref, unit, shard):
    pieces = weight_ref[unit, shard]
    return pieces.reshape(pieces.shape[0] * pieces.shape[1], pieces.shape[2])


def once(shape, index):
    return pl.BlockSpec(shape, lambda *_: index, pipeline_mode=pl.Buffered(1))


def weight_args(layer, own, held, first_unit, units):
    specs = [once((1,) + own.shape[1:], (layer, 0, 0))]
    specs += [once((units,) + held[0].shape[1:], (first_unit // units, 0, 0, 0))] * len(held)
    return (far(own), *held), specs


def attend_kernel(shifted, held_count, ids_ref, x_ref, vector_ref, bias_ref, mask_ref, *refs):
    own_ref, held, refs = refs[0], refs[1 : 1 + held_count], refs[1 + held_count :]
    middle_ref, project_ref, prob_ref, attended_ref, field, states, heads_out, weight_ref = refs
    shard_count = weight_ref.shape[1]
    piece = weight_ref.shape[4]
    width = x_ref.shape[1]

    @pl.when(pl.program_id(0) == 0)
    def _():
        fill_weights(ids_ref, own_ref, held, weight_ref)

    third = 3 * shard_count // 4
    head_scale = (width // HEADS) ** (-0.5)
    into_windows(field, x_ref, shifted)
    states[ROWS:SPARE, :] = jnp.zeros((SPARE - ROWS, states.shape[1]), jnp.float32)
    unit, _ = unit_norm(field[:ROWS, :])
    normed = (unit * vector_ref[0:1, :] + vector_ref[1:2, :]).astype(jnp.bfloat16)
    for shard in range(third):
        part = dot(normed, weight_of(weight_ref, 0, shard))
        kind, start = divmod(shard * piece, width)
        if kind == 0:
            part = part + vector_ref[4:5, start : start + piece]
        if kind == 2:
            part = part + vector_ref[5:6, start : start + piece]
        states[:ROWS, shard * piece : (shard + 1) * piece] = part
        project_ref[:, shard * piece : (shard + 1) * piece] = part.astype(jnp.bfloat16)
    select = block_mask(SLOT)
    for window in range(WINDOWS):
        rows = slice(window * WINDOW_ROWS, window * WINDOW_ROWS + SLOT)
        if shifted:
            mask = mask_ref[window]
            mask = jnp.concatenate([mask] * (GROUP * SLOT // mask.shape[1]), axis=1)
        for group in range(HEADS // GROUP):
            lanes = slice(group * 128, (group + 1) * 128)
            query = states[rows, group * 128 : group * 128 + 128].astype(jnp.bfloat16)
            key = states[rows, width + group * 128 : width + group * 128 + 128]
            value = states[rows, 2 * width + group * 128 : 2 * width + group * 128 + 128]
            spread = jnp.concatenate([query] * GROUP, axis=0) * select
            cols = slice(group * GROUP * SLOT, (group + 1) * GROUP * SLOT)
            raw = dot_cols(key.astype(jnp.bfloat16), spread)[:WINDOW_ROWS]
            scores = raw * head_scale + bias_ref[:, cols]
            if shifted:
                scores = scores + mask
            top = jnp.max(scores, axis=0, keepdims=True)
            powers = jnp.exp(scores - top)
            total = jnp.sum(powers, axis=0, keepdims=True)
            soft = pad_slot(powers * (1.0 / total))
            prob_ref[window, :, cols] = soft
            crossed = dot_rows(soft, value.astype(jnp.bfloat16))
            heads_out[window * WINDOW_ROWS : (window + 1) * WINDOW_ROWS, lanes] = fold_heads(
                crossed
            )[:WINDOW_ROWS]
    attended = heads_out[...].astype(jnp.bfloat16)
    attended_ref[...] = attended
    for shard in range(third, shard_count):
        start = (shard - third) * piece
        branch = dot(attended, weight_of(weight_ref, 0, shard))
        branch = branch + vector_ref[6:7, start : start + piece]
        field[:ROWS, start : start + piece] = field[:ROWS, start : start + piece] + branch
    from_windows(middle_ref, field, shifted)


def attend(shifted, ids, x_rows, weights, vectors, bias, mask, after=()):
    layer, own, held, first_unit = weights
    rep_count, shard_count = len(held), held[0].shape[1] + 1
    part_rows, piece = held[0].shape[2:]
    width = x_rows.shape[1]
    images = x_rows.shape[0] // IMAGE_ROWS
    mask_spec = (
        pl.BlockSpec((WINDOWS,) + mask.shape[1:], lambda image: (image, 0, 0))
        if shifted
        else pl.BlockSpec(mask.shape, lambda image: (0, 0, 0))
    )
    weight_values, weight_specs = weight_args(layer, own, held, first_unit, 1)
    return ordered_call(
        functools.partial(attend_kernel, shifted, rep_count),
        (ids, x_rows, vectors, bias, mask, *weight_values),
        after,
        grid=(images,),
        in_specs=[
            pl.BlockSpec(memory_space=pltpu.SMEM),
            pl.BlockSpec((IMAGE_ROWS, width), lambda image: (image, 0)),
            once(vectors.shape, (0, 0)),
            once(bias.shape, (0, 0)),
            mask_spec,
        ]
        + weight_specs,
        out_specs=[
            pl.BlockSpec((IMAGE_ROWS, width), lambda image: (image, 0)),
            pl.BlockSpec((ROWS, 3 * width), lambda image: (image, 0)),
            pl.BlockSpec((WINDOWS, SLOT, HEADS * SLOT), lambda image: (image, 0, 0)),
            pl.BlockSpec((ROWS, width), lambda image: (image, 0)),
        ],
        out_shape=[
            jax.ShapeDtypeStruct((images * IMAGE_ROWS, width), jnp.float32),
            pltpu.HBM((images * ROWS, 3 * width), jnp.bfloat16),
            pltpu.HBM((images * WINDOWS, SLOT, HEADS * SLOT), jnp.bfloat16),
            pltpu.HBM((images * ROWS, width), jnp.bfloat16),
        ],
        scratch_shapes=[
            pltpu.VMEM((SPARE, width), jnp.float32),
            pltpu.VMEM((SPARE, 3 * width), jnp.float32),
            pltpu.VMEM((ROWS, width), jnp.float32),
            pltpu.VMEM((1, shard_count, rep_count, part_rows, piece), jnp.bfloat16),
        ],
        compiler_params=params(18 * 1024 * 1024),
        cost_estimate=cost(images * ROWS * width * width * 16, 16e6, images * ROWS * HEADS * SLOT),
        name="attend_shifted" if shifted else "attend",
    )


def row_halves(rows):
    middle = -(-rows // 32) * 16
    return [slice(0, middle), slice(middle, rows)]


def feed_kernel(held_count, final, ids_ref, middle_ref, vector_ref, inner_ref, *refs):
    own_ref, held, refs = refs[0], refs[1 : 1 + held_count], refs[1 + held_count :]
    out_ref, act_ref, slope_ref, normed, work_one, work_two, weight_ref, turned = refs[:8]
    next_ref = refs[8] if final else out_ref
    chunk = pl.program_id(0)
    blocks = middle_ref.shape[0] // IMAGE_ROWS
    units, shard_count = weight_ref.shape[:2]

    @pl.when(chunk == 0)
    def _():
        fill_weights(ids_ref, own_ref, held, weight_ref)
        for block in range(blocks):
            rows = slice(block * IMAGE_ROWS, (block + 1) * IMAGE_ROWS)
            middle = middle_ref[rows, :]
            unit, _ = unit_norm(middle)
            normed[rows, :] = (unit * vector_ref[2:3, :] + vector_ref[3:4, :]).astype(
                jnp.bfloat16
            )
            next_ref[rows, :] = middle + vector_ref[7:8, :]

    up = weight_of(weight_ref, chunk % units, chunk // units)
    down = weight_of(weight_ref, chunk % units, shard_count // 2 + chunk // units)
    turned[...] = down.T
    offset = inner_ref[0]
    halves = row_halves(blocks * IMAGE_ROWS)
    for half, work in zip(halves, (work_one, work_two)):
        work[...] = dot(normed[half, :], up)
    step = 16
    for half, work in zip(halves, (work_one, work_two)):
        for start in range(half.start, half.stop, step):
            here = slice(start, start + step)
            points = work[start - half.start : start - half.start + step, :] + offset
            below, bell = normal_parts(points)
            act_ref[here, :] = (points * below).astype(jnp.bfloat16)
            slope_ref[here, :] = (below + points * bell).astype(jnp.bfloat16)
        next_ref[half, :] += dot(act_ref[half, :], turned[...])

    if final:

        @pl.when(chunk == pl.num_programs(0) - 1)
        def _():
            for image in range(blocks):
                rows_to_field(out_ref, image, next_ref, image * IMAGE_ROWS)


def feed(ids, middle, weights, vectors, inner, final_shape=None, after=()):
    layer, own, held, first_unit = weights
    rep_count, shard_count = len(held), held[0].shape[1] + 1
    part_rows, piece = held[0].shape[2:]
    tokens, width = middle.shape
    chunks = 4 * width // piece
    units = 2 * chunks // shard_count
    weight_values, weight_specs = weight_args(layer, own, held, first_unit, units)
    return ordered_call(
        functools.partial(feed_kernel, rep_count, final_shape is not None),
        (ids, middle, vectors, inner.reshape(chunks, 1, piece), *weight_values),
        after,
        grid=(chunks,),
        in_specs=[
            pl.BlockSpec(memory_space=pltpu.SMEM),
            once((tokens, width), (0, 0)),
            once(vectors.shape, (0, 0)),
            pl.BlockSpec((1, 1, piece), lambda chunk: (chunk, 0, 0)),
        ]
        + weight_specs,
        out_specs=[
            once(final_shape, (0, 0, 0, 0)) if final_shape else once((tokens, width), (0, 0)),
            pl.BlockSpec((tokens, piece), lambda chunk: (0, chunk)),
            pl.BlockSpec((tokens, piece), lambda chunk: (0, chunk)),
        ],
        out_shape=[
            jax.ShapeDtypeStruct(final_shape, jnp.bfloat16)
            if final_shape
            else jax.ShapeDtypeStruct((tokens, width), jnp.float32),
            pltpu.HBM((tokens, chunks * piece), jnp.bfloat16),
            pltpu.HBM((tokens, chunks * piece), jnp.bfloat16),
        ],
        scratch_shapes=[
            pltpu.VMEM((tokens, width), jnp.bfloat16),
        ]
        + [
            pltpu.VMEM((half.stop - half.start, piece), jnp.float32) for half in row_halves(tokens)
        ]
        + [
            pltpu.VMEM((units, shard_count, rep_count, part_rows, piece), jnp.bfloat16),
            pltpu.VMEM((piece, width), jnp.bfloat16),
        ]
        + ([pltpu.VMEM((tokens, width), jnp.float32)] if final_shape else []),
        compiler_params=params(30 * 1024 * 1024),
        cost_estimate=cost(tokens * width * width * 16, 16e6, tokens * 8 * width),
        name="feed",
    )


def split_halves(values, stage, core, keep_ref, send_ref, lead):
    stage[...] = values.reshape(stage.shape)
    for chip in range(stage.shape[0] // 2):
        keep_ref[lead + (chip,)] = stage[2 * chip + core].astype(jnp.bfloat16)
        send_ref[lead + (chip,)] = stage[2 * chip + 1 - core].astype(jnp.bfloat16)


def feed_back_kernel(
    held_count, raw, ids_ref, count_ref, grad_ref, middle_ref, vector_ref, act_ref, slope_ref, *refs
):
    own_ref, held, refs = refs[0], refs[1 : 1 + held_count], refs[1 + held_count :]
    out_ref, small_ref, inner_ref, keep_ref, send_ref = refs[:5]
    normed, low_grad, inner_grad, total, stage, weight_ref = refs[5:11]
    turned_normed, turned_grad, turned, work_one, work_two = refs[11:16]
    field_ref, grad_ref = grad_ref, refs[16] if raw else grad_ref
    chunk = pl.program_id(0)
    core = lax.rem(ids_ref[1], 2)
    blocks = middle_ref.shape[0] // IMAGE_ROWS
    units, shard_count = weight_ref.shape[:2]

    @pl.when(chunk == 0)
    def _():
        fill_weights(ids_ref, own_ref, held, weight_ref)
        if raw:
            for image in range(blocks):
                live = jnp.where(image < count_ref[0], 1.0, 0.0)
                field_to_rows(grad_ref, image * IMAGE_ROWS, field_ref, image, live)
        bias_sum = jnp.zeros((1, low_grad.shape[1]), jnp.float32)
        for block in range(blocks):
            rows = slice(block * IMAGE_ROWS, (block + 1) * IMAGE_ROWS)
            unit, _ = unit_norm(middle_ref[rows, :])
            normed[rows, :] = (unit * vector_ref[2:3, :] + vector_ref[3:4, :]).astype(
                jnp.bfloat16
            )
            rounded = grad_ref[rows, :].astype(jnp.bfloat16)
            low_grad[rows, :] = rounded
            bias_sum = bias_sum + jnp.sum(rounded.astype(jnp.float32), axis=0, keepdims=True)
            total[rows, :] = jnp.zeros((IMAGE_ROWS, total.shape[1]), jnp.float32)
        small_ref[2:3, :] = bias_sum
        turned_normed[...] = normed[...].T
        turned_grad[...] = low_grad[...].T

    up = weight_of(weight_ref, chunk % units, chunk // units)
    down = weight_of(weight_ref, chunk % units, shard_count // 2 + chunk // units)
    turned[...] = up.T
    bias_sum = jnp.zeros((1, up.shape[1]), jnp.float32)
    halves = row_halves(blocks * IMAGE_ROWS)
    for half, work in zip(halves, (work_one, work_two)):
        work[...] = dot(low_grad[half, :], down)
    step = 16
    for half, work in zip(halves, (work_one, work_two)):
        for start in range(half.start, half.stop, step):
            here = slice(start, start + step)
            slope = slope_ref[here, :].astype(jnp.float32)
            grad_act = work[start - half.start : start - half.start + step, :]
            grad_pre = (grad_act * slope).astype(jnp.bfloat16)
            inner_grad[here, :] = grad_pre
            bias_sum = bias_sum + jnp.sum(grad_pre.astype(jnp.float32), axis=0, keepdims=True)
        total[half, :] += dot(inner_grad[half, :], turned[...])
    inner_ref[0] = bias_sum
    grad_up = dot(turned_normed[...], inner_grad[...])
    split_halves(grad_up, stage, core, keep_ref, send_ref, (0, 0, 0))
    grad_down = dot(turned_grad[...], act_ref[...])
    split_halves(grad_down, stage, core, keep_ref, send_ref, (0, 1, 0))

    @pl.when(chunk == pl.num_programs(0) - 1)
    def _():
        gain_sum = jnp.zeros((1, total.shape[1]), jnp.float32)
        offset_sum = jnp.zeros((1, total.shape[1]), jnp.float32)
        for block in range(blocks):
            rows = slice(block * IMAGE_ROWS, (block + 1) * IMAGE_ROWS)
            unit, inverse = unit_norm(middle_ref[rows, :])
            pulled = total[rows, :]
            gain_sum = gain_sum + jnp.sum(pulled * unit, axis=0, keepdims=True)
            offset_sum = offset_sum + jnp.sum(pulled, axis=0, keepdims=True)
            out_ref[rows, :] = grad_ref[rows, :] + norm_pull(
                pulled, unit, inverse, vector_ref[2:3, :]
            )
        small_ref[0:1, :] = gain_sum
        small_ref[1:2, :] = offset_sum


def feed_back(ids, counts, grad, middle, weights, vectors, act, slope, after=()):
    layer, own, held, first_unit = weights
    rep_count, shard_count = len(held), held[0].shape[1] + 1
    part_rows, piece = held[0].shape[2:]
    tokens, width = middle.shape
    chunks = 4 * width // piece
    half = shard_count // 2
    units = chunks // half
    grad_shape = (units, 2, half, rep_count // 2, part_rows, piece)
    grad_spec = pl.BlockSpec(
        (1, 2, 1) + grad_shape[3:], lambda chunk: (chunk % units, 0, chunk // units, 0, 0, 0)
    )
    weight_values, weight_specs = weight_args(layer, own, held, first_unit, units)
    out = ordered_call(
        functools.partial(feed_back_kernel, rep_count, grad.ndim > 2),
        (ids, counts, grad, middle, vectors, act, slope, *weight_values),
        after,
        grid=(chunks,),
        in_specs=[
            pl.BlockSpec(memory_space=pltpu.SMEM),
            pl.BlockSpec(memory_space=pltpu.SMEM),
            once(grad.shape, (0,) * grad.ndim),
            once((tokens, width), (0, 0)),
            once(vectors.shape, (0, 0)),
            pl.BlockSpec((tokens, piece), lambda chunk: (0, chunk)),
            pl.BlockSpec((tokens, piece), lambda chunk: (0, chunk)),
        ]
        + weight_specs,
        out_specs=[
            pl.BlockSpec((tokens, width), lambda chunk: (0, 0)),
            pl.BlockSpec((8, width), lambda chunk: (0, 0)),
            pl.BlockSpec((1, 1, piece), lambda chunk: (chunk, 0, 0)),
            grad_spec,
            grad_spec,
        ],
        out_shape=[
            jax.ShapeDtypeStruct((tokens, width), jnp.float32),
            jax.ShapeDtypeStruct((8, width), jnp.float32),
            jax.ShapeDtypeStruct((chunks, 1, piece), jnp.float32),
            jax.ShapeDtypeStruct(grad_shape, jnp.bfloat16),
            jax.ShapeDtypeStruct(grad_shape, jnp.bfloat16),
        ],
        scratch_shapes=[
            pltpu.VMEM((tokens, width), jnp.bfloat16),
            pltpu.VMEM((tokens, width), jnp.bfloat16),
            pltpu.VMEM((tokens, piece), jnp.bfloat16),
            pltpu.VMEM((tokens, width), jnp.float32),
            pltpu.VMEM((rep_count, part_rows, piece), jnp.float32),
            pltpu.VMEM((units, shard_count, rep_count, part_rows, piece), jnp.bfloat16),
            pltpu.VMEM((width, tokens), jnp.bfloat16),
            pltpu.VMEM((width, tokens), jnp.bfloat16),
            pltpu.VMEM((piece, width), jnp.bfloat16),
        ]
        + [
            pltpu.VMEM((half.stop - half.start, piece), jnp.float32) for half in row_halves(tokens)
        ]
        + ([pltpu.VMEM((tokens, width), jnp.float32)] if grad.ndim > 2 else []),
        compiler_params=params(38 * 1024 * 1024),
        cost_estimate=cost(tokens * width * width * 32, 24e6),
        name="feed_back",
    )
    flat = (units, shard_count) + grad_shape[3:]
    return out[0], out[1], out[2], out[3].reshape(flat), out[4].reshape(flat), out[5]


def attend_back_kernel(
    shifted,
    held_count,
    final,
    ids_ref,
    grad_ref,
    x_ref,
    vector_ref,
    project_ref,
    prob_ref,
    attended_ref,
    *refs,
):
    own_ref, held, refs = refs[0], refs[1 : 1 + held_count], refs[1 + held_count :]
    out_ref, small_ref, score_ref = refs[:3]
    keep_refs, send_refs, refs = refs[3:5], refs[5:7], refs[7:]
    field, grad_field, states, grad_heads, grad_states = refs[:5]
    normed_all, project_all, attended_all, grad_all, stage, weight_ref, turned = refs[5:12]
    image = pl.program_id(0)
    core = lax.rem(ids_ref[1], 2)
    shard_count = weight_ref.shape[1]
    piece = weight_ref.shape[4]
    width = x_ref.shape[1]
    third = 3 * shard_count // 4
    head_scale = (width // HEADS) ** (-0.5)
    rows_all = pl.ds(pl.multiple_of(image * ROWS, ROWS), ROWS)

    @pl.when(image == 0)
    def _():
        fill_weights(ids_ref, own_ref, held, weight_ref)
        for shard in range(shard_count):
            turned[shard] = weight_of(weight_ref, 0, shard).T
        small_ref[...] = jnp.zeros(small_ref.shape, jnp.float32)
        score_ref[...] = jnp.zeros(score_ref.shape, jnp.float32)

    into_windows(field, x_ref, shifted)
    into_windows(grad_field, grad_ref, shifted)
    unit, inverse = unit_norm(field[:ROWS, :])
    normed_all[rows_all, :] = (unit * vector_ref[0:1, :] + vector_ref[1:2, :]).astype(
        jnp.bfloat16
    )
    field[:ROWS, :] = unit
    grad_branch = grad_field[:ROWS, :].astype(jnp.bfloat16)
    grad_all[rows_all, :] = grad_branch
    attended_all[rows_all, :] = attended_ref[...]
    small_ref[4:5, :] += jnp.sum(grad_branch.astype(jnp.float32), axis=0, keepdims=True)
    grad_heads[ROWS:SPARE, :] = jnp.zeros((SPARE - ROWS, width), jnp.float32)
    states[ROWS:SPARE, :] = jnp.zeros((SPARE - ROWS, states.shape[1]), jnp.float32)
    states[:ROWS, :] = project_ref[...].astype(jnp.float32)
    branch = jnp.zeros((ROWS, width), jnp.float32)
    for shard in range(third, shard_count):
        start = (shard - third) * piece
        branch = branch + dot(grad_branch[:, start : start + piece], turned[shard])
    grad_heads[:ROWS, :] = branch
    select = block_mask(TOKENS)
    for window in range(WINDOWS):
        rows = slice(window * WINDOW_ROWS, window * WINDOW_ROWS + SLOT)
        out_rows = slice(window * WINDOW_ROWS, (window + 1) * WINDOW_ROWS)
        for group in range(HEADS // GROUP):
            first = group * 128
            cols = slice(group * GROUP * SLOT, (group + 1) * GROUP * SLOT)
            query = states[rows, first : first + 128].astype(jnp.bfloat16)
            key = states[rows, width + first : width + first + 128].astype(jnp.bfloat16)
            value = states[rows, 2 * width + first : 2 * width + first + 128].astype(jnp.bfloat16)
            arrived = grad_heads[rows, first : first + 128].astype(jnp.bfloat16)
            spread_query = jnp.concatenate([query] * GROUP, axis=0) * select
            spread_grad = jnp.concatenate([arrived] * GROUP, axis=0) * select
            soft = prob_ref[window, :, cols]
            exact = soft.astype(jnp.float32)[:WINDOW_ROWS]
            grad_soft = dot_cols(value, spread_grad)[:WINDOW_ROWS]
            delta = jnp.sum(grad_soft * exact, axis=0, keepdims=True)
            grad_scores = exact * (grad_soft - delta)
            score_ref[:, cols] += grad_scores
            grad_raw = pad_slot(grad_scores * head_scale)
            grad_key = dot(grad_raw, spread_query)[:WINDOW_ROWS]
            grad_value = dot(soft, spread_grad)[:WINDOW_ROWS]
            grad_query = fold_heads(dot_rows(grad_raw, key))[:WINDOW_ROWS]
            grad_states[out_rows, first : first + 128] = grad_query
            grad_states[out_rows, width + first : width + first + 128] = grad_key
            grad_states[out_rows, 2 * width + first : 2 * width + first + 128] = grad_value
    grad_project = grad_states[...].astype(jnp.bfloat16)
    project_all[rows_all, :] = grad_project
    column = jnp.sum(grad_project.astype(jnp.float32), axis=0, keepdims=True)
    small_ref[2:3, :] += column[:, :width]
    small_ref[3:4, :] += column[:, 2 * width :]
    pulled = jnp.zeros((ROWS, width), jnp.float32)
    for shard in range(third):
        pulled = pulled + dot(
            grad_project[:, shard * piece : (shard + 1) * piece], turned[shard]
        )
    unit = field[:ROWS, :]
    small_ref[0:1, :] += jnp.sum(pulled * unit, axis=0, keepdims=True)
    small_ref[1:2, :] += jnp.sum(pulled, axis=0, keepdims=True)
    grad_field[:ROWS, :] = grad_field[:ROWS, :] + norm_pull(
        pulled, unit, inverse, vector_ref[0:1, :]
    )
    if final:
        from_windows(refs[12], grad_field, shifted)
        rows_to_field(out_ref, 0, refs[12], 0)
    else:
        from_windows(out_ref, grad_field, shifted)

    @pl.when(image == pl.num_programs(0) - 1)
    def _():
        turned_normed, turned_attended = normed_all[...].T, attended_all[...].T
        for shard in range(shard_count):
            if shard < third:
                grad = dot(turned_normed, project_all[:, shard * piece : (shard + 1) * piece])
            else:
                start = (shard - third) * piece
                grad = dot(turned_attended, grad_all[:, start : start + piece])
            half, index = divmod(shard, shard_count // 2)
            split_halves(grad, stage, core, keep_refs[half], send_refs[half], (0, index))


def attend_back(
    shifted, ids, grad, x_rows, weights, vectors, project, prob, attended, final_shape, after=()
):
    layer, own, held, first_unit = weights
    rep_count, shard_count = len(held), held[0].shape[1] + 1
    part_rows, piece = held[0].shape[2:]
    width = x_rows.shape[1]
    images = x_rows.shape[0] // IMAGE_ROWS
    grad_shape = (1, shard_count // 2, rep_count // 2, part_rows, piece)
    weight_values, weight_specs = weight_args(layer, own, held, first_unit, 1)
    return ordered_call(
        functools.partial(attend_back_kernel, shifted, rep_count, final_shape is not None),
        (ids, grad, x_rows, vectors, project, prob, attended, *weight_values),
        after,
        grid=(images,),
        in_specs=[
            pl.BlockSpec(memory_space=pltpu.SMEM),
            pl.BlockSpec((IMAGE_ROWS, width), lambda image: (image, 0)),
            pl.BlockSpec((IMAGE_ROWS, width), lambda image: (image, 0)),
            once(vectors.shape, (0, 0)),
            pl.BlockSpec((ROWS, 3 * width), lambda image: (image, 0)),
            pl.BlockSpec((WINDOWS, SLOT, HEADS * SLOT), lambda image: (image, 0, 0)),
            pl.BlockSpec((ROWS, width), lambda image: (image, 0)),
        ]
        + weight_specs,
        out_specs=[
            pl.BlockSpec((1,) + final_shape[1:], lambda image: (image, 0, 0, 0))
            if final_shape
            else pl.BlockSpec((IMAGE_ROWS, width), lambda image: (image, 0)),
            pl.BlockSpec((8, width), lambda image: (0, 0)),
            pl.BlockSpec((WINDOW_ROWS, HEADS * SLOT), lambda image: (0, 0)),
        ]
        + [pl.BlockSpec(grad_shape, lambda image: (0, 0, 0, 0, 0))] * 4,
        out_shape=[
            jax.ShapeDtypeStruct(final_shape, jnp.bfloat16)
            if final_shape
            else jax.ShapeDtypeStruct((images * IMAGE_ROWS, width), jnp.float32),
            jax.ShapeDtypeStruct((8, width), jnp.float32),
            jax.ShapeDtypeStruct((WINDOW_ROWS, HEADS * SLOT), jnp.float32),
        ]
        + [jax.ShapeDtypeStruct(grad_shape, jnp.bfloat16)] * 4,
        scratch_shapes=[
            pltpu.VMEM((SPARE, width), jnp.float32),
            pltpu.VMEM((SPARE, width), jnp.float32),
            pltpu.VMEM((SPARE, 3 * width), jnp.float32),
            pltpu.VMEM((SPARE, width), jnp.float32),
            pltpu.VMEM((ROWS, 3 * width), jnp.float32),
            pltpu.VMEM((images * ROWS, width), jnp.bfloat16),
            pltpu.VMEM((images * ROWS, 3 * width), jnp.bfloat16),
            pltpu.VMEM((images * ROWS, width), jnp.bfloat16),
            pltpu.VMEM((images * ROWS, width), jnp.bfloat16),
            pltpu.VMEM((rep_count, part_rows, piece), jnp.float32),
            pltpu.VMEM((1, shard_count, rep_count, part_rows, piece), jnp.bfloat16),
            pltpu.VMEM((shard_count, piece, width), jnp.bfloat16),
        ]
        + ([pltpu.VMEM((IMAGE_ROWS, width), jnp.float32)] if final_shape else []),
        compiler_params=params(34 * 1024 * 1024),
        cost_estimate=cost(images * ROWS * width * width * 32, 20e6),
        name="attend_back_shifted" if shifted else "attend_back",
    )


def relay_kernel(count, extra, ids_ref, *refs):
    arrived, outs = refs[:count], refs[count:]
    for key, ref in enumerate(arrived):
        spot = 0
        for line_ref in outs[:-1] if extra else outs:
            rows = line_ref.shape[2]
            for index in range(line_ref.shape[0]):
                if ref.shape[0] == 1:
                    line_ref[index, key] = ref[0, spot * rows : (spot + 1) * rows, :]
                else:
                    line_ref[index, key] = ref[spot]
                spot += 1
        if extra:
            outs[-1][ids_ref[0] ^ (key + 1)] = ref[0, ref.shape[1] - extra :, :]


def relay(ids, arrived, split, extra, after=(), memory=SMALL_VMEM):
    units, rows, piece = arrived[0].shape
    part_rows = (units * rows - extra) // sum(split)
    shapes = [(count, len(arrived), part_rows, piece) for count in split]
    if extra:
        shapes.append((len(arrived) + 1, extra, piece))
    return ordered_call(
        functools.partial(relay_kernel, len(arrived), extra),
        (ids, *arrived),
        after,
        [pl.BlockSpec(memory_space=pltpu.SMEM)]
        + [pl.BlockSpec(memory_space=pltpu.VMEM)] * len(arrived),
        out_shape=[jax.ShapeDtypeStruct(shape, jnp.bfloat16) for shape in shapes],
        compiler_params=params(memory),
        cost_estimate=cost(0, 1e6),
        name="relay",
    )


def parts_kernel(layers, ids_ref, *refs):
    vector_ref, weight_refs, outs = refs[0], refs[1 : 1 + 2 * layers], refs[1 + 2 * layers :]
    piece = outs[0].shape[2]
    rows = weight_refs[0].shape[1]

    def units_of(index):
        ref = weight_refs[index]
        return [
            ref[0, :, start : start + piece].astype(jnp.bfloat16)
            for start in range(0, ref.shape[2], piece)
        ]

    spot = 0
    for part in units_of(1) + units_of(0):
        outs[0][0, spot : spot + rows, :] = part
        spot += rows
    lines = []
    length = vector_ref.shape[1]
    for layer in range(layers):
        for start in range(0, length, piece):
            line = vector_ref[layer : layer + 1, start : min(start + piece, length)]
            if line.shape[1] < piece:
                spare = jnp.zeros((1, piece - line.shape[1]), jnp.float32)
                line = jnp.concatenate([line, spare], axis=1)
            lines.append(line)
    lines.append(jnp.zeros((outs[0].shape[1] - spot - len(lines), piece), jnp.float32))
    outs[0][0, spot:, :] = jnp.concatenate(lines, axis=0).astype(jnp.bfloat16)
    unit = 0
    for layer in range(1, layers):
        for part in units_of(2 * layer + 1) + units_of(2 * layer):
            outs[1][unit] = part
            unit += 1


def cut_parts(ids, attention, feedforward, vectors, extra):
    layers, rows, piece = attention.shape
    part_rows = rows // lax.axis_size("rep")
    units = 1 + feedforward.shape[2] // piece

    def spec(weight, layer):
        return pl.BlockSpec(
            (1, part_rows, weight.shape[2]), lambda step, ids: (layer, ids[1], 0)
        )

    shapes = [(1, units * part_rows + extra, piece), ((layers - 1) * units, part_rows, piece)]
    return ordered_call(
        functools.partial(parts_kernel, layers),
        (ids, vectors, *([attention, feedforward] * layers)),
        (),
        [pl.BlockSpec(vectors.shape, lambda step, ids: (0, 0))]
        + [spec(weight, layer) for layer in range(layers) for weight in (attention, feedforward)],
        prefetch=1,
        grid=(1,),
        out_specs=[pl.BlockSpec(shape, lambda step, ids: (0, 0, 0)) for shape in shapes],
        out_shape=[jax.ShapeDtypeStruct(shape, jnp.bfloat16) for shape in shapes],
        compiler_params=params(),
        cost_estimate=cost(0, 5e5),
        name="cut_parts",
    )


def xor_send(value, axis, key):
    size = lax.axis_size(axis)
    return lax.ppermute(value, axis, [(index, index ^ key) for index in range(size)])


def send_line(part, gate=None):
    held = {0: part}
    for bit in reversed(range(lax.axis_size("shard").bit_length() - 1)):
        for key in list(held):
            block = held[key]
            if gate is not None and len(held) > 1:
                block, _ = lax.optimization_barrier((block, gate))
            held[key ^ (1 << bit)] = xor_send(block, "shard", 1 << bit)
    return [held[key] for key in range(1, len(held))]


def hold(chips, after=()):
    token = ()
    if after:
        *chips, token = lax.optimization_barrier((*chips, *after))
        token = [token]
    own, _ = lax.optimization_barrier((chips[0], chips[1]))
    others = [xor_send(block, "rep", 1) for block in [own] + chips[1:]]
    return [block for pair in zip(chips, others) for block in pair], token


def core_sum_kernel(units, ids_ref, *refs):
    chip = ids_ref[1] // 2
    outs = refs[2 * len(units) :]
    first = 0
    for group, count in enumerate(units):
        keep_ref, arrived_ref = refs[2 * group : 2 * group + 2]

        @pl.when((pl.program_id(0) >= first) & (pl.program_id(0) < first + count))
        def _():
            for key, out in enumerate(outs):
                for shard in range(keep_ref.shape[1]):
                    total = keep_ref[0, shard, chip ^ key].astype(jnp.float32)
                    total = total + arrived_ref[0, shard, chip ^ key].astype(jnp.float32)
                    out[0, shard] = total.astype(jnp.bfloat16)

        first += count


def core_sum(ids, pairs, after=(), moved=1e5):
    half = lax.axis_size("shard") // 2
    pairs = [
        [value.reshape((-1, half) + value.shape[2:]) for value in pair] for pair in pairs
    ]
    _, _, chips, part_rows, piece = pairs[0][0].shape
    units = [keep.shape[0] for keep, _ in pairs]
    specs, first = [], 0
    for count in units:

        def index(unit, first=first, count=count):
            return (jnp.clip(unit - first, 0, count - 1), 0, 0, 0, 0)

        specs += [pl.BlockSpec((1, half, chips, part_rows, piece), index)] * 2
        first += count
    *sums, token = ordered_call(
        functools.partial(core_sum_kernel, units),
        (ids, *[value for pair in pairs for value in pair]),
        after,
        [pl.BlockSpec(memory_space=pltpu.SMEM)] + specs,
        grid=(sum(units),),
        out_specs=[pl.BlockSpec((1, half, part_rows, piece), lambda unit: (unit, 0, 0, 0))]
        * chips,
        out_shape=[jax.ShapeDtypeStruct((sum(units), half, part_rows, piece), jnp.bfloat16)]
        * chips,
        compiler_params=params(SMALL_VMEM),
        cost_estimate=cost(1e5, moved),
        name="core_sum",
    )
    return [part.reshape((-1, 2 * half, part_rows, piece)) for part in sums] + [token]


def plane_sum_kernel(count, rows, ids_ref, *refs):
    parts, vectors, outs = refs[:count], refs[count:-2], refs[-2:]
    for key in range(parts[0].shape[1]):
        shard = ids_ref[0] ^ key
        out = outs[key % 2]
        for unit in range(parts[0].shape[0]):
            total = parts[0][unit, shard].astype(jnp.float32)
            for part in parts[1:]:
                total = total + part[unit, shard].astype(jnp.float32)
            out[key // 2, unit, :rows, :] = total.astype(jnp.bfloat16)
        if vectors:
            total = vectors[0][shard].astype(jnp.float32) + vectors[1][shard].astype(jnp.float32)
            out[key // 2, 0, rows:, :] = total.astype(jnp.bfloat16)


def plane_sum(ids, parts, vectors=(), after=(), moved=4e6):
    units, shard_count, part_rows, piece = parts[0].shape
    extra = vectors[0].shape[1] if vectors else 0
    shape = (shard_count // 2, units, part_rows + extra, piece)
    return ordered_call(
        functools.partial(plane_sum_kernel, len(parts), part_rows),
        (ids, *parts, *vectors),
        after,
        [pl.BlockSpec(memory_space=pltpu.SMEM)]
        + [pl.BlockSpec(memory_space=pltpu.VMEM)] * (len(parts) + len(vectors)),
        out_shape=[jax.ShapeDtypeStruct(shape, jnp.bfloat16)] * 2,
        compiler_params=params(SMALL_VMEM),
        cost_estimate=cost(parts[0].size * 4, moved),
        name="plane_sum",
    )


def pair_sum_kernel(keep_ref, arrived_ref, *outs):
    for index in range(keep_ref.shape[0]):
        total = keep_ref[index].astype(jnp.float32) + arrived_ref[index].astype(jnp.float32)
        outs[index % 2][index // 2] = total.astype(jnp.bfloat16)


def pair_sum(keep, arrived, after=(), moved=4e6):
    count = keep.shape[0]
    shape = (max(count // 2, 1),) + keep.shape[1:]
    return ordered_call(
        pair_sum_kernel,
        (keep, arrived),
        after,
        [pl.BlockSpec(memory_space=pltpu.VMEM)] * 2,
        out_shape=[jax.ShapeDtypeStruct(shape, jnp.bfloat16)] * min(count, 2),
        compiler_params=params(SMALL_VMEM),
        cost_estimate=cost(keep.size, moved),
        name="pair_sum",
    )


def final_sum_kernel(*refs):
    out_ref = refs[-1]
    spot = 0
    for keep_ref, arrived_ref in (refs[0:2], refs[2:4]):
        rows = keep_ref.shape[2]
        for unit in range(keep_ref.shape[1]):
            total = keep_ref[0, unit].astype(jnp.float32) + arrived_ref[0, unit].astype(jnp.float32)
            out_ref[0, spot : spot + rows, :] = total.astype(jnp.bfloat16)
            spot += rows


def final_sum(first, second, after=()):
    rows = sum(pair[0].shape[1] * pair[0].shape[2] for pair in (first, second))
    args = (*first, *second)
    return ordered_call(
        final_sum_kernel,
        args,
        after,
        [pl.BlockSpec(memory_space=pltpu.VMEM)] * len(args),
        out_shape=jax.ShapeDtypeStruct((1, rows, args[0].shape[3]), jnp.bfloat16),
        compiler_params=params(SMALL_VMEM),
        cost_estimate=cost(1e6, 4e6),
        name="final_sum",
    )


def send_pair(value):
    return xor_send(value, "rep", 1)


def send_chips(parts):
    return [parts[0]] + [
        xor_send(parts[key], "rep", 2 * key) for key in range(1, lax.axis_size("rep") // 2)
    ]


def swap_line(away):
    stage = lax.axis_size("shard") // (2 * away.shape[0])
    return xor_send(away, "shard", stage)


def narrow_line(keep, arrived, after):
    token = after[0]
    while keep.shape[0] > 1:
        keep, away, token = pair_sum(keep, arrived, [token])
        arrived = swap_line(away)
    return keep, arrived, token


def finish_line(keep, arrived, after):
    while True:
        *sums, token = pair_sum(keep, arrived, after)
        if len(sums) == 1:
            return sums[0][0], token
        keep, away = sums
        arrived, after = swap_line(away), ()


def spread(total):
    chips = [total] + [
        xor_send(total, "rep", 2 * key) for key in range(1, lax.axis_size("rep") // 2)
    ]
    others = [send_pair(block) for block in chips]
    return [block for pair in zip(chips, others) for block in pair]


def adam_terms(weight, grad, first, second, rate, decay):
    first_new = BETA_ONE * first + (1.0 - BETA_ONE) * grad
    second_new = BETA_TWO * second + (1.0 - BETA_TWO) * grad * grad
    second_hat = second_new * (1.0 / (1.0 - BETA_TWO**STEP))
    below = second_hat * lax.rsqrt(jnp.maximum(second_hat, 1e-37)) + EPS_ADAM
    near = pl.reciprocal(below, approx=True)
    near = near * (2.0 - below * near)
    weight_new = weight * (1.0 - rate * decay) - first_new * (rate / (1.0 - BETA_ONE**STEP)) * near
    return (weight_new, first_new, second_new)


def ahead_kernel(jobs, *refs):
    count = 3 * len(jobs)
    states, outs, sems = refs[: -count - 1], refs[-count - 1 : -1], refs[-1]
    copies = []
    for job, (kind, layer, _) in enumerate(jobs):
        for index in range(3):
            copies.append(
                pltpu.make_async_copy(
                    states[3 * kind + index].at[layer],
                    outs[3 * job + index],
                    sems.at[3 * job + index],
                )
            )
    start_all(copies)
    for copy in copies:
        copy.wait()


def start_all(copies):
    for copy in copies:
        copy.start()


def load_ahead(jobs, kinds, after):
    states = [far(state) for kind in kinds for state in kind]
    *outs, token = ordered_call(
        functools.partial(ahead_kernel, jobs),
        tuple(states),
        after,
        [pl.BlockSpec(memory_space=pl.ANY)] * len(states),
        out_specs=[pl.BlockSpec(memory_space=pltpu.VMEM)] * (3 * len(jobs)),
        out_shape=[
            pltpu.VMEM(kinds[kind][0].shape[1:], jnp.float32) for kind, _, _ in jobs for _ in range(3)
        ],
        scratch_shapes=[pltpu.SemaphoreType.DMA((3 * len(jobs),))],
        compiler_params=params(SMALL_VMEM),
        cost_estimate=cost(1e5, 1e6),
        name="load_ahead",
    )
    return outs, token


def adam_kernel(count, jobs, ahead, ids_ref, *refs):
    held, refs = refs[:count], refs[count:]
    ready, refs = refs[: 3 * len(jobs) * ahead], refs[3 * len(jobs) * ahead :]
    kinds = 1 + max(kind for kind, _, _ in jobs)
    states = []
    if not ahead:
        states, refs = [refs[3 * kind : 3 * kind + 3] for kind in range(kinds)], refs[3 * kinds :]
    sems, refs = refs[-3:], refs[:-3]
    made, refs = refs[-len(jobs) :], refs[: -len(jobs)]
    loaded = [ready[3 * job : 3 * job + 3] for job in range(len(jobs))]
    if not ahead:
        loaded, refs = refs[-len(jobs) :], refs[: -len(jobs)]
    stage, refs = refs[-1], refs[:-1]
    outs = refs[-4 * kinds :]
    outs = [outs[4 * kind : 4 * kind + 4] for kind in range(kinds)]
    steps, rows = made[0].shape[1:3]
    piece = stage.shape[2]
    part_rows = rows * steps // count
    held_copies = [
        pltpu.make_async_copy(held[key].at[0], stage.at[ids_ref[1] ^ key], sems[0].at[key])
        for key in range(count)
    ]
    loads, stores = {}, {}
    for job, (kind, layer, _) in enumerate(jobs):
        for step in range(steps):
            here = pl.ds(step * rows, rows)
            loads[job, step] = [
                pltpu.make_async_copy(
                    state.at[layer, here], loaded[job].at[index, step], sems[1].at[job, index, step]
                )
                for index, state in enumerate(states[kind] if states else [])
            ]
            stores[job, step] = [
                pltpu.make_async_copy(
                    made[job].at[index, step], out.at[layer, here], sems[2].at[job, index, step]
                )
                for index, out in enumerate(outs[kind])
            ]
    for copy in held_copies + [copy for copies in loads.values() for copy in copies]:
        copy.start()
    for copy in held_copies:
        copy.wait()
    for job, (_, _, first) in enumerate(jobs):
        for step in range(steps):
            for copy in loads[job, step]:
                copy.wait()
            for part in range(rows // part_rows):
                lines = slice(part * part_rows, (part + 1) * part_rows)
                for unit in range(made[job].shape[3] // piece):
                    cols = slice(unit * piece, (unit + 1) * piece)
                    spot = first + unit * part_rows
                    grad = stage[step * (rows // part_rows) + part, spot : spot + part_rows, :]
                    grad = grad.astype(jnp.float32)
                    made[job][0, step, lines, cols] = grad
                    if ahead:
                        spots = slice(step * rows + lines.start, step * rows + lines.stop)
                        old = [ref[spots, cols] for ref in loaded[job]]
                    else:
                        old = [loaded[job][index, step, lines, cols] for index in range(3)]
                    new = adam_terms(old[0], grad, *old[1:], RATE_MATRIX, DECAY_MATRIX)
                    for index, value in enumerate(new):
                        made[job][index + 1, step, lines, cols] = value
            for copy in stores[job, step]:
                copy.start()
    for copies in stores.values():
        for copy in copies:
            copy.wait()


def adam(ids, held, jobs, kinds, prior=(), after=(), ready=()):
    held_rows, piece = held[0].shape[1:]
    steps = 4
    states = [] if ready else [far(state) for kind in kinds for state in kind]
    shapes = [kind[0].shape for kind in kinds]
    blocks = [(steps, shapes[kind][1] // steps, shapes[kind][2]) for kind, _, _ in jobs]
    start = 1 + len(held) + len(ready) + len(states)
    first_out = 4 * (len(kinds) - 1)
    anywhere = pl.BlockSpec(memory_space=pl.ANY)
    *outs, token = ordered_call(
        functools.partial(adam_kernel, len(held), jobs, int(bool(ready))),
        (ids, *held, *ready, *states, *prior),
        after,
        [pl.BlockSpec(memory_space=pltpu.SMEM)]
        + [anywhere] * len(held)
        + [pl.BlockSpec(memory_space=pltpu.VMEM)] * len(ready)
        + [anywhere] * (len(states) + len(prior)),
        out_specs=[anywhere] * (4 * len(kinds)),
        out_shape=[
            jax.ShapeDtypeStruct(shape, jnp.float32) for shape in shapes for _ in range(4)
        ],
        input_output_aliases={start + index: first_out + index for index in range(len(prior))},
        scratch_shapes=[pltpu.VMEM((len(held), held_rows, piece), jnp.bfloat16)]
        + ([] if ready else [pltpu.VMEM((3,) + block, jnp.float32) for block in blocks])
        + [pltpu.VMEM((4,) + block, jnp.float32) for block in blocks]
        + [
            pltpu.SemaphoreType.DMA((len(held),)),
            pltpu.SemaphoreType.DMA((len(jobs), 3, steps)),
            pltpu.SemaphoreType.DMA((len(jobs), 4, steps)),
        ],
        compiler_params=params(40 * 1024 * 1024 if ready else 20 * 1024 * 1024),
        cost_estimate=cost(1e6, 3e7),
        name="adam",
    )
    return [outs[4 * kind : 4 * kind + 4] for kind in range(len(kinds))], token


def vector_adam_kernel(count, rows, ids_ref, *refs):
    totals, states = refs[:count], refs[count : count + 3]
    outs, stage = refs[count + 3 : count + 7], refs[-1]
    for key, ref in enumerate(totals):
        stage[(ids_ref[1] // 2) ^ key] = ref[0, rows:, :].astype(jnp.float32)
    total = stage[0]
    for chip in range(1, count):
        total = total + stage[chip]
    layers, length = states[0].shape
    piece = total.shape[1]
    line = 0
    for layer in range(layers):
        for start in range(0, length, piece):
            here = slice(start, min(start + piece, length))
            this = slice(layer, layer + 1)
            grad = total[line : line + 1, : here.stop - here.start]
            outs[0][this, here] = grad
            new = adam_terms(*[ref[this, here] for ref in states[:1]], grad, *[
                ref[this, here] for ref in states[1:]
            ], RATE_VECTOR, 0.0)
            for out, value in zip(outs[1:], new):
                out[this, here] = value
            line += 1


def vector_adam(ids, totals, rows, weight, first, second, after=()):
    extra = totals[0].shape[1] - rows
    return ordered_call(
        functools.partial(vector_adam_kernel, len(totals), rows),
        (ids, *totals, weight, first, second),
        after,
        [pl.BlockSpec(memory_space=pltpu.SMEM)]
        + [pl.BlockSpec(memory_space=pltpu.VMEM)] * (len(totals) + 3),
        out_shape=[jax.ShapeDtypeStruct(weight.shape, jnp.float32)] * 4,
        scratch_shapes=[pltpu.VMEM((len(totals), extra, totals[0].shape[2]), jnp.float32)],
        compiler_params=params(SMALL_VMEM),
        cost_estimate=cost(weight.size * 10, weight.size * 16),
        name="vector_adam",
    )


def join_vectors(lines, layers, length):
    shard_count, _, piece = lines.shape
    used = -(-length // piece)
    lines = lines[:, : layers * used].reshape(shard_count, layers, used * piece)[:, :, :length]
    return lines.transpose(1, 0, 2).reshape(layers, shard_count * length)


def pack_kernel(length, has_prior, rel_ref, one_ref, two_ref, inner_ref, score_ref, *refs):
    prior_ref = refs[0] if has_prior else None
    out_ref, turned = refs[-2:]
    shard_count, _, piece = out_ref.shape
    spare = jnp.zeros((SLOT - WINDOW_ROWS, score_ref.shape[1]), jnp.float32)
    turned[...] = jnp.concatenate([score_ref[...], spare], axis=0).T
    entries = lax.broadcasted_iota(jnp.int32, (SLOT, 256), 1)
    table = jnp.zeros((2 * HEADS, 256), jnp.float32)
    for token in range(TOKENS):
        exact = turned[pl.ds(token, HEADS, stride=SLOT), :]
        high = exact.astype(jnp.bfloat16)
        low = (exact - high.astype(jnp.float32)).astype(jnp.bfloat16)
        same = jnp.where(rel_ref[:, token : token + 1] == entries, 1.0, 0.0).astype(jnp.bfloat16)
        table = table + dot(jnp.concatenate([high, low], axis=0), same)
    table = table[:HEADS] + table[HEADS:]
    if piece > 256:
        table = jnp.concatenate([table, jnp.zeros((HEADS, piece - 256), jnp.float32)], axis=1)
    rows = []
    for ref, row in (
        (one_ref, 0),
        (one_ref, 1),
        (two_ref, 0),
        (two_ref, 1),
        (one_ref, 2),
        (one_ref, 3),
        (one_ref, 4),
        (two_ref, 2),
    ):
        for start in range(0, one_ref.shape[1], piece):
            rows.append(ref[row : row + 1, start : start + piece])
    rows += [inner_ref[chunk] for chunk in range(inner_ref.shape[0])]
    lanes = lax.broadcasted_iota(jnp.int32, (1, piece), 1)
    entry_rows = [jnp.zeros((1, piece), jnp.float32)] * (-(-HEADS * TABLE // piece) + 1)
    for head in range(HEADS):
        row, lane = divmod(head * TABLE, piece)
        moved = table[head : head + 1]
        if lane:
            moved = pltpu.roll(moved, lane, 1)
        entry_rows[row] = entry_rows[row] + jnp.where(lanes >= lane, moved, 0.0)
        if lane + TABLE > piece:
            entry_rows[row + 1] = entry_rows[row + 1] + jnp.where(lanes < lane, moved, 0.0)
    used = -(-length // piece)
    rows += entry_rows
    rows += [jnp.zeros((1, piece), jnp.float32)] * (-len(rows) % 8 + 8)
    flat = jnp.concatenate(rows, axis=0)
    lanes = lax.broadcasted_iota(jnp.int32, (used, piece), 1)
    for shard in range(shard_count):
        row, lane = divmod(shard * length, piece)
        moved = pltpu.roll(flat, piece - lane, 1) if lane else flat
        lines = jnp.where(lanes < piece - lane, moved[row : row + used], moved[row + 1 : row + 1 + used])
        parts = [lines]
        if has_prior:
            parts.append(prior_ref[shard, :used, :])
        count = len(parts) * used
        parts.append(jnp.zeros((out_ref.shape[1] - count, piece), jnp.float32))
        out_ref[shard] = jnp.concatenate(parts, axis=0).astype(out_ref.dtype)


def pack(rel_slots, small_one, small_two, inner, scores, length, extra, prior=None, after=()):
    shard_count = lax.axis_size("shard")
    prior = () if prior is None else (prior,)
    args = (rel_slots, small_one, small_two, inner, scores) + prior
    return ordered_call(
        functools.partial(pack_kernel, length, len(prior)),
        args,
        after,
        [pl.BlockSpec(memory_space=pltpu.VMEM)] * len(args),
        out_shape=jax.ShapeDtypeStruct(
            (shard_count, extra if prior else 8, inner.shape[2]),
            jnp.bfloat16 if prior else jnp.float32,
        ),
        scratch_shapes=[pltpu.VMEM((HEADS * SLOT, SLOT), jnp.float32)],
        compiler_params=params(SMALL_VMEM),
        cost_estimate=cost(1e6, 1e6),
        name="pack",
    )


def image_rows(field):
    images, width = field.shape[0], field.shape[-1]
    flat = field.reshape(images, IMAGE, width)
    flat = jnp.pad(flat, ((0, 0), (0, IMAGE_ROWS - IMAGE), (0, 0)))
    return flat.reshape(images * IMAGE_ROWS, width)


def pair_mask(region_ids):
    images = region_ids.shape[0]
    cells = region_ids.reshape(images, ACROSS, WINDOW, ACROSS, WINDOW).transpose(0, 1, 3, 2, 4)
    cells = cells.reshape(images * WINDOWS, TOKENS)
    keys = jnp.pad(cells, ((0, 0), (0, WINDOW_ROWS - TOKENS)))
    queries = jnp.pad(cells, ((0, 0), (0, SLOT - TOKENS)))
    queries = jnp.concatenate([queries] * (128 // SLOT), axis=1)
    same = keys[:, :, None] == queries[:, None, :]
    return jnp.where(same, jnp.float32(0.0), jnp.float32(MASK_FILL))


def pair_slots(rel_index):
    spare = SLOT - TOKENS
    return jnp.pad(rel_index.T, ((0, spare), (0, spare)), constant_values=-1)


def pair_onehot(rel_slots):
    turned = rel_slots[:WINDOW_ROWS].reshape(1, -1)
    return (jnp.arange(TABLE)[:, None] == turned).astype(jnp.bfloat16)


def spread_table(table, onehot):
    bias = dot(table, onehot).reshape(HEADS, WINDOW_ROWS, SLOT).transpose(1, 0, 2)
    bias = bias.reshape(WINDOW_ROWS, HEADS * SLOT)
    real = jnp.arange(WINDOW_ROWS)[:, None] < TOKENS
    return jnp.where(real, bias, jnp.float32(PAD_FILL))


def shards(
    images,
    region_ids,
    image_counts,
    rel_index,
    cotangent,
    attention_weight,
    feedforward_weight,
    vector_params,
    attention_first,
    feedforward_first,
    vector_first,
    attention_second,
    feedforward_second,
    vector_second,
):
    shard_id, rep_id = lax.axis_index("shard"), lax.axis_index("rep")
    ids = jnp.stack([shard_id, rep_id]).astype(jnp.int32)
    width, piece = attention_weight.shape[1:]
    layers, length = vector_params.shape
    extra = -(-layers * -(-length // piece) // 16) * 16
    attention, feedforward = attention_weight, feedforward_weight

    rel_slots = pair_slots(rel_index)
    onehot = pair_onehot(rel_slots)
    mask = pair_mask(region_ids)
    no_mask = jnp.zeros((1, 8, 128), jnp.float32)
    residual = image_rows(images.astype(jnp.float32))

    feed_units = feedforward.shape[2] // piece
    part_zero, part_one, _ = cut_parts(ids, attention, feedforward, vector_params, extra)
    arrived_zero = send_line(part_zero)
    part_one, _ = lax.optimization_barrier((part_one, arrived_zero[1]))
    arrived_one = send_line(part_one, arrived_zero[-1])
    line_zero, lines, token = relay(ids, arrived_zero, [feed_units + 1], extra)
    lines = lax.dynamic_update_index_in_dim(lines, part_zero[0, -extra:], shard_id, 0)
    vectors_full = join_vectors(lines, layers, length)
    bulks = [flat[: 12 * width].astype(jnp.float32).reshape(12, width) for flat in vectors_full]
    inners = [bulk[8:].reshape(-1, 1, piece) for bulk in bulks]
    biases = [
        spread_table(flat[12 * width :].reshape(HEADS, -1), onehot) for flat in vectors_full
    ]
    chip_count = lax.axis_size("rep") // 2
    chips_zero = send_chips([line_zero] * chip_count)
    line_one, token = relay(ids, arrived_one, [feed_units + 1], 0)
    held_zero, token = hold(chips_zero, [token])
    chips_one = send_chips([line_one] * chip_count)
    attend_weights = [(0, attention, held_zero, feed_units)]
    feed_weights = [(0, feedforward, held_zero, 0)]
    first = attend(
        False,
        ids,
        residual,
        attend_weights[0],
        bulks[0],
        biases[0],
        no_mask,
        [*token, mask, biases[1], *bulks, *inners],
    )
    second = feed(ids, first[0], feed_weights[0], bulks[0], inners[0])
    held_one, token = hold(chips_one, [second[3]])
    attend_weights.append((1, attention, held_one, feed_units))
    feed_weights.append((1, feedforward, held_one, 0))
    stored = [(residual, bulks[0]) + tuple(first[:4]) + tuple(second[1:3])]
    residual = second[0]
    first = attend(
        True,
        ids,
        residual,
        attend_weights[1],
        bulks[1],
        biases[1],
        mask,
        token,
    )
    second = feed(ids, first[0], feed_weights[1], bulks[1], inners[1], images.shape)
    stored.append((residual, bulks[1]) + tuple(first[:4]) + tuple(second[1:3]))
    block_out = second[0]

    def back_feed(layer, grad, after):
        _, bulk, middle, _, _, _, act, slope = stored[layer]
        layer_id, own, held, first_unit = feed_weights[layer]
        weights = (layer_id, own, [far(block) for block in held], first_unit)
        if layer == LAYERS - 1:
            grad = far(grad)
        return feed_back(
            ids, image_counts, grad, far(middle), weights, bulk, far(act), far(slope), after
        )

    def back_attend(layer, grad, after):
        residual, bulk, _, project, prob, attended, _, _ = stored[layer]
        layer_id, own, held, first_unit = attend_weights[layer]
        weights = (layer_id, own, [far(block) for block in held], first_unit)
        return attend_back(
            layer % 2 == 1,
            ids,
            grad,
            far(residual),
            weights,
            bulk,
            far(project),
            far(prob),
            far(attended),
            images.shape if layer == 0 else None,
            after,
        )

    grad_state, small_f1, inner_f1, keep_f1, send_f1, _ = back_feed(1, cotangent, ())
    came_f1 = send_pair(send_f1)
    grad_state, small_a1, scores_a1, *halves, token = back_attend(1, grad_state, ())
    pairs_a1 = [(halves[index], send_pair(halves[2 + index])) for index in range(2)]
    *chips, token = core_sum(ids, [(keep_f1, came_f1)], [token])
    chips_f1 = send_chips(chips)
    grad_state, small_f0, inner_f0, keep_f0, send_f0, token = back_feed(0, grad_state, [token])
    keep_f1, away, token = plane_sum(ids, chips_f1, (), [token], 60e6)
    came_f0 = send_pair(lax.optimization_barrier((send_f0, token))[0])
    came_f1 = swap_line(away)
    vector_one, token = pack(
        rel_slots, small_a1, small_f1, inner_f1, scores_a1, length, extra, None, [token]
    )
    *chips, token = core_sum(ids, pairs_a1 + [(keep_f0, came_f0)], [token], 4e6)
    chips_af = send_chips(chips)
    input_grad, small_a0, scores_a0, *halves, token = back_attend(0, grad_state, [token])
    keep_f1, away, token = pair_sum(keep_f1, came_f1, [token], 60e6)
    came_f1 = swap_line(away)
    *send_a0, _ = lax.optimization_barrier((*halves[2:], token))
    pairs_a0 = [(halves[index], send_pair(send_a0[index])) for index in range(2)]
    *chips, token = core_sum(ids, pairs_a0, [token])
    chips_a0 = send_chips(chips)
    vectors, token = pack(
        rel_slots, small_a0, small_f0, inner_f0, scores_a0, length, extra, vector_one, [token]
    )
    came_vectors = send_pair(vectors)
    attention_states = (attention, attention_first, attention_second)
    feedforward_states = (feedforward, feedforward_first, feedforward_second)
    part_rows = attention.shape[1] // lax.axis_size("rep")
    jobs = ((0, 1, 0), (1, 0, part_rows), (0, 0, part_rows * (1 + feed_units)))
    ready, token = load_ahead(jobs, (attention_states, feedforward_states), [token])
    total_f1, token = finish_line(keep_f1, came_f1, [token])
    keep_af, away, token = plane_sum(ids, chips_af, (), [token], 1e5)
    came_af = swap_line(away)
    total_f1, token = lax.optimization_barrier((total_f1, token))
    chips_f1 = send_chips([total_f1.reshape(1, -1, piece)] * (lax.axis_size("rep") // 2))
    keep_af, came_af, token = narrow_line(keep_af, came_af, [token])
    keep_a0, away, token = plane_sum(ids, chips_a0, (vectors, came_vectors), [token])
    came_a0 = swap_line(away)
    keep_a0, came_a0, token = narrow_line(keep_a0, came_a0, [token])
    held_f1, (token,) = hold(chips_f1, [token])
    total, token = final_sum((keep_af, came_af), (keep_a0, came_a0), [token])
    chips = send_chips([total] * (lax.axis_size("rep") // 2))
    (feedforward_out,), token = adam(ids, held_f1, ((0, 1, 0),), (feedforward_states,), (), [token])
    held, (token,) = hold(chips, [token])
    *vector_out, token = vector_adam(
        ids,
        held[::2],
        total.shape[1] - extra,
        vector_params,
        vector_first,
        vector_second,
        [token],
    )
    (attention_out, feedforward_out), _ = adam(
        ids,
        held,
        jobs,
        (attention_states, feedforward_states),
        feedforward_out,
        [token],
        ready,
    )
    vector_grad, vector_new, first_vector, second_vector = vector_out
    attention_grad, attention_new, first_attention, second_attention = attention_out
    feedforward_grad, feedforward_new, first_feedforward, second_feedforward = feedforward_out
    return (
        block_out,
        input_grad,
        attention_grad,
        feedforward_grad,
        vector_grad,
        attention_new,
        feedforward_new,
        vector_new,
        first_attention,
        first_feedforward,
        first_vector,
        second_attention,
        second_feedforward,
        second_vector,
    )


def solution(mesh):
    rows = P(("shard", "rep"), None, None, None)
    matrix = P(None, None, "shard")
    vector = P(None, "shard")
    states = (matrix, matrix, vector)
    return jax.shard_map(
        shards,
        mesh=mesh,
        in_specs=(rows, P(("shard", "rep"), None, None), P(("shard", "rep")), P(), rows)
        + states * 3,
        out_specs=(rows, rows) + states * 4,
        check_vma=False,
    )
```

```python
import functools

import jax
import jax.numpy as jnp
from jax import lax
from jax.experimental import pallas as pl
from jax.experimental.pallas import tpu as pltpu
from jax.sharding import PartitionSpec as P

HEADS = 16
WINDOW = 7
SIDE = 14
SHIFT = 3
TABLE = 169
LAYERS = 2
STEP = 10

EPS_NORM = 1e-05
EPS_ADAM = 1e-08
BETA_ONE = 0.9
BETA_TWO = 0.999
RATE_MATRIX = 0.1
RATE_VECTOR = 1.0
DECAY_MATRIX = 0.05
MASK_FILL = -100.0
PAD_FILL = -1e30
HIGH = lax.Precision.HIGHEST

ACROSS = SIDE // WINDOW
WINDOWS = ACROSS * ACROSS
TOKENS = WINDOW * WINDOW
IMAGE = SIDE * SIDE
IMAGE_ROWS = 208
WINDOW_ROWS = 56
SLOT = 64
ROWS = WINDOWS * WINDOW_ROWS
SPARE = ROWS + 8
GROUP = 4
VMEM_BYTES = 56 * 1024 * 1024
SMALL_VMEM = 14 * 1024 * 1024


def params(bytes_limit=VMEM_BYTES):
    return pltpu.CompilerParams(vmem_limit_bytes=bytes_limit)


def cost(flops, moved, exps=0):
    return pl.CostEstimate(flops=int(flops), bytes_accessed=int(moved), transcendentals=int(exps))


def ordered_call(body, args, after, in_specs, prefetch=0, grid=None, **rest):
    count, extra = len(args), len(after)
    shapes = rest.pop("out_shape")
    shapes = list(shapes) if isinstance(shapes, (list, tuple)) else [shapes]
    results = len(shapes)

    def run(*refs):
        ins, refs = refs[:count], refs[count + extra :]
        outs, token, scratch = refs[:results], refs[results], refs[results + 1 :]
        token[...] = jnp.zeros(token.shape, token.dtype)
        return body(*ins, *outs, *scratch)

    in_specs = list(in_specs) + [pl.BlockSpec(memory_space=pl.ANY)] * extra
    out_specs = rest.pop("out_specs", [pl.BlockSpec(memory_space=pltpu.VMEM)] * results)
    out_specs = list(out_specs) if isinstance(out_specs, (list, tuple)) else [out_specs]
    if grid is None:
        out_specs.append(pl.BlockSpec(memory_space=pltpu.VMEM))
    else:
        out_specs.append(pl.BlockSpec((8, 128), lambda *_: (0, 0)))
    shapes.append(jax.ShapeDtypeStruct((8, 128), jnp.float32))
    if prefetch:
        rest["grid_spec"] = pltpu.PrefetchScalarGridSpec(
            num_scalar_prefetch=prefetch,
            grid=grid,
            in_specs=in_specs,
            out_specs=out_specs,
            scratch_shapes=rest.pop("scratch_shapes", ()),
        )
    else:
        rest.update(in_specs=in_specs, out_specs=out_specs)
        if grid is not None:
            rest["grid"] = grid
    return pl.pallas_call(run, out_shape=shapes, **rest)(*args, *after)


def far(value):
    return pltpu.with_memory_space_constraint(value, pltpu.HBM)


def dot(left, right):
    return jnp.dot(left, right, preferred_element_type=jnp.float32)


def dot_cols(left, right):
    return lax.dot_general(
        left, right, (((1,), (1,)), ((), ())), preferred_element_type=jnp.float32
    )


def dot_rows(left, right):
    return lax.dot_general(
        left, right, (((0,), (0,)), ((), ())), preferred_element_type=jnp.float32
    )


def segments(shifted):
    move = SHIFT if shifted else 0
    found = []
    for down in range(ACROSS):
        for right in range(ACROSS):
            base = (down * ACROSS + right) * WINDOW_ROWS
            for line in range(WINDOW):
                row = (down * WINDOW + line + move) % SIDE
                col = (right * WINDOW + move) % SIDE
                first = min(WINDOW, SIDE - col)
                spot = base + line * WINDOW
                found.append((spot, row * SIDE + col, first))
                if first < WINDOW:
                    found.append((spot + first, row * SIDE, WINDOW - first))
    return found


def into_windows(window_ref, image_ref, shifted):
    for window in range(WINDOWS):
        start = window * WINDOW_ROWS + TOKENS
        stop = (window + 1) * WINDOW_ROWS
        window_ref[start:stop, :] = jnp.zeros((stop - start, window_ref.shape[1]), jnp.float32)
    for spot, source, count in segments(shifted):
        window_ref[spot : spot + count, :] = image_ref[source : source + count, :]


def from_windows(image_ref, window_ref, shifted):
    image_ref[IMAGE:IMAGE_ROWS, :] = jnp.zeros(
        (IMAGE_ROWS - IMAGE, image_ref.shape[1]), jnp.float32
    )
    for spot, source, count in segments(shifted):
        image_ref[source : source + count, :] = window_ref[spot : spot + count, :]


def rows_to_field(field_ref, image, rows_ref, start):
    for line in range(SIDE):
        here = slice(start + line * SIDE, start + (line + 1) * SIDE)
        field_ref[image, line] = rows_ref[here, :].astype(jnp.bfloat16)


def field_to_rows(rows_ref, start, field_ref, image, factor):
    for line in range(SIDE):
        here = slice(start + line * SIDE, start + (line + 1) * SIDE)
        rows_ref[here, :] = field_ref[image, line].astype(jnp.float32) * factor
    rows_ref[start + IMAGE : start + IMAGE_ROWS, :] = jnp.zeros(
        (IMAGE_ROWS - IMAGE, rows_ref.shape[1]), jnp.float32
    )


def unit_norm(values):
    width = values.shape[-1]
    centered = values - jnp.sum(values, axis=-1, keepdims=True) * (1.0 / width)
    variance = jnp.sum(centered * centered, axis=-1, keepdims=True) * (1.0 / width)
    inverse = lax.rsqrt(variance + EPS_NORM)
    return centered * inverse, inverse


def normal_parts(points):
    below = 0.5 + 0.5 * lax.erf(points * (0.5**0.5))
    return below, jnp.exp(points * points * -0.5) * 0.3989422804014327


def norm_pull(grad, unit, inverse, gain):
    width = grad.shape[-1]
    scaled = grad * gain
    mean_one = jnp.sum(scaled, axis=-1, keepdims=True) * (1.0 / width)
    mean_two = jnp.sum(scaled * unit, axis=-1, keepdims=True) * (1.0 / width)
    return inverse * (scaled - mean_one - unit * mean_two)


def block_mask(token_limit):
    rows = lax.broadcasted_iota(jnp.int32, (GROUP * SLOT, GROUP * 32), 0)
    cols = lax.broadcasted_iota(jnp.int32, (GROUP * SLOT, GROUP * 32), 1)
    keep = ((rows // SLOT) == (cols // 32)) & ((rows % SLOT) < token_limit)
    return jnp.where(keep, 1.0, 0.0).astype(jnp.bfloat16)


def fold_heads(crossed):
    lanes = lax.broadcasted_iota(jnp.int32, (SLOT, GROUP * 32), 1) // 32
    total = jnp.where(lanes == 0, crossed[:SLOT], 0.0)
    for head in range(1, GROUP):
        part = crossed[head * SLOT : (head + 1) * SLOT]
        total = jnp.where(lanes == head, part, total)
    return total


def pad_slot(values):
    spare = jnp.zeros((SLOT - WINDOW_ROWS, values.shape[1]), jnp.float32)
    return jnp.concatenate([values, spare], axis=0).astype(jnp.bfloat16)


def fill_weights(ids_ref, own_ref, held, weight_ref):
    units, _, rep_count, part_rows, piece = weight_ref.shape
    for unit in range(units):
        for rep in range(rep_count):
            rows = own_ref[
                0, rep * part_rows : (rep + 1) * part_rows, unit * piece : (unit + 1) * piece
            ]
            weight_ref[unit, ids_ref[0], rep] = rows.astype(jnp.bfloat16)
        for key, ref in enumerate(held):
            for line in range(ref.shape[1]):
                weight_ref[unit, ids_ref[0] ^ (line + 1), ids_ref[1] ^ key] = ref[unit, line]


def weight_of(weight_ref, unit, shard):
    pieces = weight_ref[unit, shard]
    return pieces.reshape(pieces.shape[0] * pieces.shape[1], pieces.shape[2])


def once(shape, index):
    return pl.BlockSpec(shape, lambda *_: index, pipeline_mode=pl.Buffered(1))


def weight_args(layer, own, held, first_unit, units):
    specs = [once((1,) + own.shape[1:], (layer, 0, 0))]
    specs += [once((units,) + held[0].shape[1:], (first_unit // units, 0, 0, 0))] * len(held)
    return (far(own), *held), specs


def attend_kernel(shifted, held_count, ids_ref, x_ref, vector_ref, bias_ref, mask_ref, *refs):
    own_ref, held, refs = refs[0], refs[1 : 1 + held_count], refs[1 + held_count :]
    middle_ref, project_ref, prob_ref, attended_ref, field, states, heads_out, weight_ref = refs
    shard_count = weight_ref.shape[1]
    piece = weight_ref.shape[4]
    width = x_ref.shape[1]

    @pl.when(pl.program_id(0) == 0)
    def _():
        fill_weights(ids_ref, own_ref, held, weight_ref)

    third = 3 * shard_count // 4
    head_scale = (width // HEADS) ** (-0.5)
    into_windows(field, x_ref, shifted)
    states[ROWS:SPARE, :] = jnp.zeros((SPARE - ROWS, states.shape[1]), jnp.float32)
    unit, _ = unit_norm(field[:ROWS, :])
    normed = (unit * vector_ref[0:1, :] + vector_ref[1:2, :]).astype(jnp.bfloat16)
    for shard in range(third):
        part = dot(normed, weight_of(weight_ref, 0, shard))
        kind, start = divmod(shard * piece, width)
        if kind == 0:
            part = part + vector_ref[4:5, start : start + piece]
        if kind == 2:
            part = part + vector_ref[5:6, start : start + piece]
        states[:ROWS, shard * piece : (shard + 1) * piece] = part
        project_ref[:, shard * piece : (shard + 1) * piece] = part.astype(jnp.bfloat16)
    select = block_mask(SLOT)
    for window in range(WINDOWS):
        rows = slice(window * WINDOW_ROWS, window * WINDOW_ROWS + SLOT)
        if shifted:
            mask = mask_ref[window]
            mask = jnp.concatenate([mask] * (GROUP * SLOT // mask.shape[1]), axis=1)
        for group in range(HEADS // GROUP):
            lanes = slice(group * 128, (group + 1) * 128)
            query = states[rows, group * 128 : group * 128 + 128].astype(jnp.bfloat16)
            key = states[rows, width + group * 128 : width + group * 128 + 128]
            value = states[rows, 2 * width + group * 128 : 2 * width + group * 128 + 128]
            spread = jnp.concatenate([query] * GROUP, axis=0) * select
            cols = slice(group * GROUP * SLOT, (group + 1) * GROUP * SLOT)
            raw = dot_cols(key.astype(jnp.bfloat16), spread)[:WINDOW_ROWS]
            scores = raw * head_scale + bias_ref[:, cols]
            if shifted:
                scores = scores + mask
            top = jnp.max(scores, axis=0, keepdims=True)
            powers = jnp.exp(scores - top)
            total = jnp.sum(powers, axis=0, keepdims=True)
            soft = pad_slot(powers * (1.0 / total))
            prob_ref[window, :, cols] = soft
            crossed = dot_rows(soft, value.astype(jnp.bfloat16))
            heads_out[window * WINDOW_ROWS : (window + 1) * WINDOW_ROWS, lanes] = fold_heads(
                crossed
            )[:WINDOW_ROWS]
    attended = heads_out[...].astype(jnp.bfloat16)
    attended_ref[...] = attended
    for shard in range(third, shard_count):
        start = (shard - third) * piece
        branch = dot(attended, weight_of(weight_ref, 0, shard))
        branch = branch + vector_ref[6:7, start : start + piece]
        field[:ROWS, start : start + piece] = field[:ROWS, start : start + piece] + branch
    from_windows(middle_ref, field, shifted)


def attend(shifted, ids, x_rows, weights, vectors, bias, mask, after=()):
    layer, own, held, first_unit = weights
    rep_count, shard_count = len(held), held[0].shape[1] + 1
    part_rows, piece = held[0].shape[2:]
    width = x_rows.shape[1]
    images = x_rows.shape[0] // IMAGE_ROWS
    mask_spec = (
        pl.BlockSpec((WINDOWS,) + mask.shape[1:], lambda image: (image, 0, 0))
        if shifted
        else pl.BlockSpec(mask.shape, lambda image: (0, 0, 0))
    )
    weight_values, weight_specs = weight_args(layer, own, held, first_unit, 1)
    return ordered_call(
        functools.partial(attend_kernel, shifted, rep_count),
        (ids, x_rows, vectors, bias, mask, *weight_values),
        after,
        grid=(images,),
        in_specs=[
            pl.BlockSpec(memory_space=pltpu.SMEM),
            pl.BlockSpec((IMAGE_ROWS, width), lambda image: (image, 0)),
            once(vectors.shape, (0, 0)),
            once(bias.shape, (0, 0)),
            mask_spec,
        ]
        + weight_specs,
        out_specs=[
            pl.BlockSpec((IMAGE_ROWS, width), lambda image: (image, 0)),
            pl.BlockSpec((ROWS, 3 * width), lambda image: (image, 0)),
            pl.BlockSpec((WINDOWS, SLOT, HEADS * SLOT), lambda image: (image, 0, 0)),
            pl.BlockSpec((ROWS, width), lambda image: (image, 0)),
        ],
        out_shape=[
            jax.ShapeDtypeStruct((images * IMAGE_ROWS, width), jnp.float32),
            pltpu.HBM((images * ROWS, 3 * width), jnp.bfloat16),
            pltpu.HBM((images * WINDOWS, SLOT, HEADS * SLOT), jnp.bfloat16),
            pltpu.HBM((images * ROWS, width), jnp.bfloat16),
        ],
        scratch_shapes=[
            pltpu.VMEM((SPARE, width), jnp.float32),
            pltpu.VMEM((SPARE, 3 * width), jnp.float32),
            pltpu.VMEM((ROWS, width), jnp.float32),
            pltpu.VMEM((1, shard_count, rep_count, part_rows, piece), jnp.bfloat16),
        ],
        compiler_params=params(18 * 1024 * 1024),
        cost_estimate=cost(images * ROWS * width * width * 16, 16e6, images * ROWS * HEADS * SLOT),
        name="attend_shifted" if shifted else "attend",
    )


def row_halves(rows):
    middle = -(-rows // 32) * 16
    return [slice(0, middle), slice(middle, rows)]


def feed_kernel(held_count, final, ids_ref, middle_ref, vector_ref, inner_ref, *refs):
    own_ref, held, refs = refs[0], refs[1 : 1 + held_count], refs[1 + held_count :]
    out_ref, act_ref, slope_ref, normed, work_one, work_two, weight_ref, turned = refs[:8]
    next_ref = refs[8] if final else out_ref
    chunk = pl.program_id(0)
    blocks = middle_ref.shape[0] // IMAGE_ROWS
    units, shard_count = weight_ref.shape[:2]

    @pl.when(chunk == 0)
    def _():
        fill_weights(ids_ref, own_ref, held, weight_ref)
        for block in range(blocks):
            rows = slice(block * IMAGE_ROWS, (block + 1) * IMAGE_ROWS)
            middle = middle_ref[rows, :]
            unit, _ = unit_norm(middle)
            normed[rows, :] = (unit * vector_ref[2:3, :] + vector_ref[3:4, :]).astype(
                jnp.bfloat16
            )
            next_ref[rows, :] = middle + vector_ref[7:8, :]

    up = weight_of(weight_ref, chunk % units, chunk // units)
    down = weight_of(weight_ref, chunk % units, shard_count // 2 + chunk // units)
    turned[...] = down.T
    offset = inner_ref[0]
    halves = row_halves(blocks * IMAGE_ROWS)
    for half, work in zip(halves, (work_one, work_two)):
        work[...] = dot(normed[half, :], up)
    step = 16
    for half, work in zip(halves, (work_one, work_two)):
        for start in range(half.start, half.stop, step):
            here = slice(start, start + step)
            points = work[start - half.start : start - half.start + step, :] + offset
            below, bell = normal_parts(points)
            act_ref[here, :] = (points * below).astype(jnp.bfloat16)
            slope_ref[here, :] = (below + points * bell).astype(jnp.bfloat16)
        next_ref[half, :] += dot(act_ref[half, :], turned[...])

    if final:

        @pl.when(chunk == pl.num_programs(0) - 1)
        def _():
            for image in range(blocks):
                rows_to_field(out_ref, image, next_ref, image * IMAGE_ROWS)


def feed(ids, middle, weights, vectors, inner, final_shape=None, after=()):
    layer, own, held, first_unit = weights
    rep_count, shard_count = len(held), held[0].shape[1] + 1
    part_rows, piece = held[0].shape[2:]
    tokens, width = middle.shape
    chunks = 4 * width // piece
    units = 2 * chunks // shard_count
    weight_values, weight_specs = weight_args(layer, own, held, first_unit, units)
    return ordered_call(
        functools.partial(feed_kernel, rep_count, final_shape is not None),
        (ids, middle, vectors, inner.reshape(chunks, 1, piece), *weight_values),
        after,
        grid=(chunks,),
        in_specs=[
            pl.BlockSpec(memory_space=pltpu.SMEM),
            once((tokens, width), (0, 0)),
            once(vectors.shape, (0, 0)),
            pl.BlockSpec((1, 1, piece), lambda chunk: (chunk, 0, 0)),
        ]
        + weight_specs,
        out_specs=[
            once(final_shape, (0, 0, 0, 0)) if final_shape else once((tokens, width), (0, 0)),
            pl.BlockSpec((tokens, piece), lambda chunk: (0, chunk)),
            pl.BlockSpec((tokens, piece), lambda chunk: (0, chunk)),
        ],
        out_shape=[
            jax.ShapeDtypeStruct(final_shape, jnp.bfloat16)
            if final_shape
            else jax.ShapeDtypeStruct((tokens, width), jnp.float32),
            pltpu.HBM((tokens, chunks * piece), jnp.bfloat16),
            pltpu.HBM((tokens, chunks * piece), jnp.bfloat16),
        ],
        scratch_shapes=[
            pltpu.VMEM((tokens, width), jnp.bfloat16),
        ]
        + [
            pltpu.VMEM((half.stop - half.start, piece), jnp.float32) for half in row_halves(tokens)
        ]
        + [
            pltpu.VMEM((units, shard_count, rep_count, part_rows, piece), jnp.bfloat16),
            pltpu.VMEM((piece, width), jnp.bfloat16),
        ]
        + ([pltpu.VMEM((tokens, width), jnp.float32)] if final_shape else []),
        compiler_params=params(30 * 1024 * 1024),
        cost_estimate=cost(tokens * width * width * 16, 16e6, tokens * 8 * width),
        name="feed",
    )


def split_halves(values, stage, core, keep_ref, send_ref, lead):
    stage[...] = values.reshape(stage.shape)
    for chip in range(stage.shape[0] // 2):
        keep_ref[lead + (chip,)] = stage[2 * chip + core].astype(jnp.bfloat16)
        send_ref[lead + (chip,)] = stage[2 * chip + 1 - core].astype(jnp.bfloat16)


def feed_back_kernel(
    held_count, raw, ids_ref, count_ref, grad_ref, middle_ref, vector_ref, act_ref, slope_ref, *refs
):
    own_ref, held, refs = refs[0], refs[1 : 1 + held_count], refs[1 + held_count :]
    out_ref, small_ref, inner_ref, keep_ref, send_ref = refs[:5]
    normed, low_grad, inner_grad, total, stage, weight_ref = refs[5:11]
    turned_normed, turned_grad, turned, work_one, work_two = refs[11:16]
    field_ref, grad_ref = grad_ref, refs[16] if raw else grad_ref
    chunk = pl.program_id(0)
    core = lax.rem(ids_ref[1], 2)
    blocks = middle_ref.shape[0] // IMAGE_ROWS
    units, shard_count = weight_ref.shape[:2]

    @pl.when(chunk == 0)
    def _():
        fill_weights(ids_ref, own_ref, held, weight_ref)
        if raw:
            for image in range(blocks):
                live = jnp.where(image < count_ref[0], 1.0, 0.0)
                field_to_rows(grad_ref, image * IMAGE_ROWS, field_ref, image, live)
        bias_sum = jnp.zeros((1, low_grad.shape[1]), jnp.float32)
        for block in range(blocks):
            rows = slice(block * IMAGE_ROWS, (block + 1) * IMAGE_ROWS)
            unit, _ = unit_norm(middle_ref[rows, :])
            normed[rows, :] = (unit * vector_ref[2:3, :] + vector_ref[3:4, :]).astype(
                jnp.bfloat16
            )
            rounded = grad_ref[rows, :].astype(jnp.bfloat16)
            low_grad[rows, :] = rounded
            bias_sum = bias_sum + jnp.sum(rounded.astype(jnp.float32), axis=0, keepdims=True)
            total[rows, :] = jnp.zeros((IMAGE_ROWS, total.shape[1]), jnp.float32)
        small_ref[2:3, :] = bias_sum
        turned_normed[...] = normed[...].T
        turned_grad[...] = low_grad[...].T

    up = weight_of(weight_ref, chunk % units, chunk // units)
    down = weight_of(weight_ref, chunk % units, shard_count // 2 + chunk // units)
    turned[...] = up.T
    bias_sum = jnp.zeros((1, up.shape[1]), jnp.float32)
    halves = row_halves(blocks * IMAGE_ROWS)
    for half, work in zip(halves, (work_one, work_two)):
        work[...] = dot(low_grad[half, :], down)
    step = 16
    for half, work in zip(halves, (work_one, work_two)):
        for start in range(half.start, half.stop, step):
            here = slice(start, start + step)
            slope = slope_ref[here, :].astype(jnp.float32)
            grad_act = work[start - half.start : start - half.start + step, :]
            grad_pre = (grad_act * slope).astype(jnp.bfloat16)
            inner_grad[here, :] = grad_pre
            bias_sum = bias_sum + jnp.sum(grad_pre.astype(jnp.float32), axis=0, keepdims=True)
        total[half, :] += dot(inner_grad[half, :], turned[...])
    inner_ref[0] = bias_sum
    grad_up = dot(turned_normed[...], inner_grad[...])
    split_halves(grad_up, stage, core, keep_ref, send_ref, (0, 0, 0))
    grad_down = dot(turned_grad[...], act_ref[...])
    split_halves(grad_down, stage, core, keep_ref, send_ref, (0, 1, 0))

    @pl.when(chunk == pl.num_programs(0) - 1)
    def _():
        gain_sum = jnp.zeros((1, total.shape[1]), jnp.float32)
        offset_sum = jnp.zeros((1, total.shape[1]), jnp.float32)
        for block in range(blocks):
            rows = slice(block * IMAGE_ROWS, (block + 1) * IMAGE_ROWS)
            unit, inverse = unit_norm(middle_ref[rows, :])
            pulled = total[rows, :]
            gain_sum = gain_sum + jnp.sum(pulled * unit, axis=0, keepdims=True)
            offset_sum = offset_sum + jnp.sum(pulled, axis=0, keepdims=True)
            out_ref[rows, :] = grad_ref[rows, :] + norm_pull(
                pulled, unit, inverse, vector_ref[2:3, :]
            )
        small_ref[0:1, :] = gain_sum
        small_ref[1:2, :] = offset_sum


def feed_back(ids, counts, grad, middle, weights, vectors, act, slope, after=()):
    layer, own, held, first_unit = weights
    rep_count, shard_count = len(held), held[0].shape[1] + 1
    part_rows, piece = held[0].shape[2:]
    tokens, width = middle.shape
    chunks = 4 * width // piece
    half = shard_count // 2
    units = chunks // half
    grad_shape = (units, 2, half, rep_count // 2, part_rows, piece)
    grad_spec = pl.BlockSpec(
        (1, 2, 1) + grad_shape[3:], lambda chunk: (chunk % units, 0, chunk // units, 0, 0, 0)
    )
    weight_values, weight_specs = weight_args(layer, own, held, first_unit, units)
    out = ordered_call(
        functools.partial(feed_back_kernel, rep_count, grad.ndim > 2),
        (ids, counts, grad, middle, vectors, act, slope, *weight_values),
        after,
        grid=(chunks,),
        in_specs=[
            pl.BlockSpec(memory_space=pltpu.SMEM),
            pl.BlockSpec(memory_space=pltpu.SMEM),
            once(grad.shape, (0,) * grad.ndim),
            once((tokens, width), (0, 0)),
            once(vectors.shape, (0, 0)),
            pl.BlockSpec((tokens, piece), lambda chunk: (0, chunk)),
            pl.BlockSpec((tokens, piece), lambda chunk: (0, chunk)),
        ]
        + weight_specs,
        out_specs=[
            pl.BlockSpec((tokens, width), lambda chunk: (0, 0)),
            pl.BlockSpec((8, width), lambda chunk: (0, 0)),
            pl.BlockSpec((1, 1, piece), lambda chunk: (chunk, 0, 0)),
            grad_spec,
            grad_spec,
        ],
        out_shape=[
            jax.ShapeDtypeStruct((tokens, width), jnp.float32),
            jax.ShapeDtypeStruct((8, width), jnp.float32),
            jax.ShapeDtypeStruct((chunks, 1, piece), jnp.float32),
            jax.ShapeDtypeStruct(grad_shape, jnp.bfloat16),
            jax.ShapeDtypeStruct(grad_shape, jnp.bfloat16),
        ],
        scratch_shapes=[
            pltpu.VMEM((tokens, width), jnp.bfloat16),
            pltpu.VMEM((tokens, width), jnp.bfloat16),
            pltpu.VMEM((tokens, piece), jnp.bfloat16),
            pltpu.VMEM((tokens, width), jnp.float32),
            pltpu.VMEM((rep_count, part_rows, piece), jnp.float32),
            pltpu.VMEM((units, shard_count, rep_count, part_rows, piece), jnp.bfloat16),
            pltpu.VMEM((width, tokens), jnp.bfloat16),
            pltpu.VMEM((width, tokens), jnp.bfloat16),
            pltpu.VMEM((piece, width), jnp.bfloat16),
        ]
        + [
            pltpu.VMEM((half.stop - half.start, piece), jnp.float32) for half in row_halves(tokens)
        ]
        + ([pltpu.VMEM((tokens, width), jnp.float32)] if grad.ndim > 2 else []),
        compiler_params=params(38 * 1024 * 1024),
        cost_estimate=cost(tokens * width * width * 32, 24e6),
        name="feed_back",
    )
    flat = (units, shard_count) + grad_shape[3:]
    return out[0], out[1], out[2], out[3].reshape(flat), out[4].reshape(flat), out[5]


def attend_back_kernel(
    shifted,
    held_count,
    final,
    ids_ref,
    grad_ref,
    x_ref,
    vector_ref,
    project_ref,
    prob_ref,
    attended_ref,
    *refs,
):
    own_ref, held, refs = refs[0], refs[1 : 1 + held_count], refs[1 + held_count :]
    out_ref, small_ref, score_ref = refs[:3]
    keep_refs, send_refs, refs = refs[3:5], refs[5:7], refs[7:]
    field, grad_field, states, grad_heads, grad_states = refs[:5]
    normed_all, project_all, attended_all, grad_all, stage, weight_ref, turned = refs[5:12]
    image = pl.program_id(0)
    core = lax.rem(ids_ref[1], 2)
    shard_count = weight_ref.shape[1]
    piece = weight_ref.shape[4]
    width = x_ref.shape[1]
    third = 3 * shard_count // 4
    head_scale = (width // HEADS) ** (-0.5)
    rows_all = pl.ds(pl.multiple_of(image * ROWS, ROWS), ROWS)

    @pl.when(image == 0)
    def _():
        fill_weights(ids_ref, own_ref, held, weight_ref)
        for shard in range(shard_count):
            turned[shard] = weight_of(weight_ref, 0, shard).T
        small_ref[...] = jnp.zeros(small_ref.shape, jnp.float32)
        score_ref[...] = jnp.zeros(score_ref.shape, jnp.float32)

    into_windows(field, x_ref, shifted)
    into_windows(grad_field, grad_ref, shifted)
    unit, inverse = unit_norm(field[:ROWS, :])
    normed_all[rows_all, :] = (unit * vector_ref[0:1, :] + vector_ref[1:2, :]).astype(
        jnp.bfloat16
    )
    field[:ROWS, :] = unit
    grad_branch = grad_field[:ROWS, :].astype(jnp.bfloat16)
    grad_all[rows_all, :] = grad_branch
    attended_all[rows_all, :] = attended_ref[...]
    small_ref[4:5, :] += jnp.sum(grad_branch.astype(jnp.float32), axis=0, keepdims=True)
    grad_heads[ROWS:SPARE, :] = jnp.zeros((SPARE - ROWS, width), jnp.float32)
    states[ROWS:SPARE, :] = jnp.zeros((SPARE - ROWS, states.shape[1]), jnp.float32)
    states[:ROWS, :] = project_ref[...].astype(jnp.float32)
    branch = jnp.zeros((ROWS, width), jnp.float32)
    for shard in range(third, shard_count):
        start = (shard - third) * piece
        branch = branch + dot(grad_branch[:, start : start + piece], turned[shard])
    grad_heads[:ROWS, :] = branch
    select = block_mask(TOKENS)
    for window in range(WINDOWS):
        rows = slice(window * WINDOW_ROWS, window * WINDOW_ROWS + SLOT)
        out_rows = slice(window * WINDOW_ROWS, (window + 1) * WINDOW_ROWS)
        for group in range(HEADS // GROUP):
            first = group * 128
            cols = slice(group * GROUP * SLOT, (group + 1) * GROUP * SLOT)
            query = states[rows, first : first + 128].astype(jnp.bfloat16)
            key = states[rows, width + first : width + first + 128].astype(jnp.bfloat16)
            value = states[rows, 2 * width + first : 2 * width + first + 128].astype(jnp.bfloat16)
            arrived = grad_heads[rows, first : first + 128].astype(jnp.bfloat16)
            spread_query = jnp.concatenate([query] * GROUP, axis=0) * select
            spread_grad = jnp.concatenate([arrived] * GROUP, axis=0) * select
            soft = prob_ref[window, :, cols]
            exact = soft.astype(jnp.float32)[:WINDOW_ROWS]
            grad_soft = dot_cols(value, spread_grad)[:WINDOW_ROWS]
            delta = jnp.sum(grad_soft * exact, axis=0, keepdims=True)
            grad_scores = exact * (grad_soft - delta)
            score_ref[:, cols] += grad_scores
            grad_raw = pad_slot(grad_scores * head_scale)
            grad_key = dot(grad_raw, spread_query)[:WINDOW_ROWS]
            grad_value = dot(soft, spread_grad)[:WINDOW_ROWS]
            grad_query = fold_heads(dot_rows(grad_raw, key))[:WINDOW_ROWS]
            grad_states[out_rows, first : first + 128] = grad_query
            grad_states[out_rows, width + first : width + first + 128] = grad_key
            grad_states[out_rows, 2 * width + first : 2 * width + first + 128] = grad_value
    grad_project = grad_states[...].astype(jnp.bfloat16)
    project_all[rows_all, :] = grad_project
    column = jnp.sum(grad_project.astype(jnp.float32), axis=0, keepdims=True)
    small_ref[2:3, :] += column[:, :width]
    small_ref[3:4, :] += column[:, 2 * width :]
    pulled = jnp.zeros((ROWS, width), jnp.float32)
    for shard in range(third):
        pulled = pulled + dot(
            grad_project[:, shard * piece : (shard + 1) * piece], turned[shard]
        )
    unit = field[:ROWS, :]
    small_ref[0:1, :] += jnp.sum(pulled * unit, axis=0, keepdims=True)
    small_ref[1:2, :] += jnp.sum(pulled, axis=0, keepdims=True)
    grad_field[:ROWS, :] = grad_field[:ROWS, :] + norm_pull(
        pulled, unit, inverse, vector_ref[0:1, :]
    )
    if final:
        from_windows(refs[12], grad_field, shifted)
        rows_to_field(out_ref, 0, refs[12], 0)
    else:
        from_windows(out_ref, grad_field, shifted)

    @pl.when(image == pl.num_programs(0) - 1)
    def _():
        turned_normed, turned_attended = normed_all[...].T, attended_all[...].T
        for shard in range(shard_count):
            if shard < third:
                grad = dot(turned_normed, project_all[:, shard * piece : (shard + 1) * piece])
            else:
                start = (shard - third) * piece
                grad = dot(turned_attended, grad_all[:, start : start + piece])
            half, index = divmod(shard, shard_count // 2)
            split_halves(grad, stage, core, keep_refs[half], send_refs[half], (0, index))


def attend_back(
    shifted, ids, grad, x_rows, weights, vectors, project, prob, attended, final_shape, after=()
):
    layer, own, held, first_unit = weights
    rep_count, shard_count = len(held), held[0].shape[1] + 1
    part_rows, piece = held[0].shape[2:]
    width = x_rows.shape[1]
    images = x_rows.shape[0] // IMAGE_ROWS
    grad_shape = (1, shard_count // 2, rep_count // 2, part_rows, piece)
    weight_values, weight_specs = weight_args(layer, own, held, first_unit, 1)
    return ordered_call(
        functools.partial(attend_back_kernel, shifted, rep_count, final_shape is not None),
        (ids, grad, x_rows, vectors, project, prob, attended, *weight_values),
        after,
        grid=(images,),
        in_specs=[
            pl.BlockSpec(memory_space=pltpu.SMEM),
            pl.BlockSpec((IMAGE_ROWS, width), lambda image: (image, 0)),
            pl.BlockSpec((IMAGE_ROWS, width), lambda image: (image, 0)),
            once(vectors.shape, (0, 0)),
            pl.BlockSpec((ROWS, 3 * width), lambda image: (image, 0)),
            pl.BlockSpec((WINDOWS, SLOT, HEADS * SLOT), lambda image: (image, 0, 0)),
            pl.BlockSpec((ROWS, width), lambda image: (image, 0)),
        ]
        + weight_specs,
        out_specs=[
            pl.BlockSpec((1,) + final_shape[1:], lambda image: (image, 0, 0, 0))
            if final_shape
            else pl.BlockSpec((IMAGE_ROWS, width), lambda image: (image, 0)),
            pl.BlockSpec((8, width), lambda image: (0, 0)),
            pl.BlockSpec((WINDOW_ROWS, HEADS * SLOT), lambda image: (0, 0)),
        ]
        + [pl.BlockSpec(grad_shape, lambda image: (0, 0, 0, 0, 0))] * 4,
        out_shape=[
            jax.ShapeDtypeStruct(final_shape, jnp.bfloat16)
            if final_shape
            else jax.ShapeDtypeStruct((images * IMAGE_ROWS, width), jnp.float32),
            jax.ShapeDtypeStruct((8, width), jnp.float32),
            jax.ShapeDtypeStruct((WINDOW_ROWS, HEADS * SLOT), jnp.float32),
        ]
        + [jax.ShapeDtypeStruct(grad_shape, jnp.bfloat16)] * 4,
        scratch_shapes=[
            pltpu.VMEM((SPARE, width), jnp.float32),
            pltpu.VMEM((SPARE, width), jnp.float32),
            pltpu.VMEM((SPARE, 3 * width), jnp.float32),
            pltpu.VMEM((SPARE, width), jnp.float32),
            pltpu.VMEM((ROWS, 3 * width), jnp.float32),
            pltpu.VMEM((images * ROWS, width), jnp.bfloat16),
            pltpu.VMEM((images * ROWS, 3 * width), jnp.bfloat16),
            pltpu.VMEM((images * ROWS, width), jnp.bfloat16),
            pltpu.VMEM((images * ROWS, width), jnp.bfloat16),
            pltpu.VMEM((rep_count, part_rows, piece), jnp.float32),
            pltpu.VMEM((1, shard_count, rep_count, part_rows, piece), jnp.bfloat16),
            pltpu.VMEM((shard_count, piece, width), jnp.bfloat16),
        ]
        + ([pltpu.VMEM((IMAGE_ROWS, width), jnp.float32)] if final_shape else []),
        compiler_params=params(34 * 1024 * 1024),
        cost_estimate=cost(images * ROWS * width * width * 32, 20e6),
        name="attend_back_shifted" if shifted else "attend_back",
    )


def relay_kernel(count, extra, ids_ref, *refs):
    arrived, outs = refs[:count], refs[count:]
    for key, ref in enumerate(arrived):
        spot = 0
        for line_ref in outs[:-1] if extra else outs:
            rows = line_ref.shape[2]
            for index in range(line_ref.shape[0]):
                if ref.shape[0] == 1:
                    line_ref[index, key] = ref[0, spot * rows : (spot + 1) * rows, :]
                else:
                    line_ref[index, key] = ref[spot]
                spot += 1
        if extra:
            outs[-1][ids_ref[0] ^ (key + 1)] = ref[0, ref.shape[1] - extra :, :]


def relay(ids, arrived, split, extra, after=(), memory=SMALL_VMEM):
    units, rows, piece = arrived[0].shape
    part_rows = (units * rows - extra) // sum(split)
    shapes = [(count, len(arrived), part_rows, piece) for count in split]
    if extra:
        shapes.append((len(arrived) + 1, extra, piece))
    return ordered_call(
        functools.partial(relay_kernel, len(arrived), extra),
        (ids, *arrived),
        after,
        [pl.BlockSpec(memory_space=pltpu.SMEM)]
        + [pl.BlockSpec(memory_space=pltpu.VMEM)] * len(arrived),
        out_shape=[jax.ShapeDtypeStruct(shape, jnp.bfloat16) for shape in shapes],
        compiler_params=params(memory),
        cost_estimate=cost(0, 1e6),
        name="relay",
    )


def parts_kernel(layers, ids_ref, *refs):
    vector_ref, weight_refs, outs = refs[0], refs[1 : 1 + 2 * layers], refs[1 + 2 * layers :]
    piece = outs[0].shape[2]
    rows = weight_refs[0].shape[1]

    def units_of(index):
        ref = weight_refs[index]
        return [
            ref[0, :, start : start + piece].astype(jnp.bfloat16)
            for start in range(0, ref.shape[2], piece)
        ]

    spot = 0
    for part in units_of(1) + units_of(0):
        outs[0][0, spot : spot + rows, :] = part
        spot += rows
    lines = []
    length = vector_ref.shape[1]
    for layer in range(layers):
        for start in range(0, length, piece):
            line = vector_ref[layer : layer + 1, start : min(start + piece, length)]
            if line.shape[1] < piece:
                spare = jnp.zeros((1, piece - line.shape[1]), jnp.float32)
                line = jnp.concatenate([line, spare], axis=1)
            lines.append(line)
    lines.append(jnp.zeros((outs[0].shape[1] - spot - len(lines), piece), jnp.float32))
    outs[0][0, spot:, :] = jnp.concatenate(lines, axis=0).astype(jnp.bfloat16)
    unit = 0
    for layer in range(1, layers):
        for part in units_of(2 * layer + 1) + units_of(2 * layer):
            outs[1][unit] = part
            unit += 1


def cut_parts(ids, attention, feedforward, vectors, extra):
    layers, rows, piece = attention.shape
    part_rows = rows // lax.axis_size("rep")
    units = 1 + feedforward.shape[2] // piece

    def spec(weight, layer):
        return pl.BlockSpec(
            (1, part_rows, weight.shape[2]), lambda step, ids: (layer, ids[1], 0)
        )

    shapes = [(1, units * part_rows + extra, piece), ((layers - 1) * units, part_rows, piece)]
    return ordered_call(
        functools.partial(parts_kernel, layers),
        (ids, vectors, *([attention, feedforward] * layers)),
        (),
        [pl.BlockSpec(vectors.shape, lambda step, ids: (0, 0))]
        + [spec(weight, layer) for layer in range(layers) for weight in (attention, feedforward)],
        prefetch=1,
        grid=(1,),
        out_specs=[pl.BlockSpec(shape, lambda step, ids: (0, 0, 0)) for shape in shapes],
        out_shape=[jax.ShapeDtypeStruct(shape, jnp.bfloat16) for shape in shapes],
        compiler_params=params(),
        cost_estimate=cost(0, 5e5),
        name="cut_parts",
    )


def xor_send(value, axis, key):
    size = lax.axis_size(axis)
    return lax.ppermute(value, axis, [(index, index ^ key) for index in range(size)])


def send_line(part, gate=None):
    held = {0: part}
    for bit in reversed(range(lax.axis_size("shard").bit_length() - 1)):
        for key in list(held):
            block = held[key]
            if gate is not None and len(held) > 1:
                block, _ = lax.optimization_barrier((block, gate))
            held[key ^ (1 << bit)] = xor_send(block, "shard", 1 << bit)
    return [held[key] for key in range(1, len(held))]


def hold(chips, after=()):
    token = ()
    if after:
        *chips, token = lax.optimization_barrier((*chips, *after))
        token = [token]
    own, _ = lax.optimization_barrier((chips[0], chips[1]))
    others = [xor_send(block, "rep", 1) for block in [own] + chips[1:]]
    return [block for pair in zip(chips, others) for block in pair], token


def core_sum_kernel(units, ids_ref, *refs):
    chip = ids_ref[1] // 2
    outs = refs[2 * len(units) :]
    first = 0
    for group, count in enumerate(units):
        keep_ref, arrived_ref = refs[2 * group : 2 * group + 2]

        @pl.when((pl.program_id(0) >= first) & (pl.program_id(0) < first + count))
        def _():
            for key, out in enumerate(outs):
                for shard in range(keep_ref.shape[1]):
                    total = keep_ref[0, shard, chip ^ key].astype(jnp.float32)
                    total = total + arrived_ref[0, shard, chip ^ key].astype(jnp.float32)
                    out[0, shard] = total.astype(jnp.bfloat16)

        first += count


def core_sum(ids, pairs, after=(), moved=1e5):
    half = lax.axis_size("shard") // 2
    pairs = [
        [value.reshape((-1, half) + value.shape[2:]) for value in pair] for pair in pairs
    ]
    _, _, chips, part_rows, piece = pairs[0][0].shape
    units = [keep.shape[0] for keep, _ in pairs]
    specs, first = [], 0
    for count in units:

        def index(unit, first=first, count=count):
            return (jnp.clip(unit - first, 0, count - 1), 0, 0, 0, 0)

        specs += [pl.BlockSpec((1, half, chips, part_rows, piece), index)] * 2
        first += count
    *sums, token = ordered_call(
        functools.partial(core_sum_kernel, units),
        (ids, *[value for pair in pairs for value in pair]),
        after,
        [pl.BlockSpec(memory_space=pltpu.SMEM)] + specs,
        grid=(sum(units),),
        out_specs=[pl.BlockSpec((1, half, part_rows, piece), lambda unit: (unit, 0, 0, 0))]
        * chips,
        out_shape=[jax.ShapeDtypeStruct((sum(units), half, part_rows, piece), jnp.bfloat16)]
        * chips,
        compiler_params=params(SMALL_VMEM),
        cost_estimate=cost(1e5, moved),
        name="core_sum",
    )
    return [part.reshape((-1, 2 * half, part_rows, piece)) for part in sums] + [token]


def plane_sum_kernel(count, rows, ids_ref, *refs):
    parts, vectors, outs = refs[:count], refs[count:-2], refs[-2:]
    for key in range(parts[0].shape[1]):
        shard = ids_ref[0] ^ key
        out = outs[key % 2]
        for unit in range(parts[0].shape[0]):
            total = parts[0][unit, shard].astype(jnp.float32)
            for part in parts[1:]:
                total = total + part[unit, shard].astype(jnp.float32)
            out[key // 2, unit, :rows, :] = total.astype(jnp.bfloat16)
        if vectors:
            total = vectors[0][shard].astype(jnp.float32) + vectors[1][shard].astype(jnp.float32)
            out[key // 2, 0, rows:, :] = total.astype(jnp.bfloat16)


def plane_sum(ids, parts, vectors=(), after=(), moved=4e6):
    units, shard_count, part_rows, piece = parts[0].shape
    extra = vectors[0].shape[1] if vectors else 0
    shape = (shard_count // 2, units, part_rows + extra, piece)
    return ordered_call(
        functools.partial(plane_sum_kernel, len(parts), part_rows),
        (ids, *parts, *vectors),
        after,
        [pl.BlockSpec(memory_space=pltpu.SMEM)]
        + [pl.BlockSpec(memory_space=pltpu.VMEM)] * (len(parts) + len(vectors)),
        out_shape=[jax.ShapeDtypeStruct(shape, jnp.bfloat16)] * 2,
        compiler_params=params(SMALL_VMEM),
        cost_estimate=cost(parts[0].size * 4, moved),
        name="plane_sum",
    )


def pair_sum_kernel(keep_ref, arrived_ref, *outs):
    for index in range(keep_ref.shape[0]):
        total = keep_ref[index].astype(jnp.float32) + arrived_ref[index].astype(jnp.float32)
        outs[index % 2][index // 2] = total.astype(jnp.bfloat16)


def pair_sum(keep, arrived, after=(), moved=4e6):
    count = keep.shape[0]
    shape = (max(count // 2, 1),) + keep.shape[1:]
    return ordered_call(
        pair_sum_kernel,
        (keep, arrived),
        after,
        [pl.BlockSpec(memory_space=pltpu.VMEM)] * 2,
        out_shape=[jax.ShapeDtypeStruct(shape, jnp.bfloat16)] * min(count, 2),
        compiler_params=params(SMALL_VMEM),
        cost_estimate=cost(keep.size, moved),
        name="pair_sum",
    )


def final_sum_kernel(*refs):
    out_ref = refs[-1]
    spot = 0
    for keep_ref, arrived_ref in (refs[0:2], refs[2:4]):
        rows = keep_ref.shape[2]
        for unit in range(keep_ref.shape[1]):
            total = keep_ref[0, unit].astype(jnp.float32) + arrived_ref[0, unit].astype(jnp.float32)
            out_ref[0, spot : spot + rows, :] = total.astype(jnp.bfloat16)
            spot += rows


def final_sum(first, second, after=()):
    rows = sum(pair[0].shape[1] * pair[0].shape[2] for pair in (first, second))
    args = (*first, *second)
    return ordered_call(
        final_sum_kernel,
        args,
        after,
        [pl.BlockSpec(memory_space=pltpu.VMEM)] * len(args),
        out_shape=jax.ShapeDtypeStruct((1, rows, args[0].shape[3]), jnp.bfloat16),
        compiler_params=params(SMALL_VMEM),
        cost_estimate=cost(1e6, 4e6),
        name="final_sum",
    )


def send_pair(value):
    return xor_send(value, "rep", 1)


def send_chips(parts):
    return [parts[0]] + [
        xor_send(parts[key], "rep", 2 * key) for key in range(1, lax.axis_size("rep") // 2)
    ]


def swap_line(away):
    stage = lax.axis_size("shard") // (2 * away.shape[0])
    return xor_send(away, "shard", stage)


def narrow_line(keep, arrived, after):
    token = after[0]
    while keep.shape[0] > 1:
        keep, away, token = pair_sum(keep, arrived, [token])
        arrived = swap_line(away)
    return keep, arrived, token


def finish_line(keep, arrived, after):
    while True:
        *sums, token = pair_sum(keep, arrived, after)
        if len(sums) == 1:
            return sums[0][0], token
        keep, away = sums
        arrived, after = swap_line(away), ()


def spread(total):
    chips = [total] + [
        xor_send(total, "rep", 2 * key) for key in range(1, lax.axis_size("rep") // 2)
    ]
    others = [send_pair(block) for block in chips]
    return [block for pair in zip(chips, others) for block in pair]


def adam_terms(weight, grad, first, second, rate, decay):
    first_new = BETA_ONE * first + (1.0 - BETA_ONE) * grad
    second_new = BETA_TWO * second + (1.0 - BETA_TWO) * grad * grad
    second_hat = second_new * (1.0 / (1.0 - BETA_TWO**STEP))
    below = second_hat * lax.rsqrt(jnp.maximum(second_hat, 1e-37)) + EPS_ADAM
    near = pl.reciprocal(below, approx=True)
    near = near * (2.0 - below * near)
    weight_new = weight * (1.0 - rate * decay) - first_new * (rate / (1.0 - BETA_ONE**STEP)) * near
    return (weight_new, first_new, second_new)


def ahead_kernel(jobs, *refs):
    count = 3 * len(jobs)
    states, outs, sems = refs[: -count - 1], refs[-count - 1 : -1], refs[-1]
    copies = []
    for job, (kind, layer, _) in enumerate(jobs):
        for index in range(3):
            copies.append(
                pltpu.make_async_copy(
                    states[3 * kind + index].at[layer],
                    outs[3 * job + index],
                    sems.at[3 * job + index],
                )
            )
    start_all(copies)
    for copy in copies:
        copy.wait()


def start_all(copies):
    for copy in copies:
        copy.start()


def load_ahead(jobs, kinds, after):
    states = [far(state) for kind in kinds for state in kind]
    *outs, token = ordered_call(
        functools.partial(ahead_kernel, jobs),
        tuple(states),
        after,
        [pl.BlockSpec(memory_space=pl.ANY)] * len(states),
        out_specs=[pl.BlockSpec(memory_space=pltpu.VMEM)] * (3 * len(jobs)),
        out_shape=[
            pltpu.VMEM(kinds[kind][0].shape[1:], jnp.float32) for kind, _, _ in jobs for _ in range(3)
        ],
        scratch_shapes=[pltpu.SemaphoreType.DMA((3 * len(jobs),))],
        compiler_params=params(SMALL_VMEM),
        cost_estimate=cost(1e5, 1e6),
        name="load_ahead",
    )
    return outs, token


def adam_kernel(count, jobs, ahead, ids_ref, *refs):
    held, refs = refs[:count], refs[count:]
    ready, refs = refs[: 3 * len(jobs) * ahead], refs[3 * len(jobs) * ahead :]
    kinds = 1 + max(kind for kind, _, _ in jobs)
    states = []
    if not ahead:
        states, refs = [refs[3 * kind : 3 * kind + 3] for kind in range(kinds)], refs[3 * kinds :]
    sems, refs = refs[-3:], refs[:-3]
    made, refs = refs[-len(jobs) :], refs[: -len(jobs)]
    loaded = [ready[3 * job : 3 * job + 3] for job in range(len(jobs))]
    if not ahead:
        loaded, refs = refs[-len(jobs) :], refs[: -len(jobs)]
    stage, refs = refs[-1], refs[:-1]
    outs = refs[-4 * kinds :]
    outs = [outs[4 * kind : 4 * kind + 4] for kind in range(kinds)]
    steps, rows = made[0].shape[1:3]
    piece = stage.shape[2]
    part_rows = rows * steps // count
    held_copies = [
        pltpu.make_async_copy(held[key].at[0], stage.at[ids_ref[1] ^ key], sems[0].at[key])
        for key in range(count)
    ]
    loads, stores = {}, {}
    for job, (kind, layer, _) in enumerate(jobs):
        for step in range(steps):
            here = pl.ds(step * rows, rows)
            loads[job, step] = [
                pltpu.make_async_copy(
                    state.at[layer, here], loaded[job].at[index, step], sems[1].at[job, index, step]
                )
                for index, state in enumerate(states[kind] if states else [])
            ]
            stores[job, step] = [
                pltpu.make_async_copy(
                    made[job].at[index, step], out.at[layer, here], sems[2].at[job, index, step]
                )
                for index, out in enumerate(outs[kind])
            ]
    for copy in held_copies + [copy for copies in loads.values() for copy in copies]:
        copy.start()
    for copy in held_copies:
        copy.wait()
    for job, (_, _, first) in enumerate(jobs):
        for step in range(steps):
            for copy in loads[job, step]:
                copy.wait()
            for part in range(rows // part_rows):
                lines = slice(part * part_rows, (part + 1) * part_rows)
                for unit in range(made[job].shape[3] // piece):
                    cols = slice(unit * piece, (unit + 1) * piece)
                    spot = first + unit * part_rows
                    grad = stage[step * (rows // part_rows) + part, spot : spot + part_rows, :]
                    grad = grad.astype(jnp.float32)
                    made[job][0, step, lines, cols] = grad
                    if ahead:
                        spots = slice(step * rows + lines.start, step * rows + lines.stop)
                        old = [ref[spots, cols] for ref in loaded[job]]
                    else:
                        old = [loaded[job][index, step, lines, cols] for index in range(3)]
                    new = adam_terms(old[0], grad, *old[1:], RATE_MATRIX, DECAY_MATRIX)
                    for index, value in enumerate(new):
                        made[job][index + 1, step, lines, cols] = value
            for copy in stores[job, step]:
                copy.start()
    for copies in stores.values():
        for copy in copies:
            copy.wait()


def adam(ids, held, jobs, kinds, prior=(), after=(), ready=()):
    held_rows, piece = held[0].shape[1:]
    steps = 4
    states = [] if ready else [far(state) for kind in kinds for state in kind]
    shapes = [kind[0].shape for kind in kinds]
    blocks = [(steps, shapes[kind][1] // steps, shapes[kind][2]) for kind, _, _ in jobs]
    start = 1 + len(held) + len(ready) + len(states)
    first_out = 4 * (len(kinds) - 1)
    anywhere = pl.BlockSpec(memory_space=pl.ANY)
    *outs, token = ordered_call(
        functools.partial(adam_kernel, len(held), jobs, int(bool(ready))),
        (ids, *held, *ready, *states, *prior),
        after,
        [pl.BlockSpec(memory_space=pltpu.SMEM)]
        + [anywhere] * len(held)
        + [pl.BlockSpec(memory_space=pltpu.VMEM)] * len(ready)
        + [anywhere] * (len(states) + len(prior)),
        out_specs=[anywhere] * (4 * len(kinds)),
        out_shape=[
            jax.ShapeDtypeStruct(shape, jnp.float32) for shape in shapes for _ in range(4)
        ],
        input_output_aliases={start + index: first_out + index for index in range(len(prior))},
        scratch_shapes=[pltpu.VMEM((len(held), held_rows, piece), jnp.bfloat16)]
        + ([] if ready else [pltpu.VMEM((3,) + block, jnp.float32) for block in blocks])
        + [pltpu.VMEM((4,) + block, jnp.float32) for block in blocks]
        + [
            pltpu.SemaphoreType.DMA((len(held),)),
            pltpu.SemaphoreType.DMA((len(jobs), 3, steps)),
            pltpu.SemaphoreType.DMA((len(jobs), 4, steps)),
        ],
        compiler_params=params(30 * 1024 * 1024 if ready else 20 * 1024 * 1024),
        cost_estimate=cost(1e6, 3e7),
        name="adam",
    )
    return [outs[4 * kind : 4 * kind + 4] for kind in range(len(kinds))], token


def vector_adam_kernel(count, rows, ids_ref, *refs):
    totals, states = refs[:count], refs[count : count + 3]
    outs, stage = refs[count + 3 : count + 7], refs[-1]
    for key, ref in enumerate(totals):
        stage[(ids_ref[1] // 2) ^ key] = ref[0, rows:, :].astype(jnp.float32)
    total = stage[0]
    for chip in range(1, count):
        total = total + stage[chip]
    layers, length = states[0].shape
    piece = total.shape[1]
    line = 0
    for layer in range(layers):
        for start in range(0, length, piece):
            here = slice(start, min(start + piece, length))
            this = slice(layer, layer + 1)
            grad = total[line : line + 1, : here.stop - here.start]
            outs[0][this, here] = grad
            new = adam_terms(*[ref[this, here] for ref in states[:1]], grad, *[
                ref[this, here] for ref in states[1:]
            ], RATE_VECTOR, 0.0)
            for out, value in zip(outs[1:], new):
                out[this, here] = value
            line += 1


def vector_adam(ids, totals, rows, weight, first, second, after=()):
    extra = totals[0].shape[1] - rows
    return ordered_call(
        functools.partial(vector_adam_kernel, len(totals), rows),
        (ids, *totals, weight, first, second),
        after,
        [pl.BlockSpec(memory_space=pltpu.SMEM)]
        + [pl.BlockSpec(memory_space=pltpu.VMEM)] * (len(totals) + 3),
        out_shape=[jax.ShapeDtypeStruct(weight.shape, jnp.float32)] * 4,
        scratch_shapes=[pltpu.VMEM((len(totals), extra, totals[0].shape[2]), jnp.float32)],
        compiler_params=params(SMALL_VMEM),
        cost_estimate=cost(weight.size * 10, weight.size * 16),
        name="vector_adam",
    )


def join_vectors(lines, layers, length):
    shard_count, _, piece = lines.shape
    used = -(-length // piece)
    lines = lines[:, : layers * used].reshape(shard_count, layers, used * piece)[:, :, :length]
    return lines.transpose(1, 0, 2).reshape(layers, shard_count * length)


def pack_kernel(length, has_prior, rel_ref, one_ref, two_ref, inner_ref, score_ref, *refs):
    prior_ref = refs[0] if has_prior else None
    out_ref, turned = refs[-2:]
    shard_count, _, piece = out_ref.shape
    spare = jnp.zeros((SLOT - WINDOW_ROWS, score_ref.shape[1]), jnp.float32)
    turned[...] = jnp.concatenate([score_ref[...], spare], axis=0).T
    entries = lax.broadcasted_iota(jnp.int32, (SLOT, 256), 1)
    table = jnp.zeros((2 * HEADS, 256), jnp.float32)
    for token in range(TOKENS):
        exact = turned[pl.ds(token, HEADS, stride=SLOT), :]
        high = exact.astype(jnp.bfloat16)
        low = (exact - high.astype(jnp.float32)).astype(jnp.bfloat16)
        same = jnp.where(rel_ref[:, token : token + 1] == entries, 1.0, 0.0).astype(jnp.bfloat16)
        table = table + dot(jnp.concatenate([high, low], axis=0), same)
    table = table[:HEADS] + table[HEADS:]
    if piece > 256:
        table = jnp.concatenate([table, jnp.zeros((HEADS, piece - 256), jnp.float32)], axis=1)
    rows = []
    for ref, row in (
        (one_ref, 0),
        (one_ref, 1),
        (two_ref, 0),
        (two_ref, 1),
        (one_ref, 2),
        (one_ref, 3),
        (one_ref, 4),
        (two_ref, 2),
    ):
        for start in range(0, one_ref.shape[1], piece):
            rows.append(ref[row : row + 1, start : start + piece])
    rows += [inner_ref[chunk] for chunk in range(inner_ref.shape[0])]
    lanes = lax.broadcasted_iota(jnp.int32, (1, piece), 1)
    entry_rows = [jnp.zeros((1, piece), jnp.float32)] * (-(-HEADS * TABLE // piece) + 1)
    for head in range(HEADS):
        row, lane = divmod(head * TABLE, piece)
        moved = table[head : head + 1]
        if lane:
            moved = pltpu.roll(moved, lane, 1)
        entry_rows[row] = entry_rows[row] + jnp.where(lanes >= lane, moved, 0.0)
        if lane + TABLE > piece:
            entry_rows[row + 1] = entry_rows[row + 1] + jnp.where(lanes < lane, moved, 0.0)
    used = -(-length // piece)
    rows += entry_rows
    rows += [jnp.zeros((1, piece), jnp.float32)] * (-len(rows) % 8 + 8)
    flat = jnp.concatenate(rows, axis=0)
    lanes = lax.broadcasted_iota(jnp.int32, (used, piece), 1)
    for shard in range(shard_count):
        row, lane = divmod(shard * length, piece)
        moved = pltpu.roll(flat, piece - lane, 1) if lane else flat
        lines = jnp.where(lanes < piece - lane, moved[row : row + used], moved[row + 1 : row + 1 + used])
        parts = [lines]
        if has_prior:
            parts.append(prior_ref[shard, :used, :])
        count = len(parts) * used
        parts.append(jnp.zeros((out_ref.shape[1] - count, piece), jnp.float32))
        out_ref[shard] = jnp.concatenate(parts, axis=0).astype(out_ref.dtype)


def pack(rel_slots, small_one, small_two, inner, scores, length, extra, prior=None, after=()):
    shard_count = lax.axis_size("shard")
    prior = () if prior is None else (prior,)
    args = (rel_slots, small_one, small_two, inner, scores) + prior
    return ordered_call(
        functools.partial(pack_kernel, length, len(prior)),
        args,
        after,
        [pl.BlockSpec(memory_space=pltpu.VMEM)] * len(args),
        out_shape=jax.ShapeDtypeStruct(
            (shard_count, extra if prior else 8, inner.shape[2]),
            jnp.bfloat16 if prior else jnp.float32,
        ),
        scratch_shapes=[pltpu.VMEM((HEADS * SLOT, SLOT), jnp.float32)],
        compiler_params=params(SMALL_VMEM),
        cost_estimate=cost(1e6, 1e6),
        name="pack",
    )


def image_rows(field):
    images, width = field.shape[0], field.shape[-1]
    flat = field.reshape(images, IMAGE, width)
    flat = jnp.pad(flat, ((0, 0), (0, IMAGE_ROWS - IMAGE), (0, 0)))
    return flat.reshape(images * IMAGE_ROWS, width)


def pair_mask(region_ids):
    images = region_ids.shape[0]
    cells = region_ids.reshape(images, ACROSS, WINDOW, ACROSS, WINDOW).transpose(0, 1, 3, 2, 4)
    cells = cells.reshape(images * WINDOWS, TOKENS)
    keys = jnp.pad(cells, ((0, 0), (0, WINDOW_ROWS - TOKENS)))
    queries = jnp.pad(cells, ((0, 0), (0, SLOT - TOKENS)))
    queries = jnp.concatenate([queries] * (128 // SLOT), axis=1)
    same = keys[:, :, None] == queries[:, None, :]
    return jnp.where(same, jnp.float32(0.0), jnp.float32(MASK_FILL))


def pair_slots(rel_index):
    spare = SLOT - TOKENS
    return jnp.pad(rel_index.T, ((0, spare), (0, spare)), constant_values=-1)


def pair_onehot(rel_slots):
    turned = rel_slots[:WINDOW_ROWS].reshape(1, -1)
    return (jnp.arange(TABLE)[:, None] == turned).astype(jnp.bfloat16)


def spread_table(table, onehot):
    bias = dot(table, onehot).reshape(HEADS, WINDOW_ROWS, SLOT).transpose(1, 0, 2)
    bias = bias.reshape(WINDOW_ROWS, HEADS * SLOT)
    real = jnp.arange(WINDOW_ROWS)[:, None] < TOKENS
    return jnp.where(real, bias, jnp.float32(PAD_FILL))


def shards(
    images,
    region_ids,
    image_counts,
    rel_index,
    cotangent,
    attention_weight,
    feedforward_weight,
    vector_params,
    attention_first,
    feedforward_first,
    vector_first,
    attention_second,
    feedforward_second,
    vector_second,
):
    shard_id, rep_id = lax.axis_index("shard"), lax.axis_index("rep")
    ids = jnp.stack([shard_id, rep_id]).astype(jnp.int32)
    width, piece = attention_weight.shape[1:]
    layers, length = vector_params.shape
    extra = -(-layers * -(-length // piece) // 16) * 16
    attention, feedforward = attention_weight, feedforward_weight

    rel_slots = pair_slots(rel_index)
    onehot = pair_onehot(rel_slots)
    mask = pair_mask(region_ids)
    no_mask = jnp.zeros((1, 8, 128), jnp.float32)
    residual = image_rows(images.astype(jnp.float32))

    feed_units = feedforward.shape[2] // piece
    part_zero, part_one, _ = cut_parts(ids, attention, feedforward, vector_params, extra)
    arrived_zero = send_line(part_zero)
    part_one, _ = lax.optimization_barrier((part_one, arrived_zero[1]))
    arrived_one = send_line(part_one, arrived_zero[-1])
    line_zero, lines, token = relay(ids, arrived_zero, [feed_units + 1], extra)
    lines = lax.dynamic_update_index_in_dim(lines, part_zero[0, -extra:], shard_id, 0)
    vectors_full = join_vectors(lines, layers, length)
    bulks = [flat[: 12 * width].astype(jnp.float32).reshape(12, width) for flat in vectors_full]
    inners = [bulk[8:].reshape(-1, 1, piece) for bulk in bulks]
    biases = [
        spread_table(flat[12 * width :].reshape(HEADS, -1), onehot) for flat in vectors_full
    ]
    chip_count = lax.axis_size("rep") // 2
    chips_zero = send_chips([line_zero] * chip_count)
    line_one, token = relay(ids, arrived_one, [feed_units + 1], 0)
    held_zero, token = hold(chips_zero, [token])
    chips_one = send_chips([line_one] * chip_count)
    attend_weights = [(0, attention, held_zero, feed_units)]
    feed_weights = [(0, feedforward, held_zero, 0)]
    first = attend(
        False,
        ids,
        residual,
        attend_weights[0],
        bulks[0],
        biases[0],
        no_mask,
        [*token, mask, biases[1], *bulks, *inners],
    )
    second = feed(ids, first[0], feed_weights[0], bulks[0], inners[0])
    held_one, token = hold(chips_one, [second[3]])
    attend_weights.append((1, attention, held_one, feed_units))
    feed_weights.append((1, feedforward, held_one, 0))
    stored = [(residual, bulks[0]) + tuple(first[:4]) + tuple(second[1:3])]
    residual = second[0]
    first = attend(
        True,
        ids,
        residual,
        attend_weights[1],
        bulks[1],
        biases[1],
        mask,
        token,
    )
    second = feed(ids, first[0], feed_weights[1], bulks[1], inners[1], images.shape)
    stored.append((residual, bulks[1]) + tuple(first[:4]) + tuple(second[1:3]))
    block_out = second[0]

    def back_feed(layer, grad, after):
        _, bulk, middle, _, _, _, act, slope = stored[layer]
        layer_id, own, held, first_unit = feed_weights[layer]
        weights = (layer_id, own, [far(block) for block in held], first_unit)
        if layer == LAYERS - 1:
            grad = far(grad)
        return feed_back(
            ids, image_counts, grad, far(middle), weights, bulk, far(act), far(slope), after
        )

    def back_attend(layer, grad, after):
        residual, bulk, _, project, prob, attended, _, _ = stored[layer]
        layer_id, own, held, first_unit = attend_weights[layer]
        weights = (layer_id, own, [far(block) for block in held], first_unit)
        return attend_back(
            layer % 2 == 1,
            ids,
            grad,
            far(residual),
            weights,
            bulk,
            far(project),
            far(prob),
            far(attended),
            images.shape if layer == 0 else None,
            after,
        )

    grad_state, small_f1, inner_f1, keep_f1, send_f1, _ = back_feed(1, cotangent, ())
    came_f1 = send_pair(send_f1)
    grad_state, small_a1, scores_a1, *halves, token = back_attend(1, grad_state, ())
    pairs_a1 = [(halves[index], send_pair(halves[2 + index])) for index in range(2)]
    *chips, token = core_sum(ids, [(keep_f1, came_f1)], [token])
    chips_f1 = send_chips(chips)
    grad_state, small_f0, inner_f0, keep_f0, send_f0, token = back_feed(0, grad_state, [token])
    keep_f1, away, token = plane_sum(ids, chips_f1, (), [token], 60e6)
    came_f0 = send_pair(lax.optimization_barrier((send_f0, token))[0])
    came_f1 = swap_line(away)
    vector_one, token = pack(
        rel_slots, small_a1, small_f1, inner_f1, scores_a1, length, extra, None, [token]
    )
    *chips, token = core_sum(ids, pairs_a1 + [(keep_f0, came_f0)], [token], 4e6)
    chips_af = send_chips(chips)
    input_grad, small_a0, scores_a0, *halves, token = back_attend(0, grad_state, [token])
    keep_f1, away_f1, token = pair_sum(keep_f1, came_f1, [token], 60e6)
    *send_a0, _ = lax.optimization_barrier((*halves[2:], token))
    pairs_a0 = [(halves[index], send_pair(send_a0[index])) for index in range(2)]
    *chips, token = core_sum(ids, pairs_a0, [token])
    chips_a0 = send_chips(chips)
    vectors, token = pack(
        rel_slots, small_a0, small_f0, inner_f0, scores_a0, length, extra, vector_one, [token]
    )
    came_vectors = send_pair(vectors)
    away_f1, token = lax.optimization_barrier((away_f1, token))
    came_f1 = swap_line(away_f1)
    attention_states = (attention, attention_first, attention_second)
    feedforward_states = (feedforward, feedforward_first, feedforward_second)
    part_rows = attention.shape[1] // lax.axis_size("rep")
    jobs = ((0, 1, 0), (1, 0, part_rows), (0, 0, part_rows * (1 + feed_units)))
    ready, token = load_ahead(jobs, (attention_states, feedforward_states), [token])
    total_f1, token = finish_line(keep_f1, came_f1, [token])
    keep_af, away, token = plane_sum(ids, chips_af, (), [token], 1e5)
    came_af = swap_line(away)
    total_f1, token = lax.optimization_barrier((total_f1, token))
    chips_f1 = send_chips([total_f1.reshape(1, -1, piece)] * (lax.axis_size("rep") // 2))
    keep_af, came_af, token = narrow_line(keep_af, came_af, [token])
    keep_a0, away, token = plane_sum(ids, chips_a0, (vectors, came_vectors), [token])
    came_a0 = swap_line(away)
    keep_a0, came_a0, token = narrow_line(keep_a0, came_a0, [token])
    held_f1, (token,) = hold(chips_f1, [token])
    total, token = final_sum((keep_af, came_af), (keep_a0, came_a0), [token])
    chips = send_chips([total] * (lax.axis_size("rep") // 2))
    (feedforward_out,), token = adam(ids, held_f1, ((0, 1, 0),), (feedforward_states,), (), [token])
    held, (token,) = hold(chips, [token])
    *vector_out, token = vector_adam(
        ids,
        held[::2],
        total.shape[1] - extra,
        vector_params,
        vector_first,
        vector_second,
        [token],
    )
    (attention_out, feedforward_out), _ = adam(
        ids,
        held,
        jobs,
        (attention_states, feedforward_states),
        feedforward_out,
        [token],
        ready,
    )
    vector_grad, vector_new, first_vector, second_vector = vector_out
    attention_grad, attention_new, first_attention, second_attention = attention_out
    feedforward_grad, feedforward_new, first_feedforward, second_feedforward = feedforward_out
    return (
        block_out,
        input_grad,
        attention_grad,
        feedforward_grad,
        vector_grad,
        attention_new,
        feedforward_new,
        vector_new,
        first_attention,
        first_feedforward,
        first_vector,
        second_attention,
        second_feedforward,
        second_vector,
    )


def solution(mesh):
    rows = P(("shard", "rep"), None, None, None)
    matrix = P(None, None, "shard")
    vector = P(None, "shard")
    states = (matrix, matrix, vector)
    return jax.shard_map(
        shards,
        mesh=mesh,
        in_specs=(rows, P(("shard", "rep"), None, None), P(("shard", "rep")), P(), rows)
        + states * 3,
        out_specs=(rows, rows) + states * 4,
        check_vma=False,
    )
```
